32 devices in a mesh: fsdp: 32 (over z, y, x, core).
Axes of the slice: x: 2, y: 2, z: 4, core: 2. Of those that a mesh axis runs over, the one named last changes fastest.
Arguments:
- inputs: bfloat16 [256, 4096], P('fsdp'), may hold values from -6 to 6
- norm_gain: bfloat16 [4096], replicated, may hold values from 0.099609375 to 1.8984375
- lengths: int32 [2], replicated, may hold values from 1 to 128, 192 in all
- gate_rows: bfloat16 [10240, 4096], P('fsdp'), may hold values from -0.09375 to 0.09375
- up_rows: bfloat16 [10240, 4096], P('fsdp'), may hold values from -0.09375 to 0.09375
- down_rows: bfloat16 [10240, 4096], P('fsdp'), may hold values from -0.109375 to 0.109375
- krylov_gate: bfloat16 [8, 10240, 4096], P(None, 'fsdp'), may hold values from -30 to 30
- krylov_up: bfloat16 [8, 10240, 4096], P(None, 'fsdp'), may hold values from -30 to 30
- krylov_down: bfloat16 [8, 10240, 4096], P(None, 'fsdp'), may hold values from -30 to 30
Outputs:
- new_gate: bfloat16 [10240, 4096], P('fsdp')
- new_up: bfloat16 [10240, 4096], P('fsdp')
- new_down: bfloat16 [10240, 4096], P('fsdp')
- coefficients: float32 [9], replicated
The draws below stay inside these ranges and needn't reach their ends.
Inputs may be any that keep to these rules, and one draw needn't show every extreme that they name: The lengths sum to exactly 192.
All inputs are finite; a program needn't handle non-finite values.
Results may differ from the reference program's by a relative error of at most 0.0051.
The reference program's roundings to bfloat16 on the way (of `normed`, `probe_gate`, `hidden`, `tangent`, `loss_t` and `s_term`) count: a program that leaves them out, or rounds other values in their place, can miss the bound.
Values may be sent and summed in bfloat16 or wider, within the bound.
No kernel may reach another device: no remote copies, remote signals or barrier semaphores. Data moves between devices by JAX's collectives and lax.ppermute only.
A program may use at most 192 MiB of HBM per device.

```python
import math
import jax
import jax.numpy as jnp
import numpy as np
from jax import lax

D = 4096
FF = 10240
BASIS = 8
LEN = 128
SEQS = 2
TOKENS = 256
LIVE = 192


def krylov_common(key, salt):
    key = jax.random.fold_in(key, salt)
    keys = jax.random.split(key, 3)
    ramp = jnp.exp(math.log(3.0) * jnp.arange(FF, dtype=jnp.float32) / FF)
    row_scale = jnp.exp(jax.random.uniform(keys[0], (1, FF, 1), jnp.float32, math.log(0.4), math.log(4.0)))
    shared = jax.random.normal(keys[1], (1, FF, D), jnp.float32)
    own = jax.random.normal(keys[2], (BASIS, FF, D), jnp.float32)
    col_scale = jnp.ones((1, 1, D), jnp.float32)
    mixed = 0.6 * shared + 0.8 * own
    values = ramp[None, :, None] * row_scale * col_scale * mixed
    return jnp.clip(values, -30.0, 30.0).astype(jnp.bfloat16)


def draw_krylov_gate(key, part):
    return krylov_common(key, 11)


def draw_krylov_up(key, part):
    return krylov_common(key, 12)


def draw_krylov_down(key, part):
    return krylov_common(key, 13)


def spiked(array, key, source, target, blocks, factor):
    owner, partner = [(jnp.arange(array.shape[position]) // (array.shape[position] // blocks)).reshape([-1 if axis == position else 1 for axis in range(array.ndim)]) for position in (source, target)]
    chosen = jax.random.permutation(key, blocks)[partner]
    strong = (owner == chosen) | (owner == (partner + blocks // 2) % blocks)
    return jnp.where(strong, factor * array, array)


def block_scale(stream_key, shape, pieces, low, top_value):
    loudness = 1.0
    for axis_at, blocks in pieces:
        steps = jax.random.uniform(jax.random.fold_in(jax.random.fold_in(stream_key, 6), axis_at), (blocks,), jnp.float32, low / len(pieces), top_value / len(pieces))
        loudness = loudness * jnp.repeat(jnp.exp(steps), shape[axis_at] // blocks).reshape((-1,) + (1,) * (len(shape) - 1 - axis_at))
    return loudness


def profile(count, total, reach, lean):
    loads = [(1 << 20) // math.isqrt(rank ** lean) + 1 for rank in range(2, count + 1)]
    rest, counts = total - reach - (count - 1), [1] * (count - 1)
    while rest > 0:
        movable = [i for i in range(count - 1) if counts[i] < reach]
        whole, remaining = sum([loads[i] for i in movable]), rest
        for i in movable:
            more = min(reach - counts[i], max(1, remaining * loads[i] // whole), rest)
            counts[i] = counts[i] + more
            rest = rest - more
    return np.array([reach] + counts)


def uneven(stream_key, amount, total, bound, skew):
    if amount == 2:
        one = jax.random.randint(stream_key, (), max(1, total - bound), min(bound, total - 1) + 1)
        return jnp.stack([one, total - one])
    sizes = jnp.asarray(profile(amount, total, bound, skew), jnp.int32)
    couples = (amount - 1) // 2
    giver, receiver = sizes[1:1 + 2 * couples:2], sizes[2:2 + 2 * couples:2]
    slack = jnp.minimum(giver - 1, bound - receiver)
    passed = jax.random.randint(jax.random.fold_in(stream_key, 1), (couples,), 0, 1 << 20) % (slack + 1)
    sizes = sizes.at[1:1 + 2 * couples:2].set(giver - passed).at[2:2 + 2 * couples:2].set(receiver + passed)
    return sizes[jax.random.permutation(jax.random.fold_in(stream_key, 2), amount)]


def bell_draw(rng, shape, deviation, bound, shards=(), kind=jnp.bfloat16):
    level = block_scale(rng, shape, shards, -0.22, 0.18) if shards else 1.0
    entries = jax.random.normal(rng, shape, jnp.float32) * deviation * level
    return jnp.minimum(jnp.maximum(entries, -bound), bound).astype(kind)


def noise_with(own_key, shape, deviation, limit, cuts, heavy, held_as=jnp.bfloat16):
    values = deviation * jax.random.normal(own_key, shape, jnp.float32)
    if cuts:
        values = values * block_scale(own_key, shape, cuts, -0.22, 0.18)
    return jnp.clip(spiked(values, jax.random.fold_in(own_key, 3), *heavy), -limit, limit).astype(held_as)


def setup_inputs(seed: int = 0) -> dict:
    key_of = jax.random.split(jax.random.key(seed), 10)
    inputs = bell_draw(key_of[0], (TOKENS, D), 1.0, 6.0, ((0, 32),))
    norm_gain = jnp.clip(1.0 + 0.18 * jax.random.normal(key_of[1], (D,), jnp.float32), 0.099609375, 1.8984375).astype(jnp.bfloat16)
    lengths = uneven(key_of[2], SEQS, LIVE, LEN, 0).astype(jnp.int32)
    gate_rows = bell_draw(key_of[3], (FF, D), D ** -0.5, 0.09375, ((0, 32),))
    up_rows = bell_draw(key_of[4], (FF, D), D ** -0.5, 0.09375, ((0, 32),))
    down_rows = noise_with(key_of[5], (FF, D), FF ** -0.5, 0.109375, ((0, 32),), (0, 1, 32, 2.75))
    krylov_gate = draw_krylov_gate(jax.random.fold_in(key_of[9], 71), 0)
    krylov_up = draw_krylov_up(jax.random.fold_in(key_of[9], 71), 0)
    krylov_down = draw_krylov_down(jax.random.fold_in(key_of[9], 71), 0)
    return {"inputs": inputs, "norm_gain": norm_gain, "lengths": lengths, "gate_rows": gate_rows, "up_rows": up_rows, "down_rows": down_rows, "krylov_gate": krylov_gate, "krylov_up": krylov_up, "krylov_down": krylov_down}


def gelu_pair(gate_pre):
    coef = math.sqrt(2.0 / math.pi)
    cube = gate_pre * gate_pre * gate_pre
    tanh_val = jnp.tanh(coef * (gate_pre + 0.044715 * cube))
    act = 0.5 * gate_pre * (1.0 + tanh_val)
    slope = 0.5 * (1.0 + tanh_val) + 0.5 * gate_pre * (1.0 - tanh_val * tanh_val) * coef * (1.0 + 3.0 * 0.044715 * gate_pre * gate_pre)
    return (act, slope)

def contract_first(left, right):
    return lax.dot_general(left, right, (((0,), (0,)), ((), ())), preferred_element_type=jnp.float32)

def contract_last(left, right):
    return lax.dot_general(left, right, (((1,), (1,)), ((), ())), preferred_element_type=jnp.float32)

def reference(inputs, norm_gain, lengths, gate_rows, up_rows, down_rows, krylov_gate, krylov_up, krylov_down):
    wide = inputs.astype(jnp.float32)
    normed = (wide * lax.rsqrt(lax.optimization_barrier(jnp.mean(wide * wide, axis=1, keepdims=True)) + 1e-06) * norm_gain.astype(jnp.float32)).astype(jnp.bfloat16)
    inv_d = 1.0 / math.sqrt(D)
    inv_ff = 1.0 / math.sqrt(FF)
    probe_gate = krylov_gate[BASIS - 1]
    probe_up = krylov_up[BASIS - 1]
    probe_down = krylov_down[BASIS - 1]
    gate_pre = contract_last(gate_rows, normed)
    up_pre = contract_last(up_rows, normed)
    tan_gate = contract_last(probe_gate, normed) * inv_d
    tan_up = contract_last(probe_up, normed) * inv_d
    act, slope = gelu_pair(gate_pre)
    hidden = (act * up_pre).astype(jnp.bfloat16)
    tangent = (slope * tan_gate * up_pre + act * tan_up).astype(jnp.bfloat16)
    jvp = contract_first(down_rows, tangent) + contract_first(probe_down, hidden) * inv_ff
    positions = jnp.arange(TOKENS, dtype=jnp.int32)
    seq_ids = positions // LEN
    live = (positions % LEN < lengths[seq_ids]).astype(jnp.float32)
    loss_t = (jvp * live[None, :]).astype(jnp.bfloat16)
    back = jnp.dot(down_rows, loss_t, preferred_element_type=jnp.float32)
    s_term = (back * up_pre * slope).astype(jnp.bfloat16)
    r_term = (back * act).astype(jnp.bfloat16)
    grad_gate = jnp.dot(s_term, normed, preferred_element_type=jnp.float32) * inv_d
    grad_up = jnp.dot(r_term, normed, preferred_element_type=jnp.float32) * inv_d
    grad_down = contract_last(hidden, loss_t) * inv_ff
    count = 3.0 * D * FF

    def project(parts):
        total = jnp.sum(parts[0].astype(jnp.float32) * grad_gate)
        total = total + jnp.sum(parts[1].astype(jnp.float32) * grad_up)
        total = total + jnp.sum(parts[2].astype(jnp.float32) * grad_down)
        return total
    proj = lax.map(project, (krylov_gate, krylov_up, krylov_down)) / count

    def remove(carry, items):
        weight, kg, ku, kd = items
        return ((carry[0] - weight * kg.astype(jnp.float32), carry[1] - weight * ku.astype(jnp.float32), carry[2] - weight * kd.astype(jnp.float32)), None)
    (res_gate, res_up, res_down), unused = lax.scan(remove, (grad_gate, grad_up, grad_down), (proj, krylov_gate, krylov_up, krylov_down))
    squares = (jnp.sum(res_gate * res_gate) + jnp.sum(res_up * res_up) + jnp.sum(res_down * res_down)) / count
    norm = jnp.sqrt(squares + 1e-06)
    new_gate = (res_gate / norm).astype(jnp.bfloat16)
    new_up = (res_up / norm).astype(jnp.bfloat16)
    new_down = (res_down / norm).astype(jnp.bfloat16)
    coefficients = jnp.concatenate([proj, norm[None]])
    return (new_gate, new_up, new_down, coefficients)
```

```python
import functools
import math

import jax
import jax.numpy as jnp
from jax import lax
from jax.experimental import pallas as pl
from jax.experimental.pallas import tpu as pltpu
from jax.sharding import PartitionSpec as P

LEN = 128
LIVE = 192
GROUP = 8
LANES = 128
F32 = jnp.float32
BF16 = jnp.bfloat16


def gelu_pair(gate_pre):
    coef = math.sqrt(2.0 / math.pi)
    cube = gate_pre * gate_pre * gate_pre
    tanh_val = jnp.tanh(coef * (gate_pre + 0.044715 * cube))
    act = 0.5 * gate_pre * (1.0 + tanh_val)
    slope = 0.5 * (1.0 + tanh_val) + 0.5 * gate_pre * (1.0 - tanh_val * tanh_val) * coef * (
        1.0 + 3.0 * 0.044715 * gate_pre * gate_pre
    )
    return (act, slope)


def dot_nn(left, right):
    return jnp.dot(left, right, preferred_element_type=F32)


def dot_nt(left, right):
    return lax.dot_general(left, right, (((1,), (1,)), ((), ())), preferred_element_type=F32)


def dot_tn(left, right):
    return lax.dot_general(left, right, (((0,), (0,)), ((), ())), preferred_element_type=F32)


def total(values):
    return jnp.sum(jnp.sum(values, axis=0, keepdims=True), axis=1, keepdims=True)


def reverse_bits(value, bits):
    out = value * 0
    for bit in range(bits):
        out = out | (((value >> bit) & 1) << (bits - 1 - bit))
    return out


def exchange(block, bit):
    count = lax.axis_size("fsdp")
    return lax.ppermute(block, "fsdp", [(one, one ^ (1 << bit)) for one in range(count)])


def gather_blocks(block, bits):
    for bit in reversed(range(bits)):
        block = jnp.concatenate([block, exchange(block, bit)], axis=0)
    return block


def params(mib, grid=1):
    return pltpu.CompilerParams(
        vmem_limit_bytes=mib << 20, dimension_semantics=("arbitrary",) * grid
    )


def whole(shape):
    return pl.BlockSpec(shape, lambda *_: (0,) * len(shape))


def live_tokens(info, gathered, gain, normed, spots):
    spare = info[1] - (LIVE - LEN)
    shift = lax.rem(spare, GROUP)
    half = (LIVE - LEN) // GROUP
    per = LEN // GROUP
    scale = gain[...].astype(F32)
    row_ids = lax.broadcasted_iota(jnp.int32, (GROUP, 1), 0)

    def load(group):
        return gathered[spots(info[0], group)].astype(F32)

    def tokens(slot):
        if slot < half:
            return load(slot)
        if slot < 2 * half:
            at = slot - half
            first = load(half + at)
            second = pltpu.roll(load(per + 2 * half - 1 - at), shift, 0)
            return jnp.where(GROUP * at + row_ids < spare, first, second)
        return load(per + slot - 2 * half)

    def norm(wide):
        mean = jnp.mean(wide * wide, axis=1, keepdims=True)
        return wide * lax.rsqrt(mean + 1e-06) * scale

    for pair in range(LIVE // (2 * GROUP)):
        both = [norm(tokens(2 * pair + side)) for side in range(2)]
        normed[2 * GROUP * pair : 2 * GROUP * (pair + 1), :] = jnp.concatenate(both, 0).astype(BF16)


def jvp_columns(info, tangent, hidden, down, probe, out, inv_ff, splits, places):
    values = dot_tn(tangent, down) + dot_tn(hidden, probe) * inv_ff
    rows = LIVE // splits
    for chunk in range(places):
        column, part = chunk // splits, chunk % splits
        piece = values[part * rows : (part + 1) * rows, column * LANES : (column + 1) * LANES]
        out[chunk ^ (info[0] & (places - 1))] = piece.astype(out.dtype)


def forward_kernel(
    blocks, inv_d, inv_ff, spots, splits, places,
    info, gathered, gain, gate, up, probe_gate, probe_up, down, probe_down,
    normed, normed_t, hidden, tangent, weight, act_out, send,
    sums,
):
    step = pl.program_id(0)
    width = gate.shape[1]

    @pl.when(step == 0)
    def _():
        live_tokens(info, gathered, gain, normed, spots)
        sums[...] = jnp.zeros_like(sums)

    @pl.when(step < blocks)
    def _():
        columns = normed[:, pl.ds(pl.multiple_of(step * width, width), width)]
        turned = columns.T
        normed_t[pl.ds(pl.multiple_of(step * width, width), width), :] = turned
        for at, rows in enumerate((gate, up, probe_gate, probe_up)):
            sums[at] += dot_nn(rows[...], turned)

    @pl.when(step == blocks - 1)
    def _():
        up_pre = sums[1]
        act, slope = gelu_pair(sums[0])
        hidden[...] = (act * up_pre).astype(BF16)
        tangent[...] = (
            slope * (sums[2] * inv_d) * up_pre + act * (sums[3] * inv_d)
        ).astype(BF16)
        weight[...] = up_pre * slope
        act_out[...] = act

    @pl.when(step >= blocks)
    def _():
        jvp_columns(
            info, tangent[...], hidden[...], down[...], probe_down[...], send, inv_ff, splits, places
        )


def keep_kernel(inv_ff, splits, places, info, tangent, hidden, down, probe_down, keep):
    jvp_columns(
        info, tangent[...], hidden[...], down[...], probe_down[...], keep, inv_ff, splits, places
    )


def gram_kernel(blocks, krylov, out, sums):
    step = pl.program_id(0)
    basis, rows, width = krylov.shape
    stack = krylov[...]
    if rows % 16:
        stack = stack.astype(F32).reshape(basis * rows, width).astype(BF16)
    else:
        stack = stack.reshape(basis * rows, width)

    @pl.when(step == 0)
    def _():
        sums[...] = jnp.zeros_like(sums)

    sums[...] += dot_nt(stack, stack)

    @pl.when(step == blocks - 1)
    def _():
        size = basis * rows
        own = lax.broadcasted_iota(jnp.int32, (size, size), 0)
        other = lax.broadcasted_iota(jnp.int32, (size, size), 1)
        same = jnp.where(lax.rem(own, rows) == lax.rem(other, rows), sums[...], 0.0)
        lane = lax.broadcasted_iota(jnp.int32, (1, LANES), 1)
        group = lax.broadcasted_iota(jnp.int32, (1, size), 1) // rows
        for one in range(basis):
            line = jnp.sum(same[one * rows : (one + 1) * rows], axis=0, keepdims=True)
            entry = jnp.zeros((1, LANES), F32)
            for two in range(basis):
                value = jnp.sum(jnp.where(group == two, line, 0.0), axis=1, keepdims=True)
                entry = entry + jnp.where(lane == two, value, 0.0)
            out[one : one + 1, :] = entry


def product_kernel(krylov, normed, normed_t, out, square):
    step = pl.program_id(0)

    @pl.when(step == 0)
    def _():
        out[...] = jnp.zeros_like(out)
        square[...] = jnp.zeros_like(square)

    turned = normed_t[...]
    for one in range(krylov.shape[0]):
        out[one] += dot_nn(krylov[one], turned)
    square[...] += dot_nn(normed[...], turned)


def back_kernel(
    blocks, inv_d, inv_ff, splits,
    info, gathered, down, krylov, hidden, weight, act, prod_gate, prod_up, square,
    gram_gate, gram_up, gram_down,
    loss, s_out, r_out, stats,
    sums, loss_square,
):
    step = pl.program_id(0)
    basis, rows, width = krylov.shape

    @pl.when(step == 0)
    def _():
        for column in range(loss.shape[1] // LANES):
            pieces = [
                gathered[(column * splits + part) ^ info[0]] for part in range(splits)
            ]
            if splits > 1:
                piece = jnp.concatenate([one.astype(F32) for one in pieces], 0).astype(BF16)
            else:
                piece = pieces[0]
            loss[:, column * LANES : (column + 1) * LANES] = piece
        sums[...] = jnp.zeros_like(sums)
        loss_square[...] = jnp.zeros_like(loss_square)

    columns = loss[:, pl.ds(pl.multiple_of(step * width, width), width)]
    turned = columns.T
    for one in range(basis):
        sums[one] += dot_nn(krylov[one], turned)
    sums[basis] += dot_nn(down[...], turned)
    loss_square[...] += dot_nn(columns, turned)

    @pl.when(step == blocks - 1)
    def _():
        back = sums[basis]
        s_term = (back * weight[...]).astype(BF16)
        r_term = (back * act[...]).astype(BF16)
        s_out[...] = s_term
        r_out[...] = r_term
        held = hidden[...]
        wide_s, wide_r, wide_h = s_term.astype(F32), r_term.astype(F32), held.astype(F32)
        for one in range(basis):
            value = inv_d * (wide_s * prod_gate[one] + wide_r * prod_up[one])
            value = total(value + inv_ff * (wide_h * sums[one]))
            stats[one : one + 1, :] = jnp.broadcast_to(value, (1, LANES))
        squares = inv_d * inv_d * ((dot_tn(s_term, s_term) + dot_tn(r_term, r_term)) * square[...])
        squares = total(squares + inv_ff * inv_ff * (dot_tn(held, held) * loss_square[...]))
        stats[basis : 2 * basis, :] = jnp.broadcast_to(squares, (basis, LANES))
        stats[2 * basis : 3 * basis, :] = gram_gate[...] + gram_up[...] + gram_down[...]


def new_kernel(
    basis, count, inv_d, inv_ff,
    stats, s_term, r_term, hidden, normed, loss, krylov_gate, krylov_up, krylov_down,
    new_gate, new_up, new_down, coefficients,
    scales, wide,
):
    @pl.when(pl.program_id(0) == 0)
    def _():
        proj = [stats[one, 0] / count for one in range(basis)]
        squares = stats[basis, 0]
        for one in range(basis):
            line = stats[2 * basis + one, 0] * proj[0]
            for two in range(1, basis):
                line = line + stats[2 * basis + one, two] * proj[two]
            squares = squares + proj[one] * (line - 2.0 * stats[one, 0])
        mean = jnp.maximum(jnp.full((8, LANES), squares / count, F32), 0.0)
        norm = jnp.sqrt(mean + 1e-06)
        inverse = jnp.max(1.0 / norm)
        for one in range(basis):
            coefficients[one] = proj[one]
            scales[one] = proj[one] * inverse
        coefficients[basis] = jnp.max(norm)
        scales[basis] = inverse

    weights = [scales[one] for one in range(basis)]
    inverse = scales[basis]
    rows = s_term.shape[0]
    tile = 16 if rows % 16 == 0 else rows
    for left, right, scale, krylov, out in (
        (s_term, normed, inv_d, krylov_gate, new_gate),
        (r_term, normed, inv_d, krylov_up, new_up),
        (hidden, loss, inv_ff, krylov_down, new_down),
    ):
        wide[...] = dot_nn(left[...], right[...]) * (scale * inverse)

        def body(at, carry, krylov=krylov, out=out):
            here = pl.ds(pl.multiple_of(at * tile, tile), tile)
            value = wide[here, :]
            for one in range(basis):
                value = value - weights[one] * krylov[one, here, :].astype(F32)
            out[here, :] = value.astype(BF16)
            return carry

        lax.fori_loop(0, rows // tile, body, 0, unroll=2 if (rows // tile) % 2 == 0 else 1)


def per_device(
    inputs, norm_gain, lengths, gate_rows, up_rows, down_rows, krylov_gate, krylov_up, krylov_down
):
    basis, rows, width = krylov_gate.shape
    devices = lax.axis_size("fsdp")
    bits = devices.bit_length() - 1
    hidden_all = rows * devices
    count = 3.0 * width * hidden_all
    inv_d = 1.0 / math.sqrt(width)
    inv_ff = 1.0 / math.sqrt(hidden_all)
    me = lax.axis_index("fsdp").astype(jnp.int32)
    mirror = reverse_bits(me, bits)
    info = jnp.stack([mirror, lengths[0]])

    own_tokens = inputs.shape[0]
    tokens = own_tokens * devices
    if own_tokens % GROUP == 0:
        sub = own_tokens // GROUP
        gathered = gather_blocks(inputs.reshape(sub, GROUP, width), bits)

        def spots(flip, group):
            return (reverse_bits(group // sub, bits) ^ flip) * sub + group % sub

    else:
        gathered = lax.all_gather(inputs, "fsdp", axis=0, tiled=True)
        gathered = gathered.reshape(tokens // GROUP, GROUP, width)

        def spots(flip, group):
            return group

    splits = devices // (width // LANES)
    chunk_rows = LIVE // splits
    cols = min(512, width // 2)
    blocks = width // cols
    places = devices // blocks
    half = blocks // 2
    gain = norm_gain.reshape(1, width)

    def fwd_spec(block, at):
        return pl.BlockSpec(block, at)

    def col(step):
        return jnp.minimum(step, blocks - 1)

    def send_col(step, info):
        return (half + jnp.maximum(step - blocks, 0)) ^ (info[0] // places)

    weights = pl.BlockSpec((rows, cols), lambda step, info: (0, col(step)))
    probe = pl.BlockSpec((None, rows, cols), lambda step, info: (basis - 1, 0, col(step)))
    normed, normed_t, hidden, tangent, weight, act, send = pl.pallas_call(
        functools.partial(
            forward_kernel, blocks, inv_d, inv_ff, spots, splits, places
        ),
        grid_spec=pltpu.PrefetchScalarGridSpec(
            num_scalar_prefetch=1,
            grid=(blocks + half,),
            in_specs=[
                whole(gathered.shape),
                whole(gain.shape),
                weights,
                weights,
                probe,
                probe,
                pl.BlockSpec((rows, cols), lambda step, info: (0, send_col(step, info))),
                pl.BlockSpec(
                    (None, rows, cols), lambda step, info: (basis - 1, 0, send_col(step, info))
                ),
            ],
            out_specs=[
                whole((LIVE, width)),
                whole((width, LIVE)),
                whole((rows, LIVE)),
                whole((rows, LIVE)),
                whole((rows, LIVE)),
                whole((rows, LIVE)),
                pl.BlockSpec(
                    (places, chunk_rows, LANES),
                    lambda step, info: (jnp.maximum(step - blocks, 0), 0, 0),
                ),
            ],
            scratch_shapes=[pltpu.VMEM((4, rows, LIVE), F32)],
        ),
        out_shape=[
            jax.ShapeDtypeStruct((LIVE, width), BF16),
            jax.ShapeDtypeStruct((width, LIVE), BF16),
            jax.ShapeDtypeStruct((rows, LIVE), BF16),
            jax.ShapeDtypeStruct((rows, LIVE), BF16),
            jax.ShapeDtypeStruct((rows, LIVE), F32),
            jax.ShapeDtypeStruct((rows, LIVE), F32),
            jax.ShapeDtypeStruct((devices // 2, chunk_rows, LANES), BF16),
        ],
        compiler_params=params(32),
        cost_estimate=pl.CostEstimate(
            flops=10 * rows * width * LIVE,
            bytes_accessed=10 * rows * width + 6 * LIVE * width,
            transcendentals=rows * LIVE,
        ),
        name="forward",
    )(info, gathered, gain, gate_rows, up_rows, krylov_gate, krylov_up, down_rows, krylov_down)

    got = exchange(send, 0)

    def keep_col(step, info):
        return step ^ (info[0] // places)

    keep = pl.pallas_call(
        functools.partial(keep_kernel, inv_ff, splits, places),
        grid_spec=pltpu.PrefetchScalarGridSpec(
            num_scalar_prefetch=1,
            grid=(half,),
            in_specs=[
                whole((rows, LIVE)),
                whole((rows, LIVE)),
                pl.BlockSpec((rows, cols), lambda step, info: (0, keep_col(step, info))),
                pl.BlockSpec(
                    (None, rows, cols), lambda step, info: (basis - 1, 0, keep_col(step, info))
                ),
            ],
            out_specs=pl.BlockSpec((places, chunk_rows, LANES), lambda step, info: (step, 0, 0)),
        ),
        out_shape=jax.ShapeDtypeStruct((devices // 2, chunk_rows, LANES), F32),
        compiler_params=params(16),
        cost_estimate=pl.CostEstimate(
            flops=2 * rows * width * LIVE,
            bytes_accessed=2 * rows * width + 2 * LIVE * width,
            transcendentals=0,
        ),
        name="keep",
    )(info, tangent, hidden, down_rows, krylov_down)

    for bit in range(1, bits):
        part = keep.shape[0] // 2
        send = (keep[part:] + got[part:].astype(F32)).astype(BF16)
        keep = keep[:part] + got[:part].astype(F32)
        got = exchange(send, bit)
    loss_own = (keep + got.astype(F32)).astype(BF16)
    loss_all = gather_blocks(loss_own, bits)

    lines = 32 if rows % 32 == 0 else rows
    pieces = rows // lines

    def gram(krylov):
        return pl.pallas_call(
            functools.partial(gram_kernel, pieces),
            grid=(pieces,),
            in_specs=[pl.BlockSpec((basis, lines, width), lambda step: (0, step, 0))],
            out_specs=whole((basis, LANES)),
            out_shape=jax.ShapeDtypeStruct((basis, LANES), F32),
            scratch_shapes=[pltpu.VMEM((basis * lines, basis * lines), F32)],
            compiler_params=params(24),
            cost_estimate=pl.CostEstimate(
                flops=2 * basis * basis * lines * rows * width,
                bytes_accessed=2 * basis * rows * width,
                transcendentals=0,
            ),
            name="gram",
        )(krylov)

    def product(krylov):
        return pl.pallas_call(
            product_kernel,
            grid=(blocks,),
            in_specs=[
                pl.BlockSpec((basis, rows, cols), lambda step: (0, 0, step)),
                pl.BlockSpec((LIVE, cols), lambda step: (0, step)),
                pl.BlockSpec((cols, LIVE), lambda step: (step, 0)),
            ],
            out_specs=[whole((basis, rows, LIVE)), whole((LIVE, LIVE))],
            out_shape=[
                jax.ShapeDtypeStruct((basis, rows, LIVE), F32),
                jax.ShapeDtypeStruct((LIVE, LIVE), F32),
            ],
            compiler_params=params(24),
            cost_estimate=pl.CostEstimate(
                flops=2 * basis * rows * width * LIVE,
                bytes_accessed=2 * basis * rows * width + 4 * basis * rows * LIVE,
                transcendentals=0,
            ),
            name="product",
        )(krylov, normed, normed_t)

    gram_gate, gram_up, gram_down = gram(krylov_gate), gram(krylov_up), gram(krylov_down)
    prod_gate, square = product(krylov_gate)
    prod_up, _ = product(krylov_up)

    loss, s_term, r_term, stats = pl.pallas_call(
        functools.partial(back_kernel, blocks, inv_d, inv_ff, splits),
        grid_spec=pltpu.PrefetchScalarGridSpec(
            num_scalar_prefetch=1,
            grid=(blocks,),
            in_specs=[
                whole(loss_all.shape),
                pl.BlockSpec((rows, cols), lambda step, info: (0, step)),
                pl.BlockSpec((basis, rows, cols), lambda step, info: (0, 0, step)),
                whole((rows, LIVE)),
                whole((rows, LIVE)),
                whole((rows, LIVE)),
                whole((basis, rows, LIVE)),
                whole((basis, rows, LIVE)),
                whole((LIVE, LIVE)),
                whole((basis, LANES)),
                whole((basis, LANES)),
                whole((basis, LANES)),
            ],
            out_specs=[
                whole((LIVE, width)),
                whole((rows, LIVE)),
                whole((rows, LIVE)),
                whole((3 * basis, LANES)),
            ],
            scratch_shapes=[
                pltpu.VMEM((basis + 1, rows, LIVE), F32),
                pltpu.VMEM((LIVE, LIVE), F32),
            ],
        ),
        out_shape=[
            jax.ShapeDtypeStruct((LIVE, width), BF16),
            jax.ShapeDtypeStruct((rows, LIVE), BF16),
            jax.ShapeDtypeStruct((rows, LIVE), BF16),
            jax.ShapeDtypeStruct((3 * basis, LANES), F32),
        ],
        compiler_params=params(40),
        cost_estimate=pl.CostEstimate(
            flops=2 * (basis + 1) * rows * width * LIVE,
            bytes_accessed=2 * (basis + 1) * rows * width + 8 * basis * rows * LIVE,
            transcendentals=0,
        ),
        name="back",
    )(
        info, loss_all, down_rows, krylov_down, hidden, weight, act, prod_gate, prod_up, square,
        gram_gate, gram_up, gram_down,
    )

    for bit in range(bits):
        stats = stats + exchange(stats, bit)

    narrow = min(256, cols)
    krylov_spec = pl.BlockSpec((basis, rows, narrow), lambda step: (0, 0, step))
    token_spec = pl.BlockSpec((LIVE, narrow), lambda step: (0, step))
    out_spec = pl.BlockSpec((rows, narrow), lambda step: (0, step))
    out_shape = jax.ShapeDtypeStruct((rows, width), BF16)
    new_gate, new_up, new_down, coefficients = pl.pallas_call(
        functools.partial(new_kernel, basis, count, inv_d, inv_ff),
        grid=(width // narrow,),
        in_specs=[
            pl.BlockSpec(memory_space=pltpu.SMEM),
            whole((rows, LIVE)),
            whole((rows, LIVE)),
            whole((rows, LIVE)),
            token_spec,
            token_spec,
            krylov_spec,
            krylov_spec,
            krylov_spec,
        ],
        out_specs=[out_spec, out_spec, out_spec, pl.BlockSpec(memory_space=pltpu.SMEM)],
        out_shape=[
            out_shape,
            out_shape,
            out_shape,
            jax.ShapeDtypeStruct((basis + 1,), F32),
        ],
        scratch_shapes=[pltpu.SMEM((basis + 1,), F32), pltpu.VMEM((rows, narrow), F32)],
        compiler_params=params(32),
        cost_estimate=pl.CostEstimate(
            flops=6 * rows * width * LIVE,
            bytes_accessed=6 * (basis + 1) * rows * width,
            transcendentals=0,
        ),
        name="new",
    )(stats, s_term, r_term, hidden, normed, loss, krylov_gate, krylov_up, krylov_down)
    return (new_gate, new_up, new_down, coefficients)


def solution(mesh):
    placed = (
        P("fsdp", None),
        P(),
        P(),
        P("fsdp", None),
        P("fsdp", None),
        P("fsdp", None),
        P(None, "fsdp", None),
        P(None, "fsdp", None),
        P(None, "fsdp", None),
    )
    return jax.shard_map(
        per_device,
        mesh=mesh,
        in_specs=placed,
        out_specs=(P("fsdp", None), P("fsdp", None), P("fsdp", None), P()),
        check_vma=False,
    )
```

```python
import functools
import math

import jax
import jax.numpy as jnp
from jax import lax
from jax.experimental import pallas as pl
from jax.experimental.pallas import tpu as pltpu
from jax.sharding import PartitionSpec as P

LEN = 128
LIVE = 192
GROUP = 8
LANES = 128
F32 = jnp.float32
BF16 = jnp.bfloat16


def gelu_pair(gate_pre):
    coef = math.sqrt(2.0 / math.pi)
    cube = gate_pre * gate_pre * gate_pre
    tanh_val = jnp.tanh(coef * (gate_pre + 0.044715 * cube))
    act = 0.5 * gate_pre * (1.0 + tanh_val)
    slope = 0.5 * (1.0 + tanh_val) + 0.5 * gate_pre * (1.0 - tanh_val * tanh_val) * coef * (
        1.0 + 3.0 * 0.044715 * gate_pre * gate_pre
    )
    return (act, slope)


def dot_nn(left, right):
    return jnp.dot(left, right, preferred_element_type=F32)


def dot_nt(left, right):
    return lax.dot_general(left, right, (((1,), (1,)), ((), ())), preferred_element_type=F32)


def dot_tn(left, right):
    return lax.dot_general(left, right, (((0,), (0,)), ((), ())), preferred_element_type=F32)


def total(values):
    return jnp.sum(jnp.sum(values, axis=0, keepdims=True), axis=1, keepdims=True)


def reverse_bits(value, bits):
    out = value * 0
    for bit in range(bits):
        out = out | (((value >> bit) & 1) << (bits - 1 - bit))
    return out


def exchange(block, bit):
    count = lax.axis_size("fsdp")
    return lax.ppermute(block, "fsdp", [(one, one ^ (1 << bit)) for one in range(count)])


def gather_blocks(block, bits, beside):
    made = []
    for bit in reversed(range(bits)):
        other = exchange(block, bit)
        if bit in beside:
            extra = beside[bit](block)
            other, extra = lax.optimization_barrier((other, extra))
            made.append(extra)
        if bit:
            block = jnp.concatenate([block, other], axis=0)
    return block, other, made


def after(value, earlier):
    return lax.optimization_barrier((value, earlier))[0]


def stacked(krylov):
    basis, rows, width = krylov.shape
    if rows % 16:
        return krylov.astype(F32).reshape(basis * rows, width).astype(BF16)
    return krylov.reshape(basis * rows, width)


def params(mib, grid=1):
    return pltpu.CompilerParams(
        vmem_limit_bytes=mib << 20, dimension_semantics=("arbitrary",) * grid
    )


def whole(shape):
    return pl.BlockSpec(shape, lambda *_: (0,) * len(shape))


def live_tokens(info, lower, upper, gain, normed, spots):
    spare = info[1] - (LIVE - LEN)
    shift = lax.rem(spare, GROUP)
    half = (LIVE - LEN) // GROUP
    per = LEN // GROUP
    scale = gain[...].astype(F32)
    row_ids = lax.broadcasted_iota(jnp.int32, (GROUP, 1), 0)

    half_groups = lower.shape[0]

    def load(group):
        spot = spots(info[0], group)
        place = lax.rem(spot, half_groups)
        return jnp.where(spot < half_groups, lower[place], upper[place]).astype(F32)

    def tokens(slot):
        if slot < half:
            return load(slot)
        if slot < 2 * half:
            at = slot - half
            first = load(half + at)
            second = pltpu.roll(load(per + 2 * half - 1 - at), shift, 0)
            return jnp.where(GROUP * at + row_ids < spare, first, second)
        return load(per + slot - 2 * half)

    def norm(wide):
        mean = jnp.mean(wide * wide, axis=1, keepdims=True)
        return wide * lax.rsqrt(mean + 1e-06) * scale

    for pair in range(LIVE // (2 * GROUP)):
        both = [norm(tokens(2 * pair + side)) for side in range(2)]
        normed[2 * GROUP * pair : 2 * GROUP * (pair + 1), :] = jnp.concatenate(both, 0).astype(BF16)


def jvp_columns(info, tangent, hidden, down, probe, out, inv_ff, splits, places):
    values = dot_tn(tangent, down) + dot_tn(hidden, probe) * inv_ff
    rows = LIVE // splits
    for chunk in range(places):
        column, part = chunk // splits, chunk % splits
        piece = values[part * rows : (part + 1) * rows, column * LANES : (column + 1) * LANES]
        out[chunk ^ (info[0] & (places - 1))] = piece.astype(out.dtype)


def forward_kernel(
    blocks, inv_d, inv_ff, spots, splits, places,
    info, lower, upper, gain, gate, up, probe_gate, probe_up, down, probe_down,
    normed_out, hidden, tangent, weight, act_out, send,
    normed, sums,
):
    step = pl.program_id(0)
    width = gate.shape[1]

    @pl.when(step == 0)
    def _():
        live_tokens(info, lower, upper, gain, normed, spots)
        sums[...] = jnp.zeros_like(sums)

    @pl.when(step < blocks)
    def _():
        columns = normed[:, pl.ds(pl.multiple_of(step * width, width), width)]
        normed_out[...] = columns
        turned = columns.T
        for at, rows in enumerate((gate, up, probe_gate, probe_up)):
            sums[at] += dot_nn(rows[...], turned)

    @pl.when(step == blocks - 1)
    def _():
        up_pre = sums[1]
        act, slope = gelu_pair(sums[0])
        hidden[...] = (act * up_pre).astype(BF16)
        tangent[...] = (
            slope * (sums[2] * inv_d) * up_pre + act * (sums[3] * inv_d)
        ).astype(BF16)
        weight[...] = up_pre * slope
        act_out[...] = act

    @pl.when(step >= blocks)
    def _():
        jvp_columns(
            info, tangent[...], hidden[...], down[...], probe_down[...], send, inv_ff, splits, places
        )


def keep_kernel(inv_ff, splits, places, info, tangent, hidden, down, probe_down, keep):
    jvp_columns(
        info, tangent[...], hidden[...], down[...], probe_down[...], keep, inv_ff, splits, places
    )


def gram_kernel(blocks, krylov, out, sums):
    step = pl.program_id(0)
    basis, rows, width = krylov.shape
    stack = stacked(krylov[...])

    @pl.when(step == 0)
    def _():
        sums[...] = jnp.zeros_like(sums)

    sums[...] += dot_nt(stack, stack)

    @pl.when(step == blocks - 1)
    def _():
        size = basis * rows
        own = lax.broadcasted_iota(jnp.int32, (size, size), 0)
        other = lax.broadcasted_iota(jnp.int32, (size, size), 1)
        same = jnp.where(lax.rem(own, rows) == lax.rem(other, rows), sums[...], 0.0)
        lane = lax.broadcasted_iota(jnp.int32, (1, LANES), 1)
        group = lax.broadcasted_iota(jnp.int32, (1, size), 1) // rows
        for one in range(basis):
            line = jnp.sum(same[one * rows : (one + 1) * rows], axis=0, keepdims=True)
            entry = jnp.zeros((1, LANES), F32)
            for two in range(basis):
                value = jnp.sum(jnp.where(group == two, line, 0.0), axis=1, keepdims=True)
                entry = entry + jnp.where(lane == two, value, 0.0)
            out[one : one + 1, :] = entry


def product_kernel(krylov, normed, out, square):
    basis, rows, width = krylov.shape
    columns = normed[...]
    turned = columns.T
    made = dot_nn(stacked(krylov[...]), turned).reshape(basis, rows, LIVE)
    made_square = dot_nn(columns, turned)
    first = pl.program_id(0) == 0

    @pl.when(first)
    def _():
        out[...] = made
        square[...] = made_square

    @pl.when(jnp.logical_not(first))
    def _():
        out[...] += made
        square[...] += made_square


def loss_columns(flip, load, places, splits):
    made = []
    for column in range(places // splits):
        pieces = [
            load((column * splits + part) ^ (flip & (places - 1))) for part in range(splits)
        ]
        if splits > 1:
            pieces = [jnp.concatenate([one.astype(F32) for one in pieces], 0).astype(BF16)]
        made.append(pieces[0])
    return jnp.concatenate(made, axis=1)


def back_columns(info, chunks, down, krylov, sums, square, splits, start):
    basis, rows, width = krylov.shape
    columns = loss_columns(info[0], lambda at: chunks[at], chunks.shape[0], splits)
    turned = columns.T
    size = basis * rows
    made = dot_nn(stacked(krylov[...]), turned)
    made_down = dot_nn(down[...], turned)
    made_square = dot_nn(columns, turned)

    @pl.when(start)
    def _():
        sums[0:size, :] = made
        sums[size : size + rows, :] = made_down
        square[...] = made_square

    @pl.when(jnp.logical_not(start))
    def _():
        sums[0:size, :] += made
        sums[size : size + rows, :] += made_down
        square[...] += made_square


def back_half_kernel(splits, info, chunks, down, krylov, sums, square):
    back_columns(info, chunks, down, krylov, sums, square, splits, pl.program_id(0) == 0)


def back_kernel(
    blocks, inv_d, inv_ff, splits, parts,
    info, chunks, down, krylov, hidden, weight, act, square, loss_square_half, grams,
    sums_half, *rest,
):
    prods = rest[: 2 * parts]
    s_out, r_out, stats, sums, loss_square, half_held, gate_held, up_held, sems = rest[2 * parts :]
    step = pl.program_id(0)
    basis, rows, width = krylov.shape
    size = basis * rows
    share = basis // parts

    copies = [pltpu.make_async_copy(sums_half, half_held, sems.at[0])]
    for part in range(parts):
        here = pl.ds(part * share, share)
        copies.append(
            pltpu.make_async_copy(prods[part], gate_held.at[here], sems.at[1 + part])
        )
        copies.append(
            pltpu.make_async_copy(
                prods[parts + part], up_held.at[here], sems.at[1 + parts + part]
            )
        )

    @pl.when(step == 0)
    def _():
        for copy in copies:
            copy.start()

    back_columns(info, chunks, down, krylov, sums, loss_square, splits, step == 0)

    @pl.when(step == blocks - 1)
    def _():
        for copy in copies:
            copy.wait()
        back = sums[size : size + rows, :] + half_held[size : size + rows, :]
        s_term = (back * weight[...]).astype(BF16)
        r_term = (back * act[...]).astype(BF16)
        s_out[...] = s_term
        r_out[...] = r_term
        held = hidden[...]
        wide_s = s_term.astype(F32) * inv_d
        wide_r = r_term.astype(F32) * inv_d
        wide_h = held.astype(F32) * inv_ff
        for one in range(basis):
            here = slice(one * rows, (one + 1) * rows)
            value = wide_s * gate_held[one] + wide_r * up_held[one]
            value = total(value + wide_h * (sums[here, :] + half_held[here, :]))
            stats[one : one + 1, :] = jnp.broadcast_to(value, (1, LANES))
        squares = inv_d * inv_d * ((dot_tn(s_term, s_term) + dot_tn(r_term, r_term)) * square[...])
        other = loss_square[...] + loss_square_half[...]
        squares = total(squares + inv_ff * inv_ff * (dot_tn(held, held) * other))
        stats[basis : 2 * basis, :] = jnp.broadcast_to(squares, (basis, LANES))
        stats[2 * basis : 3 * basis, :] = jnp.sum(grams[...], axis=0)


def split_three(value):
    first = value.astype(BF16)
    rest = value - first.astype(F32)
    second = rest.astype(BF16)
    return first, second, (rest - second.astype(F32)).astype(BF16)


def new_kernel(
    basis, count, inv_d, inv_ff, splits, lines,
    info, stats, s_term, r_term, hidden, normed, lower, upper,
    krylov_gate, krylov_up, krylov_down,
    new_gate, new_up, new_down, coefficients,
    scale_held, mixer, wide,
):
    step = pl.program_id(0)
    size = basis * lines

    @pl.when(step == 0)
    def _():
        proj = [stats[one, 0] / count for one in range(basis)]
        squares = stats[basis, 0]
        for one in range(basis):
            line = stats[2 * basis + one, 0] * proj[0]
            for two in range(1, basis):
                line = line + stats[2 * basis + one, two] * proj[two]
            squares = squares + proj[one] * (line - 2.0 * stats[one, 0])
        mean = jnp.maximum(jnp.full((8, LANES), squares / count, F32), 0.0)
        norm = jnp.sqrt(mean + 1e-06)
        inverse = jnp.max(1.0 / norm)
        for one in range(basis):
            coefficients[one] = proj[one]
        coefficients[basis] = jnp.max(norm)
        scale_held[0] = inverse
        lane = lax.broadcasted_iota(jnp.int32, (lines, size), 1)
        row = lax.broadcasted_iota(jnp.int32, (lines, size), 0)
        values = jnp.zeros((lines, size), F32)
        for one in range(basis):
            values = jnp.where(lane == one * lines + row, proj[one] * inverse, values)
        terms = [term.astype(F32) for term in split_three(values)]
        mixer[...] = jnp.concatenate(terms, axis=0).astype(BF16)

    inverse = scale_held[0]
    rows = s_term.shape[0]
    low = step < pl.num_programs(0) // 2
    loss = loss_columns(
        info[0], lambda at: jnp.where(low, lower[at], upper[at]), lower.shape[0], splits
    )
    mix = mixer[...]
    for left, right, scale, krylov, out in (
        (s_term, normed[...], inv_d, krylov_gate, new_gate),
        (r_term, normed[...], inv_d, krylov_up, new_up),
        (hidden, loss, inv_ff, krylov_down, new_down),
    ):
        wide[...] = dot_nn(left[...], right) * (scale * inverse)
        for at in range(rows // lines):
            here = slice(at * lines, (at + 1) * lines)
            mixed = dot_nn(mix, stacked(krylov[:, here, :]))
            mixed = mixed[:lines] + (mixed[lines : 2 * lines] + mixed[2 * lines :])
            out[here, :] = (wide[here, :] - mixed).astype(BF16)


def per_device(
    inputs, norm_gain, lengths, gate_rows, up_rows, down_rows, krylov_gate, krylov_up, krylov_down
):
    basis, rows, width = krylov_gate.shape
    devices = lax.axis_size("fsdp")
    bits = devices.bit_length() - 1
    hidden_all = rows * devices
    count = 3.0 * width * hidden_all
    inv_d = 1.0 / math.sqrt(width)
    inv_ff = 1.0 / math.sqrt(hidden_all)
    me = lax.axis_index("fsdp").astype(jnp.int32)
    mirror = reverse_bits(me, bits)
    info = jnp.stack([mirror, lengths[0]])

    splits = devices // (width // LANES)
    chunk_rows = LIVE // splits
    cols = min(512, width // 2)
    blocks = width // cols
    places = devices // blocks
    half = blocks // 2
    lines = 32 if rows % 32 == 0 else rows
    pieces = rows // lines
    parts = 2 if basis % 2 == 0 else 1
    share = basis // parts

    def gram(krylov, first, number, earlier):
        return pl.pallas_call(
            functools.partial(gram_kernel, number),
            grid=(number,),
            in_specs=[pl.BlockSpec((basis, lines, width), lambda step: (0, first + step, 0))],
            out_specs=whole((basis, LANES)),
            out_shape=jax.ShapeDtypeStruct((basis, LANES), F32),
            scratch_shapes=[pltpu.VMEM((basis * lines, basis * lines), F32)],
            compiler_params=params(60),
            cost_estimate=pl.CostEstimate(
                flops=4 * basis * basis * lines * lines * number * width,
                bytes_accessed=2 * basis * lines * number * width,
                transcendentals=0,
            ),
            name="gram",
        )(after(krylov, earlier))

    cut = (pieces + 1) // 2
    gate_low = lambda earlier: gram(krylov_gate, 0, cut, earlier)
    gate_high = lambda earlier: gram(krylov_gate, cut, pieces - cut, earlier)
    up_low = lambda earlier: gram(krylov_up, 0, cut, earlier)
    up_high = lambda earlier: gram(krylov_up, cut, pieces - cut, earlier)
    down_low = lambda earlier: gram(krylov_down, 0, cut, earlier)
    down_high = lambda earlier: gram(krylov_down, cut, pieces - cut, earlier)

    own_tokens = inputs.shape[0]
    tokens = own_tokens * devices
    if own_tokens % GROUP == 0 and pieces > 1:
        sub = own_tokens // GROUP
        work = (down_low, up_high, up_low, gate_high, gate_low)
        lower, upper, grams = gather_blocks(
            inputs.reshape(sub, GROUP, width), bits, dict(enumerate(work))
        )
        grams.append(None)

        def spots(flip, group):
            return (reverse_bits(group // sub, bits) ^ flip) * sub + group % sub

    else:
        gathered = lax.all_gather(inputs, "fsdp", axis=0, tiled=True)
        gathered = gathered.reshape(tokens // GROUP, GROUP, width)
        lower, upper = jnp.split(gathered, 2)
        grams = [
            gram(one, 0, pieces, info) for one in (krylov_gate, krylov_up, krylov_down)
        ]

        def spots(flip, group):
            return group

    gain = norm_gain.reshape(1, width)

    def col(step):
        return jnp.minimum(step, blocks - 1)

    def send_col(step, info):
        return (half + jnp.maximum(step - blocks, 0)) ^ (info[0] // places)

    weights = pl.BlockSpec((rows, cols), lambda step, info: (0, col(step)))
    probe = pl.BlockSpec((None, rows, cols), lambda step, info: (basis - 1, 0, col(step)))
    normed, hidden, tangent, weight, act, send = pl.pallas_call(
        functools.partial(forward_kernel, blocks, inv_d, inv_ff, spots, splits, places),
        grid_spec=pltpu.PrefetchScalarGridSpec(
            num_scalar_prefetch=1,
            grid=(blocks + half,),
            in_specs=[
                whole(lower.shape),
                whole(upper.shape),
                whole(gain.shape),
                weights,
                weights,
                probe,
                probe,
                pl.BlockSpec((rows, cols), lambda step, info: (0, send_col(step, info))),
                pl.BlockSpec(
                    (None, rows, cols), lambda step, info: (basis - 1, 0, send_col(step, info))
                ),
            ],
            out_specs=[
                pl.BlockSpec((LIVE, cols), lambda step, info: (0, col(step))),
                whole((rows, LIVE)),
                whole((rows, LIVE)),
                whole((rows, LIVE)),
                whole((rows, LIVE)),
                pl.BlockSpec(
                    (places, chunk_rows, LANES),
                    lambda step, info: (jnp.maximum(step - blocks, 0), 0, 0),
                ),
            ],
            scratch_shapes=[pltpu.VMEM((LIVE, width), BF16), pltpu.VMEM((4, rows, LIVE), F32)],
        ),
        out_shape=[
            jax.ShapeDtypeStruct((LIVE, width), BF16),
            jax.ShapeDtypeStruct((rows, LIVE), BF16),
            jax.ShapeDtypeStruct((rows, LIVE), BF16),
            jax.ShapeDtypeStruct((rows, LIVE), F32),
            jax.ShapeDtypeStruct((rows, LIVE), F32),
            jax.ShapeDtypeStruct((devices // 2, chunk_rows, LANES), BF16),
        ],
        compiler_params=params(60),
        cost_estimate=pl.CostEstimate(
            flops=10 * rows * width * LIVE,
            bytes_accessed=10 * rows * width + 6 * LIVE * width,
            transcendentals=rows * LIVE,
        ),
        name="forward",
    )(
        info, lower, upper, gain, gate_rows, up_rows, krylov_gate, krylov_up, down_rows,
        krylov_down,
    )

    def product(krylov, part, earlier):
        return pl.pallas_call(
            product_kernel,
            grid=(blocks,),
            in_specs=[
                pl.BlockSpec((share, rows, cols), lambda step: (part, 0, step)),
                pl.BlockSpec((LIVE, cols), lambda step: (0, step)),
            ],
            out_specs=[whole((share, rows, LIVE)), whole((LIVE, LIVE))],
            out_shape=[
                jax.ShapeDtypeStruct((share, rows, LIVE), F32),
                jax.ShapeDtypeStruct((LIVE, LIVE), F32),
            ],
            compiler_params=params(60),
            cost_estimate=pl.CostEstimate(
                flops=2 * share * rows * width * LIVE,
                bytes_accessed=2 * share * rows * width + 4 * share * rows * LIVE,
                transcendentals=0,
            ),
            name="product",
        )(after(krylov, earlier), normed)

    got = exchange(send, 0)

    def keep_col(step, info):
        return step ^ (info[0] // places)

    keep = pl.pallas_call(
        functools.partial(keep_kernel, inv_ff, splits, places),
        grid_spec=pltpu.PrefetchScalarGridSpec(
            num_scalar_prefetch=1,
            grid=(half,),
            in_specs=[
                whole((rows, LIVE)),
                whole((rows, LIVE)),
                pl.BlockSpec((rows, cols), lambda step, info: (0, keep_col(step, info))),
                pl.BlockSpec(
                    (None, rows, cols), lambda step, info: (basis - 1, 0, keep_col(step, info))
                ),
            ],
            out_specs=pl.BlockSpec((places, chunk_rows, LANES), lambda step, info: (step, 0, 0)),
        ),
        out_shape=jax.ShapeDtypeStruct((devices // 2, chunk_rows, LANES), F32),
        compiler_params=params(60),
        cost_estimate=pl.CostEstimate(
            flops=2 * rows * width * LIVE,
            bytes_accessed=2 * rows * width + 2 * LIVE * width,
            transcendentals=0,
        ),
        name="keep",
    )(info, tangent, hidden, down_rows, krylov_down)

    jobs = [(krylov_gate, part) for part in range(parts)]
    jobs += [(krylov_up, part) for part in range(parts)]
    plan = {1: 2, 2: 1, 3: 1}
    prods = []
    for bit in range(1, bits):
        part = keep.shape[0] // 2
        send = (keep[part:] + got[part:].astype(F32)).astype(BF16)
        keep = keep[:part] + got[:part].astype(F32)
        got = exchange(send, bit)
        for _ in range(plan.get(bit, 0)):
            krylov, at = jobs[len(prods)]
            prods.append(product(krylov, at, prods[-1][0] if prods else send))
        if plan.get(bit, 0):
            got, last = lax.optimization_barrier((got, prods[-1]))
            prods[-1] = last
    square = prods[0][1]
    prods = [one for one, _ in prods]
    loss_own = (keep + got.astype(F32)).astype(BF16)

    def half_call(lower):
        return pl.pallas_call(
            functools.partial(back_half_kernel, splits),
            grid_spec=pltpu.PrefetchScalarGridSpec(
                num_scalar_prefetch=1,
                grid=(half,),
                in_specs=[
                    pl.BlockSpec((places, chunk_rows, LANES), lambda step, info: (step, 0, 0)),
                    pl.BlockSpec((rows, cols), lambda step, info: (0, keep_col(step, info))),
                    pl.BlockSpec(
                        (basis, rows, cols), lambda step, info: (0, 0, keep_col(step, info))
                    ),
                ],
                out_specs=[whole(((basis + 1) * rows, LIVE)), whole((LIVE, LIVE))],
            ),
            out_shape=[
                jax.ShapeDtypeStruct(((basis + 1) * rows, LIVE), F32),
                jax.ShapeDtypeStruct((LIVE, LIVE), F32),
            ],
            compiler_params=params(60),
            cost_estimate=pl.CostEstimate(
                flops=(basis + 1) * rows * width * LIVE,
                bytes_accessed=(basis + 1) * rows * width + 4 * (basis + 1) * rows * LIVE,
                transcendentals=0,
            ),
            name="back_half",
        )(info, lower, down_rows, krylov_down)

    beside = {0: half_call}
    if grams[-1] is None:
        beside[1] = down_high
    lower, upper, made = gather_blocks(loss_own, bits, beside)
    sums_half, loss_square_half = made[-1]
    if grams[-1] is None:
        grams[-1] = made[0]
    grams = jnp.stack(grams)

    def back_col(step, info):
        return (half + step) ^ (info[0] // places)

    anywhere = pl.BlockSpec(memory_space=pl.ANY)
    s_term, r_term, stats = pl.pallas_call(
        functools.partial(back_kernel, half, inv_d, inv_ff, splits, parts),
        grid_spec=pltpu.PrefetchScalarGridSpec(
            num_scalar_prefetch=1,
            grid=(half,),
            in_specs=[
                pl.BlockSpec((places, chunk_rows, LANES), lambda step, info: (step, 0, 0)),
                pl.BlockSpec((rows, cols), lambda step, info: (0, back_col(step, info))),
                pl.BlockSpec((basis, rows, cols), lambda step, info: (0, 0, back_col(step, info))),
                whole((rows, LIVE)),
                whole((rows, LIVE)),
                whole((rows, LIVE)),
                whole((LIVE, LIVE)),
                whole((LIVE, LIVE)),
                whole(grams.shape),
                anywhere,
            ]
            + [anywhere] * (2 * parts),
            out_specs=[
                whole((rows, LIVE)),
                whole((rows, LIVE)),
                whole((3 * basis, LANES)),
            ],
            scratch_shapes=[
                pltpu.VMEM(((basis + 1) * rows, LIVE), F32),
                pltpu.VMEM((LIVE, LIVE), F32),
                pltpu.VMEM(((basis + 1) * rows, LIVE), F32),
                pltpu.VMEM((basis, rows, LIVE), F32),
                pltpu.VMEM((basis, rows, LIVE), F32),
                pltpu.SemaphoreType.DMA((1 + 2 * parts,)),
            ],
        ),
        out_shape=[
            jax.ShapeDtypeStruct((rows, LIVE), BF16),
            jax.ShapeDtypeStruct((rows, LIVE), BF16),
            jax.ShapeDtypeStruct((3 * basis, LANES), F32),
        ],
        compiler_params=params(60),
        cost_estimate=pl.CostEstimate(
            flops=(basis + 1) * rows * width * LIVE,
            bytes_accessed=(basis + 1) * rows * width + 12 * basis * rows * LIVE,
            transcendentals=0,
        ),
        name="back",
    )(
        info, upper, down_rows, krylov_down, hidden, weight, act, square, loss_square_half, grams,
        sums_half, *prods,
    )

    for bit in range(bits):
        stats = stats + exchange(stats, bit)

    narrow = min(256, cols)
    steps = width // narrow
    near = devices // steps

    def new_col(step, info):
        return step ^ (info[0] // near)

    krylov_spec = pl.BlockSpec(
        (basis, rows, narrow), lambda step, info: (0, 0, new_col(step, info))
    )
    out_spec = pl.BlockSpec((rows, narrow), lambda step, info: (0, new_col(step, info)))
    out_shape = jax.ShapeDtypeStruct((rows, width), BF16)
    new_gate, new_up, new_down, coefficients = pl.pallas_call(
        functools.partial(new_kernel, basis, count, inv_d, inv_ff, splits, lines),
        grid_spec=pltpu.PrefetchScalarGridSpec(
            num_scalar_prefetch=1,
            grid=(steps,),
            in_specs=[
                pl.BlockSpec(memory_space=pltpu.SMEM),
                whole((rows, LIVE)),
                whole((rows, LIVE)),
                whole((rows, LIVE)),
                pl.BlockSpec((LIVE, narrow), lambda step, info: (0, new_col(step, info))),
                pl.BlockSpec(
                    (near, chunk_rows, LANES),
                    lambda step, info: (jnp.minimum(step, steps // 2 - 1), 0, 0),
                ),
                pl.BlockSpec(
                    (near, chunk_rows, LANES),
                    lambda step, info: (jnp.maximum(step - steps // 2, 0), 0, 0),
                ),
                krylov_spec,
                krylov_spec,
                krylov_spec,
            ],
            out_specs=[out_spec, out_spec, out_spec, pl.BlockSpec(memory_space=pltpu.SMEM)],
            scratch_shapes=[
                pltpu.SMEM((1,), F32),
                pltpu.VMEM((3 * lines, basis * lines), BF16),
                pltpu.VMEM((rows, narrow), F32),
            ],
        ),
        out_shape=[
            out_shape,
            out_shape,
            out_shape,
            jax.ShapeDtypeStruct((basis + 1,), F32),
        ],
        compiler_params=params(60),
        cost_estimate=pl.CostEstimate(
            flops=6 * rows * width * LIVE,
            bytes_accessed=6 * (basis + 1) * rows * width,
            transcendentals=0,
        ),
        name="new",
    )(
        info, stats, s_term, r_term, hidden, normed, lower, upper, krylov_gate, krylov_up,
        krylov_down,
    )
    return (new_gate, new_up, new_down, coefficients)


def solution(mesh):
    placed = (
        P("fsdp", None),
        P(),
        P(),
        P("fsdp", None),
        P("fsdp", None),
        P("fsdp", None),
        P(None, "fsdp", None),
        P(None, "fsdp", None),
        P(None, "fsdp", None),
    )
    return jax.shard_map(
        per_device,
        mesh=mesh,
        in_specs=placed,
        out_specs=(P("fsdp", None), P("fsdp", None), P("fsdp", None), P()),
        check_vma=False,
    )
```

```python
import functools
import math

import jax
import jax.numpy as jnp
from jax import lax
from jax.experimental import pallas as pl
from jax.experimental.pallas import tpu as pltpu
from jax.sharding import PartitionSpec as P

LEN = 128
LIVE = 192
GROUP = 8
LANES = 128
F32 = jnp.float32
BF16 = jnp.bfloat16


def gelu_pair(gate_pre):
    coef = math.sqrt(2.0 / math.pi)
    cube = gate_pre * gate_pre * gate_pre
    tanh_val = jnp.tanh(coef * (gate_pre + 0.044715 * cube))
    act = 0.5 * gate_pre * (1.0 + tanh_val)
    slope = 0.5 * (1.0 + tanh_val) + 0.5 * gate_pre * (1.0 - tanh_val * tanh_val) * coef * (
        1.0 + 3.0 * 0.044715 * gate_pre * gate_pre
    )
    return (act, slope)


def dot_nn(left, right):
    return jnp.dot(left, right, preferred_element_type=F32)


def dot_nt(left, right):
    return lax.dot_general(left, right, (((1,), (1,)), ((), ())), preferred_element_type=F32)


def dot_tn(left, right):
    return lax.dot_general(left, right, (((0,), (0,)), ((), ())), preferred_element_type=F32)


def total(values):
    return jnp.sum(jnp.sum(values, axis=0, keepdims=True), axis=1, keepdims=True)


def reverse_bits(value, bits):
    out = value * 0
    for bit in range(bits):
        out = out | (((value >> bit) & 1) << (bits - 1 - bit))
    return out


def exchange(block, bit):
    count = lax.axis_size("fsdp")
    return lax.ppermute(block, "fsdp", [(one, one ^ (1 << bit)) for one in range(count)])


def gather_blocks(block, bits, beside):
    for bit in reversed(range(bits)):
        other = exchange(block, bit)
        if bit in beside:
            work, done = beside[bit]
            other, extra = lax.optimization_barrier((other, work(block)))
            done(extra)
        if bit:
            block = jnp.concatenate([block, other], axis=0)
    return block, other


def after(value, earlier):
    return lax.optimization_barrier((value, earlier))[0]


def stacked(krylov):
    basis, rows, width = krylov.shape
    if rows % 16:
        return krylov.astype(F32).reshape(basis * rows, width).astype(BF16)
    return krylov.reshape(basis * rows, width)


def params(mib):
    return pltpu.CompilerParams(vmem_limit_bytes=mib << 20)


def cost(flops, read, transcendentals=0):
    return pl.CostEstimate(flops=flops, bytes_accessed=read, transcendentals=transcendentals)


FAST = pl.BlockSpec(memory_space=pltpu.VMEM)
SMALL = pl.BlockSpec(memory_space=pltpu.SMEM)
FAR = pl.BlockSpec(memory_space=pltpu.HBM)


def block_rows(rows):
    return 64 if rows % 64 == 0 else rows


def half_start(flip, devices, width, other):
    top = lax.div(flip, devices // 2) ^ other
    return pl.multiple_of(top * (width // 2), width // 2)


def live_tokens(info, lower, upper, gain, normed, spots):
    spare = info[1] - (LIVE - LEN)
    shift = lax.rem(spare, GROUP)
    half = (LIVE - LEN) // GROUP
    per = LEN // GROUP
    scale = gain[...].astype(F32)
    row_ids = lax.broadcasted_iota(jnp.int32, (GROUP, 1), 0)

    half_groups = lower.shape[0]

    def load(group):
        spot = spots(info[0], group)
        place = lax.rem(spot, half_groups)
        return jnp.where(spot < half_groups, lower[place], upper[place]).astype(F32)

    def tokens(slot):
        if slot < half:
            return load(slot)
        if slot < 2 * half:
            at = slot - half
            first = load(half + at)
            second = pltpu.roll(load(per + 2 * half - 1 - at), shift, 0)
            return jnp.where(GROUP * at + row_ids < spare, first, second)
        return load(per + slot - 2 * half)

    def norm(wide):
        mean = jnp.mean(wide * wide, axis=1, keepdims=True)
        return wide * lax.rsqrt(mean + 1e-06) * scale

    for pair in range(LIVE // (2 * GROUP)):
        both = [norm(tokens(2 * pair + side)) for side in range(2)]
        normed[2 * GROUP * pair : 2 * GROUP * (pair + 1), :] = jnp.concatenate(both, 0).astype(BF16)


def jvp_half(info, tangent_t, hidden_t, down, probe, out, inv_ff, splits):
    rows = LIVE // splits
    places = out.shape[0]
    width = down.shape[1]
    step = min(512, width)
    each = step // LANES
    for at in range(width // step):
        here = slice(at * step, (at + 1) * step)
        values = dot_nn(tangent_t, down[:, here]) + dot_nn(hidden_t, probe[:, here]) * inv_ff
        for column in range(each):
            for part in range(splits):
                piece = values[
                    part * rows : (part + 1) * rows, column * LANES : (column + 1) * LANES
                ]
                chunk = (at * each + column) * splits + part
                out[chunk ^ (info[0] & (places - 1))] = piece.astype(out.dtype)


def down_copies(info, devices, other, sources, held, sems):
    width = held.shape[2]
    start = half_start(info[0], devices, 2 * width, other)
    return [
        pltpu.make_async_copy(source.at[:, pl.ds(start, width)], held.at[at], sems.at[at])
        for at, source in enumerate(sources)
    ]


def forward_kernel(
    devices, inv_d, inv_ff, spots, splits,
    info, lower, upper, gain, gate, up, krylov_gate, krylov_up, down, krylov_down,
    normed, hidden, tangent_t, hidden_t, weight, act_out, send,
    held, held_down, tangent, sems, down_sems,
):
    basis = krylov_gate.shape[0]
    count, _, lines, width = held.shape
    sources = (gate, up, krylov_gate.at[basis - 1], krylov_up.at[basis - 1])
    copies = [
        [
            pltpu.make_async_copy(
                source.at[at * lines : (at + 1) * lines], held.at[at, one], sems.at[at, one]
            )
            for one, source in enumerate(sources)
        ]
        for at in range(count)
    ]
    last = down_copies(
        info, devices, 1, (down, krylov_down.at[basis - 1]), held_down, down_sems
    )
    for copy in sum(copies, []) + last:
        copy.start()
    live_tokens(info, lower, upper, gain, normed, spots)
    for at in range(count):
        for copy in copies[at]:
            copy.wait()
        made = dot_nt(stacked(held[at]), normed[...])
        gate_pre, up_pre, tan_gate, tan_up = (
            made[one * lines : (one + 1) * lines] for one in range(4)
        )
        act, slope = gelu_pair(gate_pre)
        here = slice(at * lines, (at + 1) * lines)
        hidden[here, :] = (act * up_pre).astype(BF16)
        tangent[here, :] = (
            slope * (tan_gate * inv_d) * up_pre + act * (tan_up * inv_d)
        ).astype(BF16)
        weight[here, :] = up_pre * slope
        act_out[here, :] = act
    tangent_t[...] = tangent[...].T
    hidden_t[...] = hidden[...].T
    for copy in last:
        copy.wait()
    jvp_half(
        info, tangent_t[...], hidden_t[...], held_down.at[0], held_down.at[1], send, inv_ff, splits
    )


def keep_kernel(
    devices, inv_ff, splits,
    info, tangent_t, hidden_t, down, krylov_down, keep, held_down, sems,
):
    basis = krylov_down.shape[0]
    copies = down_copies(info, devices, 0, (down, krylov_down.at[basis - 1]), held_down, sems)
    for copy in copies:
        copy.start()
    for copy in copies:
        copy.wait()
    jvp_half(
        info, tangent_t[...], hidden_t[...], held_down.at[0], held_down.at[1], keep, inv_ff, splits
    )


def row_copies(krylov, first, held, sems):
    count, _, lines, _ = held.shape

    def copy(at):
        start = (first + at) * lines
        if not isinstance(at, int):
            start = pl.multiple_of(start, lines)
        return pltpu.make_async_copy(
            krylov.at[:, pl.ds(start, lines), :], held.at[at], sems.at[at]
        )

    for at in range(count):
        copy(at).start()
    return copy


def gram_kernel(first, start, fold, krylov, earlier, out, held, sums, sems):
    count, basis, lines, _ = held.shape
    copy = row_copies(krylov, first, held, sems)
    sums[...] = jnp.zeros_like(sums) if start else earlier[...]

    def body(at, carry):
        copy(at).wait()
        stack = stacked(held[at])
        sums[...] += dot_nt(stack, stack)
        return carry

    lax.fori_loop(0, count, body, 0)
    if not fold:
        out[...] = sums[...]
        return
    size = basis * lines
    own = lax.broadcasted_iota(jnp.int32, (size, size), 0)
    other = lax.broadcasted_iota(jnp.int32, (size, size), 1)
    if lines & (lines - 1) == 0:
        same = (own & (lines - 1)) == (other & (lines - 1))
    else:
        same = lax.rem(own, lines) == lax.rem(other, lines)
    kept = jnp.where(same, sums[...], 0.0)
    rows = [
        jnp.sum(kept[one * lines : (one + 1) * lines], axis=0, keepdims=True)
        for one in range(basis)
    ]
    place = lax.broadcasted_iota(jnp.int32, (size, LANES), 0)
    lane = lax.broadcasted_iota(jnp.int32, (size, LANES), 1) * lines
    picks = jnp.where((place >= lane) & (place < lane + lines), 1.0, 0.0).astype(F32)
    out[...] = jnp.dot(
        jnp.concatenate(rows, axis=0), picks,
        precision=lax.Precision.HIGHEST, preferred_element_type=F32,
    )


def product_kernel(krylov, normed, out, square, held, sems):
    count, basis, lines, _ = held.shape
    copy = row_copies(krylov, 0, held, sems)
    square[...] = dot_nt(normed[...], normed[...])

    def body(at, carry):
        copy(at).wait()
        made = dot_nt(stacked(held[at]), normed[...])
        here = pl.ds(pl.multiple_of(at * lines, lines), lines)
        for one in range(basis):
            out[one, here, :] = made[one * lines : (one + 1) * lines]
        return carry

    lax.fori_loop(0, count, body, 0)


def loss_columns(flip, load, places, splits):
    made = []
    for column in range(places // splits):
        pieces = [
            load((column * splits + part) ^ (flip & (places - 1))) for part in range(splits)
        ]
        if splits > 1:
            pieces = [jnp.concatenate([one.astype(F32) for one in pieces], 0).astype(BF16)]
        made.append(pieces[0])
    return jnp.concatenate(made, axis=1)


def back_copies(info, devices, other, down, krylov, held_down, held, sems):
    count, _, lines, width = held.shape
    start = half_start(info[0], devices, 2 * width, other)
    columns = pl.ds(start, width)
    copies = [
        pltpu.make_async_copy(
            krylov.at[:, at * lines : (at + 1) * lines, columns], held.at[at], sems.at[at]
        )
        for at in range(count)
    ]
    return copies, pltpu.make_async_copy(down.at[:, columns], held_down, sems.at[count])


def back_half_kernel(
    devices, splits,
    info, chunks, down, krylov, sums, back_sum, square,
    loss, held_down, held, sems,
):
    count, basis, lines, _ = held.shape
    copies, first = back_copies(info, devices, 0, down, krylov, held_down, held, sems)
    for copy in [first] + copies:
        copy.start()
    loss[...] = loss_columns(info[0], lambda at: chunks[at], chunks.shape[0], splits)
    square[...] = dot_nt(loss[...], loss[...])
    first.wait()
    back_sum[...] = dot_nt(held_down[...], loss[...])
    for at in range(count):
        copies[at].wait()
        made = dot_nt(stacked(held[at]), loss[...])
        for one in range(basis):
            sums[one, at * lines : (at + 1) * lines, :] = made[one * lines : (one + 1) * lines]


def back_kernel(
    devices, inv_d, inv_ff, splits,
    info, chunks, down, krylov, hidden, weight, act, square, loss_square_half, back_half, grams,
    sums_half, prod_gate, prod_up,
    s_out, r_out, stats,
    loss, held_down, held, half_held, gate_held, up_held, sems, more_sems,
):
    count, basis, lines, _ = held.shape
    copies, first = back_copies(info, devices, 1, down, krylov, held_down, held, sems)
    more = [
        pltpu.make_async_copy(source, target, more_sems.at[at])
        for at, (source, target) in enumerate(
            ((prod_gate, gate_held), (prod_up, up_held), (sums_half, half_held))
        )
    ]
    for copy in [first] + more + copies:
        copy.start()
    loss[...] = loss_columns(info[0], lambda at: chunks[at], chunks.shape[0], splits)
    first.wait()
    back = dot_nt(held_down[...], loss[...]) + back_half[...]
    s_term = (back * weight[...]).astype(BF16)
    r_term = (back * act[...]).astype(BF16)
    s_out[...] = s_term
    r_out[...] = r_term
    wide = hidden[...]
    squares = inv_d * inv_d * ((dot_tn(s_term, s_term) + dot_tn(r_term, r_term)) * square[...])
    other = dot_nt(loss[...], loss[...]) + loss_square_half[...]
    squares = total(squares + inv_ff * inv_ff * (dot_tn(wide, wide) * other))
    stats[basis : 2 * basis, :] = jnp.broadcast_to(squares, (basis, LANES))
    stats[2 * basis : 3 * basis, :] = grams[...]
    for copy in more:
        copy.wait()
    wide_s = s_term.astype(F32) * inv_d
    wide_r = r_term.astype(F32) * inv_d
    wide_h = wide.astype(F32) * inv_ff
    values = []
    for one in range(basis):
        value = wide_s * gate_held[one] + wide_r * up_held[one] + wide_h * half_held[one]
        values.append(jnp.sum(value, axis=0, keepdims=True))
    for at in range(count):
        copies[at].wait()
        made = dot_nt(stacked(held[at]), loss[...])
        part = wide_h[at * lines : (at + 1) * lines]
        for one in range(basis):
            value = part * made[one * lines : (one + 1) * lines]
            values[one] = values[one] + jnp.sum(value, axis=0, keepdims=True)
    lined = jnp.sum(jnp.concatenate(values, axis=0), axis=1, keepdims=True)
    stats[0:basis, :] = jnp.broadcast_to(lined, (basis, LANES))


def split_three(value):
    first = value.astype(BF16)
    rest = value - first.astype(F32)
    second = rest.astype(BF16)
    return first, second, (rest - second.astype(F32)).astype(BF16)


def new_kernel(
    basis, count, inv_d, inv_ff, splits,
    info, stats, s_term, r_term, hidden, normed, lower, upper,
    krylov_gate, krylov_up, krylov_down,
    new_gate, new_up, new_down, coefficients,
    loss, wide, held, outs, sems, out_sems,
):
    depth, _, lines, width = held.shape
    outs_depth = outs.shape[0]
    rows = s_term.shape[0]
    number = rows // lines
    size = basis * lines
    sources = (krylov_gate, krylov_up, krylov_down)
    targets = (new_gate, new_up, new_down)

    def rows_at(at):
        return pl.ds(pl.multiple_of(at * lines, lines), lines)

    def copy_in(part, at):
        slot = lax.rem(part * number + at, depth)
        return pltpu.make_async_copy(
            sources[part].at[:, rows_at(at), :], held.at[slot], sems.at[slot]
        )

    def copy_out(part, at):
        slot = lax.rem(part * number + at, outs_depth)
        return pltpu.make_async_copy(
            outs.at[slot], targets[part].at[rows_at(at), :], out_sems.at[slot]
        )

    def fetch(turn):
        for part in range(3):
            @pl.when((turn >= part * number) & (turn < (part + 1) * number))
            def _(part=part):
                copy_in(part, turn - part * number).start()

    for turn in range(min(depth - 1, 3 * number)):
        copy_in(turn // number, turn % number).start()

    half_places = lower.shape[0]

    def load(place):
        at = place & (half_places - 1)
        return jnp.where(place < half_places, lower[at], upper[at])

    loss[...] = loss_columns(info[0], load, 2 * half_places, splits)
    proj = [stats[one, 0] / count for one in range(basis)]
    squares = stats[basis, 0]
    for one in range(basis):
        line = stats[2 * basis + one, 0] * proj[0]
        for two in range(1, basis):
            line = line + stats[2 * basis + one, two] * proj[two]
        squares = squares + proj[one] * (line - 2.0 * stats[one, 0])
    mean = jnp.maximum(jnp.full((8, LANES), squares / count, F32), 0.0)
    norm = jnp.sqrt(mean + 1e-06)
    inverse = jnp.max(1.0 / norm)
    for one in range(basis):
        coefficients[one] = proj[one]
    coefficients[basis] = jnp.max(norm)
    lane = lax.broadcasted_iota(jnp.int32, (lines, size), 1)
    row = lax.broadcasted_iota(jnp.int32, (lines, size), 0)
    values = jnp.zeros((lines, size), F32)
    for one in range(basis):
        values = jnp.where(lane == one * lines + row, proj[one] * inverse, values)
    terms = [term.astype(F32) for term in split_three(values)]
    mix = jnp.concatenate(terms, axis=0).astype(BF16)

    for part, (left, right, scale) in enumerate(
        ((s_term, normed, inv_d), (r_term, normed, inv_d), (hidden, loss, inv_ff))
    ):
        wide[...] = dot_nn(left[...], right[...]) * (scale * inverse)

        def body(at, carry, part=part):
            turn = part * number + at
            fetch(turn + depth - 1)
            copy_in(part, at).wait()

            @pl.when(turn >= outs_depth)
            def _():
                copy_out(part, at).wait()

            mixed = dot_nn(mix, stacked(held[lax.rem(turn, depth)]))
            mixed = mixed[:lines] + (mixed[lines : 2 * lines] + mixed[2 * lines :])
            outs[lax.rem(turn, outs_depth)] = (wide[rows_at(at), :] - mixed).astype(BF16)
            copy_out(part, at).start()
            return carry

        lax.fori_loop(0, number, body, 0)
    for turn in range(max(0, 3 * number - outs_depth), 3 * number):
        copy_out(turn // number, turn % number).wait()


def per_device(
    inputs, norm_gain, lengths, gate_rows, up_rows, down_rows, krylov_gate, krylov_up, krylov_down
):
    basis, rows, width = krylov_gate.shape
    devices = lax.axis_size("fsdp")
    bits = devices.bit_length() - 1
    hidden_all = rows * devices
    count = 3.0 * width * hidden_all
    inv_d = 1.0 / math.sqrt(width)
    inv_ff = 1.0 / math.sqrt(hidden_all)
    me = lax.axis_index("fsdp").astype(jnp.int32)
    mirror = reverse_bits(me, bits)
    info = jnp.stack([mirror, lengths[0]])

    splits = devices // (width // LANES)
    chunk_rows = LIVE // splits
    lines = 32 if rows % 32 == 0 else rows
    pieces = rows // lines
    long = block_rows(rows)
    halved = width // 2
    product_flops = 2 * rows * width * LIVE

    def gram(krylov, first, number, fold, earlier, before):
        size = basis * lines
        start = earlier is None
        if start:
            earlier = jnp.zeros((8, LANES), F32)
        krylov = krylov if before is None else after(krylov, before)
        out = (basis, LANES) if fold else (size, size)
        return pl.pallas_call(
            functools.partial(gram_kernel, first, start, fold),
            in_specs=[FAR, FAST],
            out_specs=FAST,
            out_shape=jax.ShapeDtypeStruct(out, F32),
            scratch_shapes=[
                pltpu.VMEM((number, basis, lines, width), BF16),
                pltpu.VMEM((size, size), F32),
                pltpu.SemaphoreType.DMA((number,)),
            ],
            compiler_params=params(46),
            cost_estimate=cost(2 * size * size * width * number, 2 * size * width * number),
            name="gram",
        )(krylov, earlier)

    cut = (pieces + 1) // 2
    spans = [
        (krylov, first, number)
        for krylov in (krylov_gate, krylov_up, krylov_down)
        for first, number in ((0, cut), (cut, pieces - cut))
        if number
    ]
    gram_sums = []

    def next_gram(before):
        krylov, first, number = spans[len(gram_sums)]
        fold = len(gram_sums) == len(spans) - 1
        earlier = gram_sums[-1] if gram_sums else None
        gram_sums.append(gram(krylov, first, number, fold, earlier, before))
        return gram_sums[-1]

    def done_gram(value):
        gram_sums[-1] = value

    own_tokens = inputs.shape[0]
    tokens = own_tokens * devices
    if own_tokens % GROUP == 0:
        sub = own_tokens // GROUP
        lower, upper = gather_blocks(
            inputs.reshape(sub, GROUP, width),
            bits,
            {bit: (next_gram, done_gram) for bit in range(min(bits, len(spans) - 1))},
        )

        def spots(flip, group):
            return (reverse_bits(group // sub, bits) ^ flip) * sub + group % sub

    else:
        gathered = lax.all_gather(inputs, "fsdp", axis=0, tiled=True)
        gathered = gathered.reshape(tokens // GROUP, GROUP, width)
        lower, upper = jnp.split(gathered, 2)

        def spots(flip, group):
            return group

    normed, hidden, tangent_t, hidden_t, weight, act, send = pl.pallas_call(
        functools.partial(forward_kernel, devices, inv_d, inv_ff, spots, splits),
        in_specs=[SMALL] + [FAST] * 3 + [FAR] * 6,
        out_specs=[FAST] * 7,
        out_shape=[
            jax.ShapeDtypeStruct((LIVE, width), BF16),
            jax.ShapeDtypeStruct((rows, LIVE), BF16),
            jax.ShapeDtypeStruct((LIVE, rows), BF16),
            jax.ShapeDtypeStruct((LIVE, rows), BF16),
            jax.ShapeDtypeStruct((rows, LIVE), F32),
            jax.ShapeDtypeStruct((rows, LIVE), F32),
            jax.ShapeDtypeStruct((devices // 2, chunk_rows, LANES), BF16),
        ],
        scratch_shapes=[
            pltpu.VMEM((rows // long, 4, long, width), BF16),
            pltpu.VMEM((2, rows, halved), BF16),
            pltpu.VMEM((rows, LIVE), BF16),
            pltpu.SemaphoreType.DMA((rows // long, 4)),
            pltpu.SemaphoreType.DMA((2,)),
        ],
        compiler_params=params(46),
        cost_estimate=cost(5 * product_flops, 10 * rows * width + 6 * LIVE * width, rows * LIVE),
        name="forward",
    )(
        info, lower, upper, norm_gain.reshape(1, width), gate_rows, up_rows, krylov_gate,
        krylov_up, down_rows, krylov_down,
    )

    def product(krylov, before):
        return pl.pallas_call(
            product_kernel,
            in_specs=[FAR, FAST],
            out_specs=[FAST, FAST],
            out_shape=[
                jax.ShapeDtypeStruct((basis, rows, LIVE), F32),
                jax.ShapeDtypeStruct((LIVE, LIVE), F32),
            ],
            scratch_shapes=[
                pltpu.VMEM((pieces, basis, lines, width), BF16),
                pltpu.SemaphoreType.DMA((pieces,)),
            ],
            compiler_params=params(46),
            cost_estimate=cost(
                basis * product_flops, 2 * basis * rows * width + 4 * basis * rows * LIVE
            ),
            name="product",
        )(after(krylov, before), normed)

    got = exchange(send, 0)
    keep = pl.pallas_call(
        functools.partial(keep_kernel, devices, inv_ff, splits),
        in_specs=[SMALL, FAST, FAST, FAR, FAR],
        out_specs=FAST,
        out_shape=jax.ShapeDtypeStruct((devices // 2, chunk_rows, LANES), F32),
        scratch_shapes=[
            pltpu.VMEM((2, rows, halved), BF16),
            pltpu.SemaphoreType.DMA((2,)),
        ],
        compiler_params=params(46),
        cost_estimate=cost(product_flops, 2 * rows * width + 2 * LIVE * width),
        name="keep",
    )(info, tangent_t, hidden_t, down_rows, krylov_down)

    plan = {1: krylov_gate, 2: krylov_up}
    prods = []
    for bit in range(1, bits):
        part = keep.shape[0] // 2
        send = (keep[part:] + got[part:].astype(F32)).astype(BF16)
        keep = keep[:part] + got[:part].astype(F32)
        got = exchange(send, bit)
        if bit in plan:
            got, made = lax.optimization_barrier((got, product(plan[bit], send)))
            prods.append(made)
    (prod_gate, square), (prod_up, _) = prods
    loss_own = (keep + got.astype(F32)).astype(BF16)

    def half_call(lower):
        return pl.pallas_call(
            functools.partial(back_half_kernel, devices, splits),
            in_specs=[SMALL, FAST, FAR, FAR],
            out_specs=[FAST] * 3,
            out_shape=[
                jax.ShapeDtypeStruct((basis, rows, LIVE), F32),
                jax.ShapeDtypeStruct((rows, LIVE), F32),
                jax.ShapeDtypeStruct((LIVE, LIVE), F32),
            ],
            scratch_shapes=[
                pltpu.VMEM((LIVE, halved), BF16),
                pltpu.VMEM((rows, halved), BF16),
                pltpu.VMEM((rows // long, basis, long, halved), BF16),
                pltpu.SemaphoreType.DMA((rows // long + 1,)),
            ],
            compiler_params=params(46),
            cost_estimate=cost(
                (basis + 1) * product_flops // 2,
                (basis + 1) * rows * width + 4 * basis * rows * LIVE,
            ),
            name="back_half",
        )(info, lower, down_rows, krylov_down)

    halves = []
    beside = {0: (half_call, halves.extend)}
    if 0 < len(gram_sums) < len(spans):
        beside[1] = (next_gram, done_gram)
    lower, upper = gather_blocks(loss_own, bits, beside)
    while len(gram_sums) < len(spans):
        next_gram(None)
    sums_half, back_half, loss_square_half = halves

    s_term, r_term, stats = pl.pallas_call(
        functools.partial(back_kernel, devices, inv_d, inv_ff, splits),
        in_specs=[SMALL, FAST, FAR, FAR] + [FAST] * 7 + [pl.BlockSpec(memory_space=pl.ANY)] * 3,
        out_specs=[FAST] * 3,
        out_shape=[
            jax.ShapeDtypeStruct((rows, LIVE), BF16),
            jax.ShapeDtypeStruct((rows, LIVE), BF16),
            jax.ShapeDtypeStruct((3 * basis, LANES), F32),
        ],
        scratch_shapes=[
            pltpu.VMEM((LIVE, halved), BF16),
            pltpu.VMEM((rows, halved), BF16),
            pltpu.VMEM((rows // long, basis, long, halved), BF16),
            pltpu.VMEM((basis, rows, LIVE), F32),
            pltpu.VMEM((basis, rows, LIVE), F32),
            pltpu.VMEM((basis, rows, LIVE), F32),
            pltpu.SemaphoreType.DMA((rows // long + 1,)),
            pltpu.SemaphoreType.DMA((3,)),
        ],
        compiler_params=params(46),
        cost_estimate=cost(
            (basis + 1) * product_flops // 2,
            (basis + 1) * rows * width + 12 * basis * rows * LIVE,
        ),
        name="back",
    )(
        info, upper, down_rows, krylov_down, hidden, weight, act, square, loss_square_half,
        back_half, gram_sums[-1], sums_half, prod_gate, prod_up,
    )

    for bit in range(bits):
        stats = stats + exchange(stats, bit)

    depth, outs_depth = min(8, 3 * pieces), min(4, 3 * pieces)
    out_shape = jax.ShapeDtypeStruct((rows, width), BF16)
    new_gate, new_up, new_down, coefficients = pl.pallas_call(
        functools.partial(new_kernel, basis, count, inv_d, inv_ff, splits),
        in_specs=[SMALL, SMALL] + [FAST] * 6 + [FAR] * 3,
        out_specs=[FAR] * 3 + [SMALL],
        out_shape=[out_shape, out_shape, out_shape, jax.ShapeDtypeStruct((basis + 1,), F32)],
        scratch_shapes=[
            pltpu.VMEM((LIVE, width), BF16),
            pltpu.VMEM((rows, width), F32),
            pltpu.VMEM((depth, basis, lines, width), BF16),
            pltpu.VMEM((outs_depth, lines, width), BF16),
            pltpu.SemaphoreType.DMA((depth,)),
            pltpu.SemaphoreType.DMA((outs_depth,)),
        ],
        compiler_params=params(46),
        cost_estimate=cost(3 * product_flops, 6 * (basis + 1) * rows * width),
        name="new",
    )(
        info, stats, s_term, r_term, hidden, normed, lower, upper, krylov_gate, krylov_up,
        krylov_down,
    )
    return (new_gate, new_up, new_down, coefficients)


def solution(mesh):
    placed = (
        P("fsdp", None),
        P(),
        P(),
        P("fsdp", None),
        P("fsdp", None),
        P("fsdp", None),
        P(None, "fsdp", None),
        P(None, "fsdp", None),
        P(None, "fsdp", None),
    )
    return jax.shard_map(
        per_device,
        mesh=mesh,
        in_specs=placed,
        out_specs=(P("fsdp", None), P("fsdp", None), P("fsdp", None), P()),
        check_vma=False,
    )
```

```python
import functools
import math

import jax
import jax.numpy as jnp
from jax import lax
from jax.experimental import pallas as pl
from jax.experimental.pallas import tpu as pltpu
from jax.sharding import PartitionSpec as P

LEN = 128
LIVE = 192
GROUP = 8
LANES = 128
F32 = jnp.float32
BF16 = jnp.bfloat16


def gelu_pair(gate_pre):
    coef = math.sqrt(2.0 / math.pi)
    cube = gate_pre * gate_pre * gate_pre
    tanh_val = jnp.tanh(coef * (gate_pre + 0.044715 * cube))
    act = 0.5 * gate_pre * (1.0 + tanh_val)
    slope = 0.5 * (1.0 + tanh_val) + 0.5 * gate_pre * (1.0 - tanh_val * tanh_val) * coef * (
        1.0 + 3.0 * 0.044715 * gate_pre * gate_pre
    )
    return (act, slope)


def dot_nn(left, right):
    return jnp.dot(left, right, preferred_element_type=F32)


def dot_nt(left, right):
    return lax.dot_general(left, right, (((1,), (1,)), ((), ())), preferred_element_type=F32)


def dot_tn(left, right):
    return lax.dot_general(left, right, (((0,), (0,)), ((), ())), preferred_element_type=F32)


def total(values):
    return jnp.sum(jnp.sum(values, axis=0, keepdims=True), axis=1, keepdims=True)


def reverse_bits(value, bits):
    out = value * 0
    for bit in range(bits):
        out = out | (((value >> bit) & 1) << (bits - 1 - bit))
    return out


def exchange(block, flip):
    count = lax.axis_size("fsdp")
    return lax.ppermute(block, "fsdp", [(one, one ^ flip) for one in range(count)])


def bit_groups(bits):
    return [(0, 1)] + [(low, min(2, bits - low)) for low in range(1, bits, 2)]


def flips(group):
    low, size = group
    return [reverse_bits(part, size) << low for part in range(1, 1 << size)]


def gather_blocks(block, groups, beside):
    for group in reversed(groups):
        others = [exchange(block, flip) for flip in flips(group)]
        job = beside(group, block)
        if job is not None:
            work, done = job
            others, made = lax.optimization_barrier((others, work))
            done(made)
        if group[0]:
            block = jnp.concatenate([block] + others, axis=0)
    return block, others[0]


def add_up(values):
    while len(values) > 1:
        values = [one + two for one, two in zip(values[0::2], values[1::2])]
    return values[0]


def far(value):
    return pltpu.with_memory_space_constraint(value, pltpu.HBM)


def after(value, earlier):
    return lax.optimization_barrier((value, earlier))[0]


def stacked(krylov):
    basis, rows, width = krylov.shape
    if rows % 16:
        return krylov.astype(F32).reshape(basis * rows, width).astype(BF16)
    return krylov.reshape(basis * rows, width)


def params(mib):
    return pltpu.CompilerParams(vmem_limit_bytes=mib << 20)


def cost(flops, read, transcendentals=0):
    return pl.CostEstimate(flops=flops, bytes_accessed=read, transcendentals=transcendentals)


FAST = pl.BlockSpec(memory_space=pltpu.VMEM)
SMALL = pl.BlockSpec(memory_space=pltpu.SMEM)
FAR = pl.BlockSpec(memory_space=pltpu.HBM)


def block_rows(rows):
    return 64 if rows % 64 == 0 else rows


def half_start(flip, devices, width, other):
    top = lax.div(flip, devices // 2) ^ other
    return pl.multiple_of(top * (width // 2), width // 2)


def live_tokens(info, lower, upper, gain, normed, spots):
    spare = info[1] - (LIVE - LEN)
    shift = lax.rem(spare, GROUP)
    half = (LIVE - LEN) // GROUP
    per = LEN // GROUP
    scale = gain[...].astype(F32)
    row_ids = lax.broadcasted_iota(jnp.int32, (GROUP, 1), 0)

    half_groups = lower.shape[0]

    def load(group):
        spot = spots(info[0], group)
        place = lax.rem(spot, half_groups)
        return jnp.where(spot < half_groups, lower[place], upper[place]).astype(F32)

    def tokens(slot):
        if slot < half:
            return load(slot)
        if slot < 2 * half:
            at = slot - half
            first = load(half + at)
            second = pltpu.roll(load(per + 2 * half - 1 - at), shift, 0)
            return jnp.where(GROUP * at + row_ids < spare, first, second)
        return load(per + slot - 2 * half)

    def norm(wide):
        mean = jnp.mean(wide * wide, axis=1, keepdims=True)
        return wide * lax.rsqrt(mean + 1e-06) * scale

    for pair in range(LIVE // (2 * GROUP)):
        both = [norm(tokens(2 * pair + side)) for side in range(2)]
        normed[2 * GROUP * pair : 2 * GROUP * (pair + 1), :] = jnp.concatenate(both, 0).astype(BF16)


def jvp_half(info, tangent_t, hidden_t, down, probe, out, inv_ff, splits):
    rows = LIVE // splits
    places = out.shape[0]
    width = down.shape[1]
    step = min(512, width)
    each = step // LANES
    for at in range(width // step):
        here = slice(at * step, (at + 1) * step)
        values = dot_nn(tangent_t, down[:, here]) + dot_nn(hidden_t, probe[:, here]) * inv_ff
        for column in range(each):
            for part in range(splits):
                piece = values[
                    part * rows : (part + 1) * rows, column * LANES : (column + 1) * LANES
                ]
                chunk = (at * each + column) * splits + part
                out[chunk ^ (info[0] & (places - 1))] = piece.astype(out.dtype)


def down_copies(info, devices, other, sources, held, sems):
    width = held.shape[2]
    start = half_start(info[0], devices, 2 * width, other)
    return [
        pltpu.make_async_copy(source.at[:, pl.ds(start, width)], held.at[at], sems.at[at])
        for at, source in enumerate(sources)
    ]


def forward_kernel(
    devices, inv_d, inv_ff, spots, splits,
    info, lower, upper, gain, gate, up, krylov_gate, krylov_up, down, krylov_down,
    normed, hidden, tangent_t, hidden_t, weight, act_out, send,
    held, held_down, tangent, sems, down_sems,
):
    basis = krylov_gate.shape[0]
    count, _, lines, width = held.shape
    sources = (gate, up, krylov_gate.at[basis - 1], krylov_up.at[basis - 1])
    copies = [
        [
            pltpu.make_async_copy(
                source.at[at * lines : (at + 1) * lines], held.at[at, one], sems.at[at, one]
            )
            for one, source in enumerate(sources)
        ]
        for at in range(count)
    ]
    last = down_copies(
        info, devices, 1, (down, krylov_down.at[basis - 1]), held_down, down_sems
    )
    for copy in sum(copies, []) + last:
        copy.start()
    live_tokens(info, lower, upper, gain, normed, spots)
    for at in range(count):
        for copy in copies[at]:
            copy.wait()
        made = dot_nt(stacked(held[at]), normed[...])
        gate_pre, up_pre, tan_gate, tan_up = (
            made[one * lines : (one + 1) * lines] for one in range(4)
        )
        act, slope = gelu_pair(gate_pre)
        here = slice(at * lines, (at + 1) * lines)
        hidden[here, :] = (act * up_pre).astype(BF16)
        tangent[here, :] = (
            slope * (tan_gate * inv_d) * up_pre + act * (tan_up * inv_d)
        ).astype(BF16)
        weight[here, :] = up_pre * slope
        act_out[here, :] = act
    tangent_t[...] = tangent[...].T
    hidden_t[...] = hidden[...].T
    for copy in last:
        copy.wait()
    jvp_half(
        info, tangent_t[...], hidden_t[...], held_down.at[0], held_down.at[1], send, inv_ff, splits
    )


def keep_kernel(
    devices, inv_ff, splits,
    info, tangent_t, hidden_t, down, krylov_down, keep, held_down, sems,
):
    basis = krylov_down.shape[0]
    copies = down_copies(info, devices, 0, (down, krylov_down.at[basis - 1]), held_down, sems)
    for copy in copies:
        copy.start()
    for copy in copies:
        copy.wait()
    jvp_half(
        info, tangent_t[...], hidden_t[...], held_down.at[0], held_down.at[1], keep, inv_ff, splits
    )


def row_copies(krylov, first, held, sems):
    count, _, lines, _ = held.shape

    def copy(at):
        start = (first + at) * lines
        if not isinstance(at, int):
            start = pl.multiple_of(start, lines)
        return pltpu.make_async_copy(
            krylov.at[:, pl.ds(start, lines), :], held.at[at], sems.at[at]
        )

    for at in range(count):
        copy(at).start()
    return copy


def fold_gram(sums, basis, lines):
    size = basis * lines
    own = lax.broadcasted_iota(jnp.int32, (size, size), 0)
    other = lax.broadcasted_iota(jnp.int32, (size, size), 1)
    if lines & (lines - 1) == 0:
        same = (own & (lines - 1)) == (other & (lines - 1))
    else:
        same = lax.rem(own, lines) == lax.rem(other, lines)
    kept = jnp.where(same, sums, 0.0)
    rows = [
        jnp.sum(kept[one * lines : (one + 1) * lines], axis=0, keepdims=True)
        for one in range(basis)
    ]
    place = lax.broadcasted_iota(jnp.int32, (size, LANES), 0)
    lane = lax.broadcasted_iota(jnp.int32, (size, LANES), 1) * lines
    picks = jnp.where((place >= lane) & (place < lane + lines), 1.0, 0.0).astype(F32)
    return jnp.dot(
        jnp.concatenate(rows, axis=0), picks,
        precision=lax.Precision.HIGHEST, preferred_element_type=F32,
    )


def gram_kernel(first, start, krylov, earlier, out, held, sems):
    count, _, _, _ = held.shape
    copy = row_copies(krylov, first, held, sems)
    out[...] = jnp.zeros_like(out) if start else earlier[...]

    def body(at, carry):
        copy(at).wait()
        stack = stacked(held[at])
        out[...] += dot_nt(stack, stack)
        return carry

    lax.fori_loop(0, count, body, 0)


def product_kernel(krylov, normed, out, square, held, sems):
    count, basis, lines, _ = held.shape
    copy = row_copies(krylov, 0, held, sems)
    square[...] = dot_nt(normed[...], normed[...])

    def body(at, carry):
        copy(at).wait()
        made = dot_nt(stacked(held[at]), normed[...])
        here = pl.ds(pl.multiple_of(at * lines, lines), lines)
        for one in range(basis):
            out[one, here, :] = made[one * lines : (one + 1) * lines]
        return carry

    lax.fori_loop(0, count, body, 0)


def both_kernel(first, fold, krylov, normed, earlier, out, gram_out, held, sums, sems):
    count, basis, lines, _ = held.shape
    copy = row_copies(krylov, first, held, sems)
    sums[...] = earlier[...]

    def body(at, carry):
        copy(at).wait()
        stack = stacked(held[at])
        sums[...] += dot_nt(stack, stack)
        made = dot_nt(stack, normed[...])
        here = pl.ds(pl.multiple_of(at * lines, lines), lines)
        for one in range(basis):
            out[one, here, :] = made[one * lines : (one + 1) * lines]
        return carry

    lax.fori_loop(0, count, body, 0)
    gram_out[...] = fold_gram(sums[...], basis, lines) if fold else sums[...]


def loss_columns(flip, load, places, splits):
    made = []
    for column in range(places // splits):
        pieces = [
            load((column * splits + part) ^ (flip & (places - 1))) for part in range(splits)
        ]
        if splits > 1:
            pieces = [jnp.concatenate([one.astype(F32) for one in pieces], 0).astype(BF16)]
        made.append(pieces[0])
    return jnp.concatenate(made, axis=1)


def back_copies(info, devices, other, down, krylov, held_down, held, sems):
    count, _, lines, width = held.shape
    start = half_start(info[0], devices, 2 * width, other)
    columns = pl.ds(start, width)
    copies = [
        pltpu.make_async_copy(
            krylov.at[:, at * lines : (at + 1) * lines, columns], held.at[at], sems.at[at]
        )
        for at in range(count)
    ]
    return copies, pltpu.make_async_copy(down.at[:, columns], held_down, sems.at[count])


def back_half_kernel(
    devices, splits,
    info, chunks, down, krylov, sums, back_sum, square,
    loss, held_down, held, sems,
):
    count, basis, lines, _ = held.shape
    copies, first = back_copies(info, devices, 0, down, krylov, held_down, held, sems)
    for copy in [first] + copies:
        copy.start()
    loss[...] = loss_columns(info[0], lambda at: chunks[at], chunks.shape[0], splits)
    square[...] = dot_nt(loss[...], loss[...])
    first.wait()
    back_sum[...] = dot_nt(held_down[...], loss[...])
    for at in range(count):
        copies[at].wait()
        made = dot_nt(stacked(held[at]), loss[...])
        for one in range(basis):
            sums[one, at * lines : (at + 1) * lines, :] = made[one * lines : (one + 1) * lines]


def back_kernel(
    devices, inv_d, inv_ff, splits, spans,
    info, chunks, down, krylov, hidden, weight, act, square, loss_square_half, back_half, grams,
    sums_half, prod_gate, *rest,
):
    prods_up = rest[: len(spans)]
    s_out, r_out, stats, held, loss, held_down, sems = rest[len(spans) :]
    count, basis, lines, _ = held.shape
    copies, first = back_copies(info, devices, 1, down, krylov, held_down, held, sems)
    for copy in [first] + copies:
        copy.start()
    loss[...] = loss_columns(info[0], lambda at: chunks[at], chunks.shape[0], splits)
    other = dot_nt(loss[...], loss[...]) + loss_square_half[...]
    first.wait()
    back = dot_nt(held_down[...], loss[...]) + back_half[...]
    s_term = (back * weight[...]).astype(BF16)
    r_term = (back * act[...]).astype(BF16)
    s_out[...] = s_term
    r_out[...] = r_term
    wide = hidden[...]
    squares = inv_d * inv_d * ((dot_tn(s_term, s_term) + dot_tn(r_term, r_term)) * square[...])
    squares = total(squares + inv_ff * inv_ff * (dot_tn(wide, wide) * other))
    stats[basis : 2 * basis, :] = jnp.broadcast_to(squares, (basis, LANES))
    stats[2 * basis : 3 * basis, :] = grams[...]
    wide_s = s_term.astype(F32) * inv_d
    wide_r = r_term.astype(F32) * inv_d
    wide_h = wide.astype(F32) * inv_ff
    values = []
    for one in range(basis):
        value = wide_s * prod_gate[one] + wide_h * sums_half[one]
        value = jnp.sum(value, axis=0, keepdims=True)
        for (start, number), prod in zip(spans, prods_up):
            part = wide_r[start : start + number] * prod[one]
            value = value + jnp.sum(part, axis=0, keepdims=True)
        values.append(value)
    for at in range(count):
        copies[at].wait()
        made = dot_nt(stacked(held[at]), loss[...])
        part = wide_h[at * lines : (at + 1) * lines]
        for one in range(basis):
            value = part * made[one * lines : (one + 1) * lines]
            values[one] = values[one] + jnp.sum(value, axis=0, keepdims=True)
    lined = jnp.sum(jnp.concatenate(values, axis=0), axis=1, keepdims=True)
    stats[0:basis, :] = jnp.broadcast_to(lined, (basis, LANES))


def split_three(value):
    first = value.astype(BF16)
    rest = value - first.astype(F32)
    second = rest.astype(BF16)
    return first, second, (rest - second.astype(F32)).astype(BF16)


def new_kernel(
    devices, count, inv_d, inv_ff, splits, long, number_up,
    info, stats, s_term, r_term, hidden, normed, lower, upper, krylov_gate, krylov_down,
    down_high, *rest,
):
    ups = rest[:number_up]
    new_gate, new_up, new_down, coefficients = rest[number_up : number_up + 4]
    loss, mixer, held, held_low, outs, sems, out_sems = rest[number_up + 4 :]
    depth, basis, lines, width = held.shape
    per = long // lines
    blocks = s_term.shape[0] // lines
    halved = width // 2
    size = basis * lines
    targets = (new_gate, new_up, new_down)
    low_start = half_start(info[0], devices, width, 0)
    high_start = half_start(info[0], devices, width, 1)

    def copy_in(block, part):
        here = pl.ds(pl.multiple_of(block * lines, lines), lines)
        slot = lax.rem(block, depth)
        if part == 0:
            source, target = krylov_gate.at[:, here, :], held.at[slot]
        else:
            source = krylov_down.at[:, here, pl.ds(low_start, halved)]
            target = held_low.at[slot]
        return pltpu.make_async_copy(source, target, sems.at[part // 2, slot])

    def copy_out(block, part):
        start = pl.multiple_of(block * lines, lines)
        slot = lax.rem(block, 2)
        return pltpu.make_async_copy(
            outs.at[slot, part], targets[part].at[pl.ds(start, lines), :], out_sems.at[slot, part]
        )

    for block in range(min(depth, blocks)):
        for part in (0, 2):
            copy_in(block, part).start()

    for at, half in enumerate((lower, upper)):
        loss[:, at * halved : (at + 1) * halved] = loss_columns(
            info[0], lambda place, half=half: half[place], half.shape[0], splits
        )
    proj = [stats[one, 0] / count for one in range(basis)]
    squares = stats[basis, 0]
    for one in range(basis):
        line = stats[2 * basis + one, 0] * proj[0]
        for two in range(1, basis):
            line = line + stats[2 * basis + one, two] * proj[two]
        squares = squares + proj[one] * (line - 2.0 * stats[one, 0])
    mean = jnp.maximum(jnp.full((8, LANES), squares / count, F32), 0.0)
    norm = jnp.sqrt(mean + 1e-06)
    inverse = jnp.max(1.0 / norm)
    for one in range(basis):
        coefficients[one] = proj[one]
    coefficients[basis] = jnp.max(norm)
    lane = lax.broadcasted_iota(jnp.int32, (lines, size), 1)
    row = lax.broadcasted_iota(jnp.int32, (lines, size), 0)
    values = jnp.zeros((lines, size), F32)
    for one in range(basis):
        values = jnp.where(lane == one * lines + row, proj[one] * inverse, values)
    terms = [term.astype(F32) for term in split_three(values)]
    mixer[...] = jnp.concatenate(terms, axis=0).astype(BF16)
    chunk = min(1024, halved)

    def put(part, step, left, right, scale, first, last, target, read):
        here = pl.ds(pl.multiple_of(step * long, long), long)
        for start in range(first, last, chunk):
            gradient = dot_nn(left[here, :], right[:, start : start + chunk]) * (scale * inverse)
            for sub in range(per):
                stack = stacked(read(sub, slice(start - first, start - first + chunk)))
                mixed = dot_nn(mixer[...], stack)
                mixed = mixed[:lines] + (mixed[lines : 2 * lines] + mixed[2 * lines :])
                value = gradient[sub * lines : (sub + 1) * lines] - mixed
                columns = pl.ds(pl.multiple_of(target + (start - first), chunk), chunk)
                slot = lax.rem(step * per + sub, 2)
                outs[slot, part, :, columns] = value.astype(BF16)

    def body(step, carry):
        for part in range(3):
            for sub in range(per):
                block = step * per + sub

                @pl.when(block >= 2)
                def _(part=part, block=block):
                    copy_out(block, part).wait()

                if part != 1:
                    copy_in(block, part).wait()
            if part == 0:
                put(
                    0, step, s_term, normed, inv_d, 0, width, 0,
                    lambda sub, columns: held[lax.rem(step * per + sub, depth), :, :, columns],
                )
            elif part == 1:
                ahead = 0
                for up in ups:
                    steps = up.shape[0] // per

                    @pl.when((step >= ahead) & (step < ahead + steps))
                    def _(up=up, ahead=ahead):
                        put(
                            1, step, r_term, normed, inv_d, 0, width, 0,
                            lambda sub, columns: up[(step - ahead) * per + sub, :, :, columns],
                        )

                    ahead += steps
            else:
                put(
                    2, step, hidden, loss, inv_ff, 0, halved, low_start,
                    lambda sub, columns: held_low[
                        lax.rem(step * per + sub, depth), :, :, columns
                    ],
                )
                put(
                    2, step, hidden, loss, inv_ff, halved, width, high_start,
                    lambda sub, columns: down_high[
                        step, :, sub * lines : (sub + 1) * lines, columns
                    ],
                )
            for sub in range(per):
                block = step * per + sub
                copy_out(block, part).start()
                if part != 1:
                    @pl.when(block + depth < blocks)
                    def _(part=part, block=block):
                        copy_in(block + depth, part).start()

        return carry

    lax.fori_loop(0, blocks // per, body, 0)
    for block in range(max(0, blocks - 2), blocks):
        for part in range(3):
            copy_out(block, part).wait()


def per_device(
    inputs, norm_gain, lengths, gate_rows, up_rows, down_rows, krylov_gate, krylov_up, krylov_down
):
    basis, rows, width = krylov_gate.shape
    devices = lax.axis_size("fsdp")
    bits = devices.bit_length() - 1
    groups = bit_groups(bits)
    hidden_all = rows * devices
    count = 3.0 * width * hidden_all
    inv_d = 1.0 / math.sqrt(width)
    inv_ff = 1.0 / math.sqrt(hidden_all)
    me = lax.axis_index("fsdp").astype(jnp.int32)
    mirror = reverse_bits(me, bits)
    info = jnp.stack([mirror, lengths[0]])

    splits = devices // (width // LANES)
    chunk_rows = LIVE // splits
    lines = 32 if rows % 32 == 0 else rows
    pieces = rows // lines
    long = block_rows(rows)
    halved = width // 2
    product_flops = 2 * rows * width * LIVE

    size = basis * lines

    def gram(krylov, first, number, earlier, before):
        start = earlier is None
        return pl.pallas_call(
            functools.partial(gram_kernel, first, start),
            in_specs=[FAR, FAST],
            out_specs=FAST,
            out_shape=jax.ShapeDtypeStruct((size, size), F32),
            scratch_shapes=[
                pltpu.VMEM((number, basis, lines, width), BF16),
                pltpu.SemaphoreType.DMA((number,)),
            ],
            compiler_params=params(26),
            cost_estimate=cost(2 * size * size * width * number, 2 * size * width * number),
            name="gram",
        )(far(after(krylov, before)), jnp.zeros((8, LANES), F32) if start else earlier)

    def both(krylov, first, number, fold, earlier, normed, before):
        return pl.pallas_call(
            functools.partial(both_kernel, first, fold),
            in_specs=[FAR, FAST, FAST],
            out_specs=[FAST] * 3,
            out_shape=[
                jax.ShapeDtypeStruct((basis, number * lines, LIVE), F32),
                jax.ShapeDtypeStruct((basis, LANES) if fold else (size, size), F32),
                jax.ShapeDtypeStruct((number, basis, lines, width), BF16),
            ],
            scratch_shapes=[
                pltpu.VMEM((size, size), F32),
                pltpu.SemaphoreType.DMA((number,)),
            ],
            compiler_params=params(8),
            cost_estimate=cost(
                2 * size * (size + LIVE) * width * number, 2 * size * width * number
            ),
            name="both",
        )(far(after(krylov, before)), normed, earlier)

    cut = (pieces + 1) // 2
    gram_jobs = [
        job
        for job in (
            (krylov_down, 0, cut), (krylov_gate, 0, pieces), (krylov_down, cut, pieces - cut)
        )
        if job[2]
    ]
    gram_sums = [None]

    def next_gram(group, before):
        if not gram_jobs:
            return None
        return gram(*gram_jobs.pop(0), gram_sums[-1], before), gram_sums.append

    own_tokens = inputs.shape[0]
    tokens = own_tokens * devices
    if own_tokens % GROUP == 0:
        sub = own_tokens // GROUP
        lower, upper = gather_blocks(inputs.reshape(sub, GROUP, width), groups, next_gram)

        def spots(flip, group):
            return (reverse_bits(group // sub, bits) ^ flip) * sub + group % sub

    else:
        gathered = lax.all_gather(inputs, "fsdp", axis=0, tiled=True)
        gathered = gathered.reshape(tokens // GROUP, GROUP, width)
        lower, upper = jnp.split(gathered, 2)

        def spots(flip, group):
            return group

    while gram_jobs:
        made, done = next_gram(None, inputs)
        done(made)

    normed, hidden, tangent_t, hidden_t, weight, act, send = pl.pallas_call(
        functools.partial(forward_kernel, devices, inv_d, inv_ff, spots, splits),
        in_specs=[SMALL] + [FAST] * 3 + [FAR] * 6,
        out_specs=[FAST] * 7,
        out_shape=[
            jax.ShapeDtypeStruct((LIVE, width), BF16),
            jax.ShapeDtypeStruct((rows, LIVE), BF16),
            jax.ShapeDtypeStruct((LIVE, rows), BF16),
            jax.ShapeDtypeStruct((LIVE, rows), BF16),
            jax.ShapeDtypeStruct((rows, LIVE), F32),
            jax.ShapeDtypeStruct((rows, LIVE), F32),
            jax.ShapeDtypeStruct((devices // 2, chunk_rows, LANES), BF16),
        ],
        scratch_shapes=[
            pltpu.VMEM((rows // long, 4, long, width), BF16),
            pltpu.VMEM((2, rows, halved), BF16),
            pltpu.VMEM((rows, LIVE), BF16),
            pltpu.SemaphoreType.DMA((rows // long, 4)),
            pltpu.SemaphoreType.DMA((2,)),
        ],
        compiler_params=params(24),
        cost_estimate=cost(5 * product_flops, 10 * rows * width + 6 * LIVE * width, rows * LIVE),
        name="forward",
    )(
        info, lower, upper, norm_gain.reshape(1, width), far(gate_rows), far(up_rows),
        far(krylov_gate), far(krylov_up), far(down_rows), far(krylov_down),
    )

    def product(krylov, before):
        return pl.pallas_call(
            product_kernel,
            in_specs=[FAR, FAST],
            out_specs=[FAST, FAST],
            out_shape=[
                jax.ShapeDtypeStruct((basis, rows, LIVE), F32),
                jax.ShapeDtypeStruct((LIVE, LIVE), F32),
            ],
            scratch_shapes=[
                pltpu.VMEM((pieces, basis, lines, width), BF16),
                pltpu.SemaphoreType.DMA((pieces,)),
            ],
            compiler_params=params(28),
            cost_estimate=cost(
                basis * product_flops, 2 * basis * rows * width + 4 * basis * rows * LIVE
            ),
            name="product",
        )(far(after(krylov, before)), normed)

    got = exchange(send, 1)
    keep = pl.pallas_call(
        functools.partial(keep_kernel, devices, inv_ff, splits),
        in_specs=[SMALL, FAST, FAST, FAR, FAR],
        out_specs=FAST,
        out_shape=jax.ShapeDtypeStruct((devices // 2, chunk_rows, LANES), F32),
        scratch_shapes=[
            pltpu.VMEM((2, rows, halved), BF16),
            pltpu.SemaphoreType.DMA((2,)),
        ],
        compiler_params=params(8),
        cost_estimate=cost(product_flops, 2 * rows * width + 2 * LIVE * width),
        name="keep",
    )(info, tangent_t, hidden_t, far(down_rows), far(krylov_down))

    per = long // lines
    part = (pieces // per + 2) // 3 * per
    shares = [min(part, pieces - first) for first in range(0, pieces, part)]
    up_jobs = [(sum(shares[:at]), number) for at, number in enumerate(shares)]
    up_spans = [(first * lines, number * lines) for first, number in up_jobs]
    prods_up, kept_up = [], []

    def next_both(before):
        if not up_jobs:
            return None
        first, number = up_jobs.pop(0)
        made = both(
            krylov_up, first, number, not up_jobs, gram_sums[-1], normed, before
        )

        def done(made):
            prods_up.append(made[0])
            gram_sums.append(made[1])
            kept_up.append(made[2])

        return made, done

    got = [got]
    for at, group in enumerate(groups[1:]):
        parts = flips(group)
        part = keep.shape[0] // (len(parts) + 1)
        sends = [
            add_up([one[turn * part : (turn + 1) * part].astype(F32) for one in [keep] + got])
            for turn in range(1, len(parts) + 1)
        ]
        keep = add_up([one[:part].astype(F32) for one in [keep] + got])
        sends = [one.astype(BF16) for one in sends]
        got = [exchange(one, flip) for one, flip in zip(sends, parts)]
        if at == 0:
            got, (prod_gate, square) = lax.optimization_barrier(
                (got, product(krylov_gate, sends[0]))
            )
        elif up_jobs:
            made, done = next_both(sends[0])
            got, made = lax.optimization_barrier((got, made))
            done(made)
    loss_own = add_up([one.astype(F32) for one in [keep] + got]).astype(BF16)

    def half_call(lower):
        return pl.pallas_call(
            functools.partial(back_half_kernel, devices, splits),
            in_specs=[SMALL, FAST, FAR, FAR],
            out_specs=[FAST] * 3,
            out_shape=[
                jax.ShapeDtypeStruct((basis, rows, LIVE), F32),
                jax.ShapeDtypeStruct((rows, LIVE), F32),
                jax.ShapeDtypeStruct((LIVE, LIVE), F32),
            ],
            scratch_shapes=[
                pltpu.VMEM((LIVE, halved), BF16),
                pltpu.VMEM((rows, halved), BF16),
                pltpu.VMEM((rows // long, basis, long, halved), BF16),
                pltpu.SemaphoreType.DMA((rows // long + 1,)),
            ],
            compiler_params=params(18),
            cost_estimate=cost(
                (basis + 1) * product_flops // 2,
                (basis + 1) * rows * width + 4 * basis * rows * LIVE,
            ),
            name="back_half",
        )(info, lower, far(down_rows), far(krylov_down))

    halves = []

    def beside(group, block):
        if group[0] == 0:
            return half_call(block), halves.extend
        return next_both(block)

    lower, upper = gather_blocks(loss_own, groups, beside)
    sums_half, back_half, loss_square_half = halves

    s_term, r_term, stats, down_high = pl.pallas_call(
        functools.partial(back_kernel, devices, inv_d, inv_ff, splits, up_spans),
        in_specs=[SMALL, FAST, FAR, FAR] + [FAST] * (9 + len(prods_up)),
        out_specs=[FAST] * 4,
        out_shape=[
            jax.ShapeDtypeStruct((rows, LIVE), BF16),
            jax.ShapeDtypeStruct((rows, LIVE), BF16),
            jax.ShapeDtypeStruct((3 * basis, LANES), F32),
            jax.ShapeDtypeStruct((rows // long, basis, long, halved), BF16),
        ],
        scratch_shapes=[
            pltpu.VMEM((LIVE, halved), BF16),
            pltpu.VMEM((rows, halved), BF16),
            pltpu.SemaphoreType.DMA((rows // long + 1,)),
        ],
        compiler_params=params(8),
        cost_estimate=cost(
            (basis + 1) * product_flops // 2,
            (basis + 1) * rows * width + 12 * basis * rows * LIVE,
        ),
        name="back",
    )(
        info, upper, far(down_rows), far(krylov_down), hidden, weight, act, square,
        loss_square_half, back_half, gram_sums[-1], sums_half, prod_gate, *prods_up,
    )

    for group in groups:
        stats = add_up([stats] + [exchange(stats, flip) for flip in flips(group)])

    depth = min(3, pieces)
    out_shape = jax.ShapeDtypeStruct((rows, width), BF16)
    new_gate, new_up, new_down, coefficients = pl.pallas_call(
        functools.partial(new_kernel, devices, count, inv_d, inv_ff, splits, long, len(kept_up)),
        in_specs=[SMALL, SMALL] + [FAST] * 6 + [FAR] * 2 + [FAST] * (1 + len(kept_up)),
        out_specs=[FAR] * 3 + [SMALL],
        out_shape=[out_shape, out_shape, out_shape, jax.ShapeDtypeStruct((basis + 1,), F32)],
        scratch_shapes=[
            pltpu.VMEM((LIVE, width), BF16),
            pltpu.VMEM((3 * lines, size), BF16),
            pltpu.VMEM((depth, basis, lines, width), BF16),
            pltpu.VMEM((depth, basis, lines, halved), BF16),
            pltpu.VMEM((2, 3, lines, width), BF16),
            pltpu.SemaphoreType.DMA((2, depth)),
            pltpu.SemaphoreType.DMA((2, 3)),
        ],
        compiler_params=params(20),
        cost_estimate=cost(3 * product_flops, 6 * (basis + 1) * rows * width),
        name="new",
    )(
        info, stats, s_term, r_term, hidden, normed, lower, upper, far(krylov_gate),
        far(krylov_down), down_high, *kept_up,
    )
    return (new_gate, new_up, new_down, coefficients)


def solution(mesh):
    placed = (
        P("fsdp", None),
        P(),
        P(),
        P("fsdp", None),
        P("fsdp", None),
        P("fsdp", None),
        P(None, "fsdp", None),
        P(None, "fsdp", None),
        P(None, "fsdp", None),
    )
    return jax.shard_map(
        per_device,
        mesh=mesh,
        in_specs=placed,
        out_specs=(P("fsdp", None), P("fsdp", None), P("fsdp", None), P()),
        check_vma=False,
    )
```

```python
import functools
import math

import jax
import jax.numpy as jnp
from jax import lax
from jax.experimental import pallas as pl
from jax.experimental.pallas import tpu as pltpu
from jax.sharding import PartitionSpec as P

LEN = 128
LIVE = 192
GROUP = 8
LANES = 128
F32 = jnp.float32
BF16 = jnp.bfloat16


def gelu_pair(gate_pre):
    coef = math.sqrt(2.0 / math.pi)
    cube = gate_pre * gate_pre * gate_pre
    tanh_val = jnp.tanh(coef * (gate_pre + 0.044715 * cube))
    act = 0.5 * gate_pre * (1.0 + tanh_val)
    slope = 0.5 * (1.0 + tanh_val) + 0.5 * gate_pre * (1.0 - tanh_val * tanh_val) * coef * (
        1.0 + 3.0 * 0.044715 * gate_pre * gate_pre
    )
    return (act, slope)


def dot_nn(left, right):
    return jnp.dot(left, right, preferred_element_type=F32)


def dot_nt(left, right):
    return lax.dot_general(left, right, (((1,), (1,)), ((), ())), preferred_element_type=F32)


def dot_tn(left, right):
    return lax.dot_general(left, right, (((0,), (0,)), ((), ())), preferred_element_type=F32)


def total(values):
    return jnp.sum(jnp.sum(values, axis=0, keepdims=True), axis=1, keepdims=True)


def reverse_bits(value, bits):
    out = value * 0
    for bit in range(bits):
        out = out | (((value >> bit) & 1) << (bits - 1 - bit))
    return out


def exchange(block, flip):
    count = lax.axis_size("fsdp")
    return lax.ppermute(block, "fsdp", [(one, one ^ flip) for one in range(count)])


def bit_groups(bits):
    return [(0, 1)] + [(low, min(2, bits - low)) for low in range(1, bits, 2)]


def flips(group):
    low, size = group
    return [reverse_bits(part, size) << low for part in range(1, 1 << size)]


def gather_blocks(block, groups, beside):
    for group in reversed(groups):
        others = [exchange(block, flip) for flip in flips(group)]
        job = beside(group, block)
        if job is not None:
            work, done = job
            others, made = lax.optimization_barrier((others, work))
            done(made)
        if group[0]:
            block = jnp.concatenate([block] + others, axis=0)
    return block, others[0]


def add_up(values):
    while len(values) > 1:
        values = [one + two for one, two in zip(values[0::2], values[1::2])]
    return values[0]


def far(value):
    return pltpu.with_memory_space_constraint(value, pltpu.HBM)


def after(value, earlier):
    return lax.optimization_barrier((value, earlier))[0]


def stacked(krylov):
    basis, rows, width = krylov.shape
    if rows % 16:
        return krylov.astype(F32).reshape(basis * rows, width).astype(BF16)
    return krylov.reshape(basis * rows, width)


def params(mib):
    return pltpu.CompilerParams(vmem_limit_bytes=mib << 20)


def cost(flops, read, transcendentals=0):
    return pl.CostEstimate(flops=flops, bytes_accessed=read, transcendentals=transcendentals)


FAST = pl.BlockSpec(memory_space=pltpu.VMEM)
SMALL = pl.BlockSpec(memory_space=pltpu.SMEM)
FAR = pl.BlockSpec(memory_space=pltpu.HBM)


def block_rows(rows):
    return 64 if rows % 64 == 0 else rows


def half_start(flip, devices, width, other):
    top = lax.div(flip, devices // 2) ^ other
    return pl.multiple_of(top * (width // 2), width // 2)


def live_tokens(info, lower, upper, gain, normed, spots):
    spare = info[1] - (LIVE - LEN)
    shift = lax.rem(spare, GROUP)
    half = (LIVE - LEN) // GROUP
    per = LEN // GROUP
    scale = gain[...].astype(F32)
    row_ids = lax.broadcasted_iota(jnp.int32, (GROUP, 1), 0)

    half_groups = lower.shape[0]

    def load(group):
        spot = spots(info[0], group)
        place = lax.rem(spot, half_groups)
        return jnp.where(spot < half_groups, lower[place], upper[place]).astype(F32)

    def tokens(slot):
        if slot < half:
            return load(slot)
        if slot < 2 * half:
            at = slot - half
            first = load(half + at)
            second = pltpu.roll(load(per + 2 * half - 1 - at), shift, 0)
            return jnp.where(GROUP * at + row_ids < spare, first, second)
        return load(per + slot - 2 * half)

    def norm(wide):
        mean = jnp.mean(wide * wide, axis=1, keepdims=True)
        return wide * lax.rsqrt(mean + 1e-06) * scale

    for pair in range(LIVE // (2 * GROUP)):
        both = [norm(tokens(2 * pair + side)) for side in range(2)]
        normed[2 * GROUP * pair : 2 * GROUP * (pair + 1), :] = jnp.concatenate(both, 0).astype(BF16)


def jvp_half(info, tangent_t, hidden_t, down, probe, out, inv_ff, splits):
    rows = LIVE // splits
    places = out.shape[0]
    width = down.shape[1]
    step = min(512, width)
    each = step // LANES
    for at in range(width // step):
        here = slice(at * step, (at + 1) * step)
        values = dot_nn(tangent_t, down[:, here]) + dot_nn(hidden_t, probe[:, here]) * inv_ff
        for column in range(each):
            for part in range(splits):
                piece = values[
                    part * rows : (part + 1) * rows, column * LANES : (column + 1) * LANES
                ]
                chunk = (at * each + column) * splits + part
                out[chunk ^ (info[0] & (places - 1))] = piece.astype(out.dtype)


def down_copies(info, devices, other, sources, held, sems):
    width = held.shape[2]
    start = half_start(info[0], devices, 2 * width, other)
    return [
        pltpu.make_async_copy(source.at[:, pl.ds(start, width)], held.at[at], sems.at[at])
        for at, source in enumerate(sources)
    ]


def forward_kernel(
    devices, inv_d, inv_ff, spots, splits,
    info, lower, upper, gain, gate, up, krylov_gate, krylov_up, down, krylov_down,
    normed, hidden, tangent_t, hidden_t, weight, act_out, send,
    held, held_down, tangent, sems, down_sems,
):
    basis = krylov_gate.shape[0]
    count, _, lines, width = held.shape
    sources = (gate, up, krylov_gate.at[basis - 1], krylov_up.at[basis - 1])
    copies = [
        [
            pltpu.make_async_copy(
                source.at[at * lines : (at + 1) * lines], held.at[at, one], sems.at[at, one]
            )
            for one, source in enumerate(sources)
        ]
        for at in range(count)
    ]
    last = down_copies(
        info, devices, 1, (down, krylov_down.at[basis - 1]), held_down, down_sems
    )
    for copy in sum(copies, []) + last:
        copy.start()
    live_tokens(info, lower, upper, gain, normed, spots)
    for at in range(count):
        for copy in copies[at]:
            copy.wait()
        made = dot_nt(stacked(held[at]), normed[...])
        gate_pre, up_pre, tan_gate, tan_up = (
            made[one * lines : (one + 1) * lines] for one in range(4)
        )
        act, slope = gelu_pair(gate_pre)
        here = slice(at * lines, (at + 1) * lines)
        hidden[here, :] = (act * up_pre).astype(BF16)
        tangent[here, :] = (
            slope * (tan_gate * inv_d) * up_pre + act * (tan_up * inv_d)
        ).astype(BF16)
        weight[here, :] = up_pre * slope
        act_out[here, :] = act
    tangent_t[...] = tangent[...].T
    hidden_t[...] = hidden[...].T
    for copy in last:
        copy.wait()
    jvp_half(
        info, tangent_t[...], hidden_t[...], held_down.at[0], held_down.at[1], send, inv_ff, splits
    )


def keep_kernel(
    devices, inv_ff, splits,
    info, tangent_t, hidden_t, down, krylov_down, keep, held_down, sems,
):
    basis = krylov_down.shape[0]
    copies = down_copies(info, devices, 0, (down, krylov_down.at[basis - 1]), held_down, sems)
    for copy in copies:
        copy.start()
    for copy in copies:
        copy.wait()
    jvp_half(
        info, tangent_t[...], hidden_t[...], held_down.at[0], held_down.at[1], keep, inv_ff, splits
    )


def row_copies(krylov, first, held, sems, sem=0):
    count, _, lines, _ = held.shape

    def copy(at):
        start = (first + at) * lines
        if not isinstance(at, int):
            start = pl.multiple_of(start, lines)
        return pltpu.make_async_copy(
            krylov.at[:, pl.ds(start, lines), :], held.at[at], sems.at[sem + at]
        )

    for at in range(count):
        copy(at).start()
    return copy


def fold_gram(sums, basis, lines):
    size = basis * lines
    own = lax.broadcasted_iota(jnp.int32, (size, size), 0)
    other = lax.broadcasted_iota(jnp.int32, (size, size), 1)
    if lines & (lines - 1) == 0:
        same = (own & (lines - 1)) == (other & (lines - 1))
    else:
        same = lax.rem(own, lines) == lax.rem(other, lines)
    kept = jnp.where(same, sums, 0.0)
    rows = [
        jnp.sum(kept[one * lines : (one + 1) * lines], axis=0, keepdims=True)
        for one in range(basis)
    ]
    place = lax.broadcasted_iota(jnp.int32, (size, LANES), 0)
    lane = lax.broadcasted_iota(jnp.int32, (size, LANES), 1) * lines
    picks = jnp.where((place >= lane) & (place < lane + lines), 1.0, 0.0).astype(F32)
    return jnp.dot(
        jnp.concatenate(rows, axis=0), picks,
        precision=lax.Precision.HIGHEST, preferred_element_type=F32,
    )


def gram_kernel(first, start, krylov, earlier, out, held, sems):
    count, _, _, _ = held.shape
    copy = row_copies(krylov, first, held, sems)
    out[...] = jnp.zeros_like(out) if start else earlier[...]

    def body(at, carry):
        copy(at).wait()
        stack = stacked(held[at])
        out[...] += dot_nt(stack, stack)
        return carry

    lax.fori_loop(0, count, body, 0)


def product_kernel(krylov, normed, out, square, held, sems):
    count, basis, lines, _ = held.shape
    copy = row_copies(krylov, 0, held, sems)
    square[...] = dot_nt(normed[...], normed[...])

    def body(at, carry):
        copy(at).wait()
        made = dot_nt(stacked(held[at]), normed[...])
        here = pl.ds(pl.multiple_of(at * lines, lines), lines)
        for one in range(basis):
            out[one, here, :] = made[one * lines : (one + 1) * lines]
        return carry

    lax.fori_loop(0, count, body, 0)


def both_kernel(first, krylov, normed, earlier, out, sums, *rest):
    pieces, sems = rest[:-1], rest[-1]
    ahead, copies = 0, []
    for held in pieces:
        copies.append(row_copies(krylov, first + ahead, held, sems, ahead))
        ahead += held.shape[0]
    sums[...] = earlier[...]
    ahead = 0
    for held, copy in zip(pieces, copies):
        count, basis, lines, _ = held.shape

        def body(at, carry, held=held, copy=copy, ahead=ahead):
            copy(at).wait()
            stack = stacked(held[at])
            sums[...] += dot_nt(stack, stack)
            made = dot_nt(stack, normed[...])
            here = pl.ds(pl.multiple_of((ahead + at) * lines, lines), lines)
            for one in range(basis):
                out[one, here, :] = made[one * lines : (one + 1) * lines]
            return carry

        lax.fori_loop(0, count, body, 0)
        ahead += count


def put_loss(loss, first, flip, chunks, splits):
    places = chunks.shape[0]
    for column in range(places // splits):
        pieces = [
            chunks[(column * splits + part) ^ (flip & (places - 1))] for part in range(splits)
        ]
        if splits > 1:
            pieces = [jnp.concatenate([one.astype(F32) for one in pieces], 0).astype(BF16)]
        loss[:, first + column * LANES : first + (column + 1) * LANES] = pieces[0]


def back_copies(info, devices, other, down, krylov, held_down, held, sems):
    count, _, lines, width = held.shape
    start = half_start(info[0], devices, 2 * width, other)
    columns = pl.ds(start, width)
    copies = [
        pltpu.make_async_copy(
            krylov.at[:, at * lines : (at + 1) * lines, columns], held.at[at], sems.at[at]
        )
        for at in range(count)
    ]
    return copies, pltpu.make_async_copy(down.at[:, columns], held_down, sems.at[count])


def down_products(copies, held, loss, wide, values, grams):
    count, basis, lines, _ = held.shape
    for at in range(count):
        copies[at].wait()
        stack = stacked(held[at])
        grams[...] += dot_nt(stack, stack)
        made = dot_nt(stack, loss[...])
        part = wide[at * lines : (at + 1) * lines]
        for one in range(basis):
            value = part * made[one * lines : (one + 1) * lines]
            values[one] = values[one] + jnp.sum(value, axis=0, keepdims=True)
    return jnp.concatenate(values, axis=0)


def back_half_kernel(
    devices, inv_ff, splits,
    info, chunks, down, krylov, hidden, earlier, grams, back_sum, squares, values,
    loss, held_down, held, sems,
):
    basis = held.shape[1]
    copies, first = back_copies(info, devices, 0, down, krylov, held_down, held, sems)
    for copy in [first] + copies:
        copy.start()
    grams[...] = earlier[...]
    put_loss(loss, 0, info[0], chunks, splits)
    squares[0] = dot_nt(loss[...], loss[...])
    squares[1] = dot_tn(hidden[...], hidden[...]) * (inv_ff * inv_ff)
    first.wait()
    back_sum[...] = dot_nt(held_down[...], loss[...])
    wide = hidden[...].astype(F32) * inv_ff
    zeros = [jnp.zeros((1, LIVE), F32) for _ in range(basis)]
    values[...] = down_products(copies, held, loss, wide, zeros, grams)


def back_kernel(
    devices, inv_d, inv_ff, splits, spans,
    info, chunks, down, krylov, hidden, weight, act, square, squares_half, back_half, earlier,
    values_half, prod_gate, *rest,
):
    prods_up = rest[: len(spans)]
    s_out, r_out, stats, held, loss, held_down, grams, sems = rest[len(spans) :]
    basis, lines = held.shape[1:3]
    copies, first = back_copies(info, devices, 1, down, krylov, held_down, held, sems)
    for copy in [first] + copies:
        copy.start()
    grams[...] = earlier[...]
    put_loss(loss, 0, info[0], chunks, splits)
    first.wait()
    back = dot_nt(held_down[...], loss[...]) + back_half[...]
    s_term = (back * weight[...]).astype(BF16)
    r_term = (back * act[...]).astype(BF16)
    s_out[...] = s_term
    r_out[...] = r_term
    squares = inv_d * inv_d * ((dot_tn(s_term, s_term) + dot_tn(r_term, r_term)) * square[...])
    other = dot_nt(loss[...], loss[...]) + squares_half[0]
    squares = total(squares + squares_half[1] * other)
    wide_s = s_term.astype(F32) * inv_d
    wide_r = r_term.astype(F32) * inv_d
    values = []
    for one in range(basis):
        value = jnp.sum(wide_s * prod_gate[one], axis=0, keepdims=True)
        for (start, number), prod in zip(spans, prods_up):
            part = wide_r[start : start + number] * prod[one]
            value = value + jnp.sum(part, axis=0, keepdims=True)
        values.append(value + values_half[one : one + 1, :])
    wide = hidden[...].astype(F32) * inv_ff
    lined = down_products(copies, held, loss, wide, values, grams)
    lined = jnp.sum(lined, axis=1, keepdims=True)
    lane = lax.broadcasted_iota(jnp.int32, (basis, LANES), 1)
    made = fold_gram(grams[...], basis, lines)
    stats[...] = made + jnp.where(lane == basis, lined, 0.0) + jnp.where(
        lane == basis + 1, squares, 0.0
    )


def split_three(value):
    first = value.astype(BF16)
    rest = value - first.astype(F32)
    second = rest.astype(BF16)
    return first, second, (rest - second.astype(F32)).astype(BF16)


def new_kernel(
    devices, count, inv_d, inv_ff, splits, per, number_up,
    info, stats, s_term, r_term, hidden, normed, lower, upper, krylov_gate, krylov_down,
    down_high, *rest,
):
    ups = rest[:number_up]
    new_gate, new_up, new_down, coefficients = rest[number_up : number_up + 4]
    loss, mixer, wide, held, held_low, outs, sems, out_sems = rest[number_up + 4 :]
    depth, basis, lines, width = held.shape
    long = per * lines
    blocks = s_term.shape[0] // lines
    steps = blocks // per
    halved = width // 2
    shared = basis // 2
    size = per * shared * lines
    narrow = min(256, halved)
    group = min(1024, halved)
    targets = (new_gate, new_up, new_down)
    low_start = half_start(info[0], devices, width, 0)
    high_start = half_start(info[0], devices, width, 1)

    def copy_in(block, part):
        here = pl.ds(pl.multiple_of(block * lines, lines), lines)
        slot = lax.rem(block, depth)
        if part == 0:
            source, target = krylov_gate.at[:, here, :], held.at[slot]
        else:
            source = krylov_down.at[:, here, pl.ds(low_start, halved)]
            target = held_low.at[slot]
        return pltpu.make_async_copy(source, target, sems.at[part // 2, slot])

    def copy_out(turn, step, part):
        start = pl.multiple_of(step * long, long)
        slot = lax.rem(turn, 2)
        return pltpu.make_async_copy(
            outs.at[slot], targets[part].at[pl.ds(start, long), :], out_sems.at[slot]
        )

    for part in (2, 0):
        for block in range(min(depth, blocks)):
            copy_in(block, part).start()

    for at, half in enumerate((lower, upper)):
        put_loss(loss, at * halved, info[0], half, splits)
    sums = stats[0]
    for one in range(1, devices):
        sums = sums + stats[one]
    lane = lax.broadcasted_iota(jnp.int32, sums.shape, 1)
    row = lax.broadcasted_iota(jnp.int32, sums.shape, 0)

    def pick(where):
        return jnp.sum(jnp.where(where, sums, 0.0))

    proj = [pick((lane == basis) & (row == one)) / count for one in range(basis)]
    squares = pick((lane == basis + 1) & (row == 0))
    for one in range(basis):
        line = jnp.zeros((1, LANES), F32)
        for two in range(basis):
            line = line + proj[two] * sums[two : two + 1, :]
        dots = pick((lane == basis) & (row == one))
        mixed = jnp.sum(jnp.where(lane[0:1] == one, line, 0.0))
        squares = squares + proj[one] * (mixed - 2.0 * dots)
    mean = jnp.maximum(jnp.full((8, LANES), squares / count, F32), 0.0)
    norm = jnp.sqrt(mean + 1e-06)
    inverse = jnp.max(1.0 / norm)
    for one in range(basis):
        coefficients[one] = proj[one]
    coefficients[basis] = jnp.max(norm)
    scales = [one * inverse for one in proj]

    lane = lax.broadcasted_iota(jnp.int32, (long, size), 1)
    row = lax.broadcasted_iota(jnp.int32, (long, size), 0)
    values = jnp.zeros((long, size), F32)
    for sub in range(per):
        inside = (row >= sub * lines) & (row < (sub + 1) * lines)
        for one in range(shared):
            place = (sub * shared + one - sub) * lines + row
            values = jnp.where(inside & (lane == place), scales[one], values)
    terms = [term.astype(F32) for term in split_three(values)]
    mixer[...] = jnp.concatenate(terms, axis=0).astype(BF16)

    def put(turn, step, part, pieces):
        slot = lax.rem(turn, 2)
        here = pl.ds(pl.multiple_of(step * long, long), long)

        @pl.when(turn >= 2)
        def _():
            copy_out(turn, step, part).wait()

        for first, last, target, read in pieces:

            def body(at, carry, first=first, target=target, read=read):
                for sub in range(group // narrow):
                    start = pl.multiple_of(at * group + sub * narrow, narrow)
                    columns = pl.ds(start, narrow)
                    stack = jnp.concatenate(
                        [stacked(read(block, slice(0, shared), columns)) for block in range(per)],
                        axis=0,
                    )
                    mixed = dot_nn(mixer[...], stack)
                    value = wide[here, pl.ds(pl.multiple_of(first + start, narrow), narrow)]
                    value = value - (mixed[:long] + (mixed[long : 2 * long] + mixed[2 * long :]))
                    goal = pl.ds(pl.multiple_of(target + start, narrow), narrow)
                    for block in range(per):
                        inside = slice(block * lines, (block + 1) * lines)
                        rest = value[inside]
                        others = read(block, slice(shared, basis), columns)
                        for one in range(basis - shared):
                            rest = rest - scales[shared + one] * others[one].astype(F32)
                        outs[slot, inside, goal] = rest.astype(BF16)
                return carry

            lax.fori_loop(0, (last - first) // group, body, 0)
        copy_out(turn, step, part).start()

    def refill(step, part):
        for sub in range(per):
            block = step * per + sub + depth

            @pl.when(block < blocks)
            def _(block=block):
                copy_in(block, part).start()

    for turn, part in enumerate((1, 2, 0)):
        left, right, scale = (
            (s_term, normed, inv_d), (r_term, normed, inv_d), (hidden, loss, inv_ff)
        )[part]

        def gradient(at, carry, left=left, right=right, scale=scale):
            columns = pl.ds(pl.multiple_of(at * narrow, narrow), narrow)
            wide[:, columns] = dot_nn(left[...], right[:, columns]) * (scale * inverse)
            return carry

        lax.fori_loop(0, width // narrow, gradient, 0)
        if part == 1:
            ahead = 0
            for up in ups:

                def up_body(step, carry, up=up, ahead=ahead):
                    def read(block, vectors, columns):
                        return up[(step - ahead) * per + block, vectors, :, columns]

                    put(step, step, 1, [(0, width, 0, read)])
                    return carry

                lax.fori_loop(ahead, ahead + up.shape[0] // per, up_body, 0)
                ahead += up.shape[0] // per
            continue

        def body(step, carry, turn=turn, part=part):
            for sub in range(per):
                copy_in(step * per + sub, part).wait()

            def read(block, vectors, columns):
                source = held if part == 0 else held_low
                return source[lax.rem(step * per + block, depth), vectors, :, columns]

            def read_high(block, vectors, columns):
                return down_high[step * per + block, vectors, :, columns]

            if part == 0:
                pieces = [(0, width, 0, read)]
            else:
                pieces = [(0, halved, low_start, read), (halved, width, high_start, read_high)]
            put(turn * steps + step, step, part, pieces)
            refill(step, part)
            return carry

        lax.fori_loop(0, steps, body, 0)
    for turn in range(max(0, 3 * steps - 2), 3 * steps):
        copy_out(turn, turn % steps, 0).wait()


def per_device(
    inputs, norm_gain, lengths, gate_rows, up_rows, down_rows, krylov_gate, krylov_up, krylov_down
):
    basis, rows, width = krylov_gate.shape
    devices = lax.axis_size("fsdp")
    bits = devices.bit_length() - 1
    groups = bit_groups(bits)
    hidden_all = rows * devices
    count = 3.0 * width * hidden_all
    inv_d = 1.0 / math.sqrt(width)
    inv_ff = 1.0 / math.sqrt(hidden_all)
    me = lax.axis_index("fsdp").astype(jnp.int32)
    mirror = reverse_bits(me, bits)
    info = jnp.stack([mirror, lengths[0]])

    splits = devices // (width // LANES)
    chunk_rows = LIVE // splits
    lines = 32 if rows % 32 == 0 else rows
    pieces = rows // lines
    long = block_rows(rows)
    halved = width // 2
    product_flops = 2 * rows * width * LIVE

    size = basis * lines

    def gram(krylov, first, number, earlier, before):
        start = earlier is None
        return pl.pallas_call(
            functools.partial(gram_kernel, first, start),
            in_specs=[FAR, FAST],
            out_specs=FAST,
            out_shape=jax.ShapeDtypeStruct((size, size), F32),
            scratch_shapes=[
                pltpu.VMEM((number, basis, lines, width), BF16),
                pltpu.SemaphoreType.DMA((number,)),
            ],
            compiler_params=params(26),
            cost_estimate=cost(2 * size * size * width * number, 2 * size * width * number),
            name="gram",
        )(far(after(krylov, before)), jnp.zeros((8, LANES), F32) if start else earlier)

    def both(krylov, first, number, earlier, normed, before):
        split = [min(4, number - at) for at in range(0, number, 4)]
        return pl.pallas_call(
            functools.partial(both_kernel, first),
            in_specs=[FAR, FAST, FAST],
            out_specs=[FAST] * (2 + len(split)),
            out_shape=[
                jax.ShapeDtypeStruct((basis, number * lines, LIVE), F32),
                jax.ShapeDtypeStruct((size, size), F32),
            ]
            + [jax.ShapeDtypeStruct((one, basis, lines, width), BF16) for one in split],
            scratch_shapes=[pltpu.SemaphoreType.DMA((number,))],
            compiler_params=params(8),
            cost_estimate=cost(
                2 * size * (size + LIVE) * width * number, 2 * size * width * number
            ),
            name="both",
        )(far(after(krylov, before)), normed, earlier)

    cut = (pieces + 1) // 2
    gram_jobs = [
        job
        for job in (
            (krylov_gate, 0, cut), (krylov_gate, cut, pieces - cut)
        )
        if job[2]
    ]
    gram_sums = [None]

    def next_gram(group, before):
        if not gram_jobs or group == groups[-1]:
            return None
        return gram(*gram_jobs.pop(0), gram_sums[-1], before), gram_sums.append

    own_tokens = inputs.shape[0]
    tokens = own_tokens * devices
    if own_tokens % GROUP == 0:
        sub = own_tokens // GROUP
        lower, upper = gather_blocks(inputs.reshape(sub, GROUP, width), groups, next_gram)

        def spots(flip, group):
            return (reverse_bits(group // sub, bits) ^ flip) * sub + group % sub

    else:
        gathered = lax.all_gather(inputs, "fsdp", axis=0, tiled=True)
        gathered = gathered.reshape(tokens // GROUP, GROUP, width)
        lower, upper = jnp.split(gathered, 2)

        def spots(flip, group):
            return group

    while gram_jobs:
        made, done = next_gram(None, inputs)
        done(made)

    normed, hidden, tangent_t, hidden_t, weight, act, send = pl.pallas_call(
        functools.partial(forward_kernel, devices, inv_d, inv_ff, spots, splits),
        in_specs=[SMALL] + [FAST] * 3 + [FAR] * 6,
        out_specs=[FAST] * 7,
        out_shape=[
            jax.ShapeDtypeStruct((LIVE, width), BF16),
            jax.ShapeDtypeStruct((rows, LIVE), BF16),
            jax.ShapeDtypeStruct((LIVE, rows), BF16),
            jax.ShapeDtypeStruct((LIVE, rows), BF16),
            jax.ShapeDtypeStruct((rows, LIVE), F32),
            jax.ShapeDtypeStruct((rows, LIVE), F32),
            jax.ShapeDtypeStruct((devices // 2, chunk_rows, LANES), BF16),
        ],
        scratch_shapes=[
            pltpu.VMEM((rows // long, 4, long, width), BF16),
            pltpu.VMEM((2, rows, halved), BF16),
            pltpu.VMEM((rows, LIVE), BF16),
            pltpu.SemaphoreType.DMA((rows // long, 4)),
            pltpu.SemaphoreType.DMA((2,)),
        ],
        compiler_params=params(24),
        cost_estimate=cost(5 * product_flops, 10 * rows * width + 6 * LIVE * width, rows * LIVE),
        name="forward",
    )(
        info, lower, upper, norm_gain.reshape(1, width), far(gate_rows), far(up_rows),
        far(krylov_gate), far(krylov_up), far(down_rows), far(krylov_down),
    )

    def product(krylov, before):
        return pl.pallas_call(
            product_kernel,
            in_specs=[FAR, FAST],
            out_specs=[FAST, FAST],
            out_shape=[
                jax.ShapeDtypeStruct((basis, rows, LIVE), F32),
                jax.ShapeDtypeStruct((LIVE, LIVE), F32),
            ],
            scratch_shapes=[
                pltpu.VMEM((pieces, basis, lines, width), BF16),
                pltpu.SemaphoreType.DMA((pieces,)),
            ],
            compiler_params=params(28),
            cost_estimate=cost(
                basis * product_flops, 2 * basis * rows * width + 4 * basis * rows * LIVE
            ),
            name="product",
        )(far(after(krylov, before)), normed)

    got = exchange(send, 1)
    keep = pl.pallas_call(
        functools.partial(keep_kernel, devices, inv_ff, splits),
        in_specs=[SMALL, FAST, FAST, FAR, FAR],
        out_specs=FAST,
        out_shape=jax.ShapeDtypeStruct((devices // 2, chunk_rows, LANES), F32),
        scratch_shapes=[
            pltpu.VMEM((2, rows, halved), BF16),
            pltpu.SemaphoreType.DMA((2,)),
        ],
        compiler_params=params(8),
        cost_estimate=cost(product_flops, 2 * rows * width + 2 * LIVE * width),
        name="keep",
    )(info, tangent_t, hidden_t, far(down_rows), far(krylov_down))

    per = long // lines
    part = pieces // per // 2 * per
    shares = [number for number in (part, pieces - part) if number]
    up_jobs = [(sum(shares[:at]), number) for at, number in enumerate(shares)]
    up_spans = [(first * lines, number * lines) for first, number in up_jobs]
    prods_up, kept_up = [], []

    def next_both(before):
        if not up_jobs:
            return None
        first, number = up_jobs.pop(0)
        made = both(krylov_up, first, number, gram_sums[-1], normed, before)

        def done(made):
            prods_up.append(made[0])
            gram_sums.append(made[1])
            kept_up.extend(made[2:])

        return made, done

    got = [got]
    for at, group in enumerate(groups[1:]):
        parts = flips(group)
        part = keep.shape[0] // (len(parts) + 1)
        sends = [
            add_up([one[turn * part : (turn + 1) * part].astype(F32) for one in [keep] + got])
            for turn in range(1, len(parts) + 1)
        ]
        keep = add_up([one[:part].astype(F32) for one in [keep] + got])
        sends = [one.astype(BF16) for one in sends]
        got = [exchange(one, flip) for one, flip in zip(sends, parts)]
        if at == 0:
            got, (prod_gate, square) = lax.optimization_barrier(
                (got, product(krylov_gate, sends[0]))
            )
        elif up_jobs:
            made, done = next_both(sends[0])
            got, made = lax.optimization_barrier((got, made))
            done(made)
    loss_own = add_up([one.astype(F32) for one in [keep] + got]).astype(BF16)

    back_flops = (basis + 1) * product_flops // 2 + size * size * width * pieces

    def half_call(lower):
        return pl.pallas_call(
            functools.partial(back_half_kernel, devices, inv_ff, splits),
            in_specs=[SMALL, FAST, FAR, FAR, FAST, FAST],
            out_specs=[FAST] * 4,
            out_shape=[
                jax.ShapeDtypeStruct((size, size), F32),
                jax.ShapeDtypeStruct((rows, LIVE), F32),
                jax.ShapeDtypeStruct((2, LIVE, LIVE), F32),
                jax.ShapeDtypeStruct((basis, LIVE), F32),
            ],
            scratch_shapes=[
                pltpu.VMEM((LIVE, halved), BF16),
                pltpu.VMEM((rows, halved), BF16),
                pltpu.VMEM((pieces, basis, lines, halved), BF16),
                pltpu.SemaphoreType.DMA((pieces + 1,)),
            ],
            compiler_params=params(18),
            cost_estimate=cost(back_flops, (basis + 1) * rows * width),
            name="back_half",
        )(info, lower, far(down_rows), far(krylov_down), hidden, gram_sums[-1])

    halves = []

    def beside(group, block):
        if group[0] == 0:
            return half_call(block), halves.extend
        return next_both(block) if group == groups[1] else None

    lower, upper = gather_blocks(loss_own, groups, beside)
    gram_sum, back_half, squares_half, values_half = halves

    s_term, r_term, stats, down_high = pl.pallas_call(
        functools.partial(back_kernel, devices, inv_d, inv_ff, splits, up_spans),
        in_specs=[SMALL, FAST, FAR, FAR] + [FAST] * (9 + len(prods_up)),
        out_specs=[FAST] * 4,
        out_shape=[
            jax.ShapeDtypeStruct((rows, LIVE), BF16),
            jax.ShapeDtypeStruct((rows, LIVE), BF16),
            jax.ShapeDtypeStruct((basis, LANES), F32),
            jax.ShapeDtypeStruct((pieces, basis, lines, halved), BF16),
        ],
        scratch_shapes=[
            pltpu.VMEM((LIVE, halved), BF16),
            pltpu.VMEM((rows, halved), BF16),
            pltpu.VMEM((size, size), F32),
            pltpu.SemaphoreType.DMA((pieces + 1,)),
        ],
        compiler_params=params(8),
        cost_estimate=cost(
            back_flops, (basis + 1) * rows * width + 8 * basis * rows * LIVE
        ),
        name="back",
    )(
        info, upper, far(down_rows), far(krylov_down), hidden, weight, act, square,
        squares_half, back_half, gram_sum, values_half, prod_gate, *prods_up,
    )

    stats = jnp.broadcast_to(stats[None], (devices, basis, LANES))
    stats = lax.all_to_all(stats, "fsdp", 0, 0, tiled=True)

    depth = min(per + 1, pieces)
    out_shape = jax.ShapeDtypeStruct((rows, width), BF16)
    new_gate, new_up, new_down, coefficients = pl.pallas_call(
        functools.partial(new_kernel, devices, count, inv_d, inv_ff, splits, per, len(kept_up)),
        in_specs=[SMALL] + [FAST] * 7 + [FAR] * 2 + [FAST] * (1 + len(kept_up)),
        out_specs=[FAR] * 3 + [SMALL],
        out_shape=[out_shape, out_shape, out_shape, jax.ShapeDtypeStruct((basis + 1,), F32)],
        scratch_shapes=[
            pltpu.VMEM((LIVE, width), BF16),
            pltpu.VMEM((3 * long, basis // 2 * long), BF16),
            pltpu.VMEM((rows, width), F32),
            pltpu.VMEM((depth, basis, lines, width), BF16),
            pltpu.VMEM((depth, basis, lines, halved), BF16),
            pltpu.VMEM((2, long, width), BF16),
            pltpu.SemaphoreType.DMA((2, depth)),
            pltpu.SemaphoreType.DMA((2,)),
        ],
        compiler_params=params(18),
        cost_estimate=cost(3 * product_flops, 6 * (basis + 1) * rows * width),
        name="new",
    )(
        info, stats, s_term, r_term, hidden, normed, lower, upper, far(krylov_gate),
        far(krylov_down), down_high, *kept_up,
    )
    return (new_gate, new_up, new_down, coefficients)


def solution(mesh):
    placed = (
        P("fsdp", None),
        P(),
        P(),
        P("fsdp", None),
        P("fsdp", None),
        P("fsdp", None),
        P(None, "fsdp", None),
        P(None, "fsdp", None),
        P(None, "fsdp", None),
    )
    return jax.shard_map(
        per_device,
        mesh=mesh,
        in_specs=placed,
        out_specs=(P("fsdp", None), P("fsdp", None), P("fsdp", None), P()),
        check_vma=False,
    )
```

```python
import functools
import math

import jax
import jax.numpy as jnp
from jax import lax
from jax.experimental import pallas as pl
from jax.experimental.pallas import tpu as pltpu
from jax.sharding import PartitionSpec as P

LEN = 128
LIVE = 192
GROUP = 8
LANES = 128
F32 = jnp.float32
BF16 = jnp.bfloat16


def gelu_pair(gate_pre):
    coef = math.sqrt(2.0 / math.pi)
    cube = gate_pre * gate_pre * gate_pre
    tanh_val = jnp.tanh(coef * (gate_pre + 0.044715 * cube))
    act = 0.5 * gate_pre * (1.0 + tanh_val)
    slope = 0.5 * (1.0 + tanh_val) + 0.5 * gate_pre * (1.0 - tanh_val * tanh_val) * coef * (
        1.0 + 3.0 * 0.044715 * gate_pre * gate_pre
    )
    return (act, slope)


def dot_nn(left, right):
    return jnp.dot(left, right, preferred_element_type=F32)


def dot_nt(left, right):
    return lax.dot_general(left, right, (((1,), (1,)), ((), ())), preferred_element_type=F32)


def dot_tn(left, right):
    return lax.dot_general(left, right, (((0,), (0,)), ((), ())), preferred_element_type=F32)


def total(values):
    return jnp.sum(jnp.sum(values, axis=0, keepdims=True), axis=1, keepdims=True)


def reverse_bits(value, bits):
    out = value * 0
    for bit in range(bits):
        out = out | (((value >> bit) & 1) << (bits - 1 - bit))
    return out


def exchange(block, flip):
    count = lax.axis_size("fsdp")
    return lax.ppermute(block, "fsdp", [(one, one ^ flip) for one in range(count)])


def bit_groups(bits):
    return [(0, 1)] + [(low, min(2, bits - low)) for low in range(1, bits, 2)]


def flips(group):
    low, size = group
    return [reverse_bits(part, size) << low for part in range(1, 1 << size)]


def gather_blocks(block, groups, beside):
    for group in reversed(groups):
        others = [exchange(block, flip) for flip in flips(group)]
        job = beside(group, block)
        if job is not None:
            work, done = job
            others, made = lax.optimization_barrier((others, work))
            done(made)
        if group[0]:
            block = jnp.concatenate([block] + others, axis=0)
    return block, others[0]


def add_up(values):
    while len(values) > 1:
        values = [one + two for one, two in zip(values[0::2], values[1::2])]
    return values[0]


def far(value):
    return pltpu.with_memory_space_constraint(value, pltpu.HBM)


def after(value, earlier):
    return lax.optimization_barrier((value, earlier))[0]


def stacked(krylov):
    basis, rows, width = krylov.shape
    if rows % 16:
        return krylov.astype(F32).reshape(basis * rows, width).astype(BF16)
    return krylov.reshape(basis * rows, width)


def params(mib):
    return pltpu.CompilerParams(vmem_limit_bytes=mib << 20)


def cost(flops, read, transcendentals=0):
    return pl.CostEstimate(flops=flops, bytes_accessed=read, transcendentals=transcendentals)


FAST = pl.BlockSpec(memory_space=pltpu.VMEM)
SMALL = pl.BlockSpec(memory_space=pltpu.SMEM)
FAR = pl.BlockSpec(memory_space=pltpu.HBM)


def call(name, body, operands, results, scratch, fetches, price, mib=6):
    counts = [len(arrays) for arrays, _, _ in fetches]
    placed = [SMALL] + [FAR if one[0] else FAST for one in operands[1:]]
    values = [one[1] for one in operands]
    for arrays, _, _ in fetches:
        placed += [FAR] * len(arrays)
        values += [far(one) for one in arrays]
    made = [jax.ShapeDtypeStruct(shape, BF16) for _, shape, _ in fetches]
    number = sum(shape[0] * (len(arrays) if len(arrays) > 1 else 1) for arrays, shape, _ in fetches)

    def kernel(*refs):
        at = len(operands)
        own, refs = refs[:at], refs[at:]
        sources, refs = refs[: sum(counts)], refs[sum(counts) :]
        outs, refs = refs[: len(results)], refs[len(results) :]
        targets, refs = refs[: len(fetches)], refs[len(fetches) :]
        copies = []
        for (_, _, pairs), count, target in zip(fetches, counts, targets):
            for source, goal in pairs(own[0], sources[:count], target):
                copies.append(pltpu.make_async_copy(source, goal, refs[-1].at[len(copies)]))
            sources = sources[count:]
        for copy in copies:
            copy.start()
        body(*own, *outs, *refs[: len(scratch)])
        for copy in copies:
            copy.wait()

    return pl.pallas_call(
        kernel,
        in_specs=placed,
        out_specs=[FAST] * (len(results) + len(fetches)),
        out_shape=list(results) + made,
        scratch_shapes=list(scratch) + [pltpu.SemaphoreType.DMA((max(1, number),))],
        compiler_params=params(mib),
        cost_estimate=price,
        name=name,
    )(*values)


def near(value):
    return (False, value)


def block_rows(rows):
    return 64 if rows % 64 == 0 else rows


def half_start(flip, devices, width, other):
    top = lax.div(flip, devices // 2) ^ other
    return pl.multiple_of(top * (width // 2), width // 2)


def live_tokens(info, lower, upper, gain, normed, spots):
    spare = info[1] - (LIVE - LEN)
    shift = lax.rem(spare, GROUP)
    half = (LIVE - LEN) // GROUP
    per = LEN // GROUP
    scale = gain[...].astype(F32)
    row_ids = lax.broadcasted_iota(jnp.int32, (GROUP, 1), 0)

    half_groups = lower.shape[0]

    def load(group):
        spot = spots(info[0], group)
        place = lax.rem(spot, half_groups)
        return jnp.where(spot < half_groups, lower[place], upper[place]).astype(F32)

    def tokens(slot):
        if slot < half:
            return load(slot)
        if slot < 2 * half:
            at = slot - half
            first = load(half + at)
            second = pltpu.roll(load(per + 2 * half - 1 - at), shift, 0)
            return jnp.where(GROUP * at + row_ids < spare, first, second)
        return load(per + slot - 2 * half)

    def norm(wide):
        mean = jnp.mean(wide * wide, axis=1, keepdims=True)
        return wide * lax.rsqrt(mean + 1e-06) * scale

    for pair in range(LIVE // (2 * GROUP)):
        both = [norm(tokens(2 * pair + side)) for side in range(2)]
        normed[2 * GROUP * pair : 2 * GROUP * (pair + 1), :] = jnp.concatenate(both, 0).astype(BF16)


def jvp_half(info, tangent_t, hidden_t, down, probe, out, inv_ff, splits):
    rows = LIVE // splits
    places = out.shape[0]
    width = down.shape[1]
    step = min(512, width)
    each = step // LANES
    for at in range(width // step):
        here = slice(at * step, (at + 1) * step)
        values = dot_nn(tangent_t, down[:, here]) + dot_nn(hidden_t, probe[:, here]) * inv_ff
        for column in range(each):
            for part in range(splits):
                piece = values[
                    part * rows : (part + 1) * rows, column * LANES : (column + 1) * LANES
                ]
                chunk = (at * each + column) * splits + part
                out[chunk ^ (info[0] & (places - 1))] = piece.astype(out.dtype)


def down_copies(info, devices, other, sources, held, sems):
    width = held.shape[2]
    start = half_start(info[0], devices, 2 * width, other)
    return [
        pltpu.make_async_copy(source.at[:, pl.ds(start, width)], held.at[at], sems.at[at])
        for at, source in enumerate(sources)
    ]


def forward_kernel(
    devices, inv_d, inv_ff, spots, splits,
    info, lower, upper, gain, gate, up, krylov_gate, krylov_up, down, krylov_down,
    normed, hidden, tangent_t, hidden_t, weight, act_out, send,
    held, held_down, tangent, row_sems, sems,
):
    basis = krylov_down.shape[0]
    count, _, lines, width = held.shape
    sources = (gate, up, krylov_gate.at[basis - 1], krylov_up.at[basis - 1])
    copies = [
        [
            pltpu.make_async_copy(
                source.at[at * lines : (at + 1) * lines], held.at[at, one], row_sems.at[at, one]
            )
            for one, source in enumerate(sources)
        ]
        for at in range(count)
    ]
    for copy in sum(copies, []):
        copy.start()
    last = down_copies(info, devices, 1, (down, krylov_down.at[basis - 1]), held_down, sems)
    for copy in last:
        copy.start()
    live_tokens(info, lower, upper, gain, normed, spots)
    for at in range(count):
        for copy in copies[at]:
            copy.wait()
        made = dot_nt(stacked(held[at]), normed[...])
        gate_pre, up_pre, tan_gate, tan_up = (
            made[one * lines : (one + 1) * lines] for one in range(4)
        )
        act, slope = gelu_pair(gate_pre)
        here = slice(at * lines, (at + 1) * lines)
        hidden[here, :] = (act * up_pre).astype(BF16)
        tangent[here, :] = (
            slope * (tan_gate * inv_d) * up_pre + act * (tan_up * inv_d)
        ).astype(BF16)
        weight[here, :] = up_pre * slope
        act_out[here, :] = act
    tangent_t[...] = tangent[...].T
    hidden_t[...] = hidden[...].T
    for copy in last:
        copy.wait()
    jvp_half(
        info, tangent_t[...], hidden_t[...], held_down.at[0], held_down.at[1], send, inv_ff, splits
    )


def keep_kernel(inv_ff, splits, info, tangent_t, hidden_t, held_down, keep):
    jvp_half(
        info, tangent_t[...], hidden_t[...], held_down.at[0], held_down.at[1], keep, inv_ff, splits
    )


def fold_gram(sums, basis, lines):
    size = basis * lines
    own = lax.broadcasted_iota(jnp.int32, (size, size), 0)
    other = lax.broadcasted_iota(jnp.int32, (size, size), 1)
    if lines & (lines - 1) == 0:
        same = (own & (lines - 1)) == (other & (lines - 1))
    else:
        same = lax.rem(own, lines) == lax.rem(other, lines)
    kept = jnp.where(same, sums, 0.0)
    rows = [
        jnp.sum(kept[one * lines : (one + 1) * lines], axis=0, keepdims=True)
        for one in range(basis)
    ]
    place = lax.broadcasted_iota(jnp.int32, (size, LANES), 0)
    lane = lax.broadcasted_iota(jnp.int32, (size, LANES), 1) * lines
    picks = jnp.where((place >= lane) & (place < lane + lines), 1.0, 0.0).astype(F32)
    return jnp.dot(
        jnp.concatenate(rows, axis=0), picks,
        precision=lax.Precision.HIGHEST, preferred_element_type=F32,
    )


def gram_kernel(start, info, held, *rest):
    out = rest[-1]
    out[...] = jnp.zeros_like(out) if start else rest[0][...]

    def body(at, carry):
        stack = stacked(held[at])
        out[...] += dot_nt(stack, stack)
        return carry

    lax.fori_loop(0, held.shape[0], body, 0)


def put_products(held, normed, out, ahead, sums):
    count, basis, lines, _ = held.shape

    def body(at, carry):
        stack = stacked(held[at])
        if sums is not None:
            sums[...] += dot_nt(stack, stack)
        made = dot_nt(stack, normed[...])
        here = pl.ds(pl.multiple_of((ahead + at) * lines, lines), lines)
        for one in range(basis):
            out[one, here, :] = made[one * lines : (one + 1) * lines]
        return carry

    lax.fori_loop(0, count, body, 0)


def product_kernel(info, normed, *rest):
    helds, (out, square) = rest[:-2], rest[-2:]
    square[...] = dot_nt(normed[...], normed[...])
    ahead = 0
    for held in helds:
        put_products(held, normed, out, ahead, None)
        ahead += held.shape[0]


def both_kernel(info, normed, earlier, held, out, sums):
    sums[...] = earlier[...]
    put_products(held, normed, out, 0, sums)


def put_loss(loss, first, flip, chunks, splits):
    places = chunks.shape[0]
    for column in range(places // splits):
        pieces = [
            chunks[(column * splits + part) ^ (flip & (places - 1))] for part in range(splits)
        ]
        if splits > 1:
            pieces = [jnp.concatenate([one.astype(F32) for one in pieces], 0).astype(BF16)]
        loss[:, first + column * LANES : first + (column + 1) * LANES] = pieces[0]


def down_products(held, ahead, loss, wide, values, grams):
    count, basis, lines, _ = held.shape
    values = list(values)
    for at in range(count):
        stack = stacked(held[at])
        grams[...] += dot_nt(stack, stack)
        made = dot_nt(stack, loss[...])
        part = wide[(ahead + at) * lines : (ahead + at + 1) * lines]
        for one in range(basis):
            value = part * made[one * lines : (one + 1) * lines]
            values[one] = values[one] + jnp.sum(value, axis=0, keepdims=True)
    return values


def back_half_kernel(
    inv_ff, splits,
    info, chunks, held, held_down, hidden, earlier, grams, back_sum, squares, values, loss,
):
    basis = held.shape[1]
    grams[...] = earlier[...]
    put_loss(loss, 0, info[0], chunks, splits)
    squares[0] = dot_nt(loss[...], loss[...])
    squares[1] = dot_tn(hidden[...], hidden[...]) * (inv_ff * inv_ff)
    back_sum[...] = dot_nt(held_down[0], loss[...])
    wide = hidden[...].astype(F32) * inv_ff
    zeros = [jnp.zeros((1, LIVE), F32) for _ in range(basis)]
    values[...] = jnp.concatenate(down_products(held, 0, loss, wide, zeros, grams), axis=0)


def back_kernel(
    devices, inv_d, inv_ff, splits, spans, more,
    info, chunks, held, held_down, hidden, weight, act, square, squares_half, back_half, earlier,
    values_half, prod_gate, *rest,
):
    prods_up, rest = rest[: len(spans)], rest[len(spans) :]
    copies, other_held = [], None
    if more:
        krylov, s_out, r_out, stats, other_held, loss, grams, sems = rest
        start = half_start(info[0], devices, krylov.shape[2], 1)
        first, lines = held.shape[0], held.shape[2]
        for at in range(more):
            here = slice((first + at) * lines, (first + at + 1) * lines)
            source = krylov.at[:, here, pl.ds(start, held.shape[3])]
            copies.append(pltpu.make_async_copy(source, other_held.at[at], sems.at[at]))
            copies[-1].start()
    else:
        s_out, r_out, stats, loss, grams = rest
    basis, lines = held.shape[1:3]
    grams[...] = earlier[...]
    put_loss(loss, 0, info[0], chunks, splits)
    back = dot_nt(held_down[0], loss[...]) + back_half[...]
    s_term = (back * weight[...]).astype(BF16)
    r_term = (back * act[...]).astype(BF16)
    s_out[...] = s_term
    r_out[...] = r_term
    squares = inv_d * inv_d * ((dot_tn(s_term, s_term) + dot_tn(r_term, r_term)) * square[...])
    other = dot_nt(loss[...], loss[...]) + squares_half[0]
    squares = total(squares + squares_half[1] * other)
    wide_s = s_term.astype(F32) * inv_d
    wide_r = r_term.astype(F32) * inv_d
    values = []
    for one in range(basis):
        value = jnp.sum(wide_s * prod_gate[one], axis=0, keepdims=True)
        for (start, number), prod in zip(spans, prods_up):
            part = wide_r[start : start + number] * prod[one]
            value = value + jnp.sum(part, axis=0, keepdims=True)
        values.append(value + values_half[one : one + 1, :])
    wide = hidden[...].astype(F32) * inv_ff
    values = down_products(held, 0, loss, wide, values, grams)
    for copy in copies:
        copy.wait()
    if copies:
        values = down_products(other_held, held.shape[0], loss, wide, values, grams)
    lined = jnp.sum(jnp.concatenate(values, axis=0), axis=1, keepdims=True)
    lane = lax.broadcasted_iota(jnp.int32, (basis, LANES), 1)
    made = fold_gram(grams[...], basis, lines)
    stats[...] = made + jnp.where(lane == basis, lined, 0.0) + jnp.where(
        lane == basis + 1, squares, 0.0
    )


def split_three(value):
    first = value.astype(BF16)
    rest = value - first.astype(F32)
    second = rest.astype(BF16)
    return first, second, (rest - second.astype(F32)).astype(BF16)


def new_kernel(
    devices, count, inv_d, inv_ff, splits, number_high,
    info, stats, s_term, r_term, hidden, normed, lower, upper, krylov_gate, krylov_up,
    krylov_down, *rest,
):
    highs, rest = rest[:number_high], rest[number_high:]
    new_gate, new_up, new_down, coefficients = rest[:4]
    loss, mixer, wide, held, held_low, outs, sems, low_sems, out_sems = rest[4:]
    depth, basis, lines, width = held.shape
    blocks = s_term.shape[0] // lines
    halved = width // 2
    size = basis * lines
    narrow = min(256, halved)
    group = min(1024, halved)
    outs_depth, low_depth = outs.shape[0], held_low.shape[0]
    targets = (new_gate, new_up, new_down)
    low_start = half_start(info[0], devices, width, 0)
    high_start = half_start(info[0], devices, width, 1)

    def copy_in(turn, part):
        block = turn - part * blocks
        here = pl.ds(pl.multiple_of(block * lines, lines), lines)
        slot = lax.rem(turn, depth)
        source = (krylov_gate, krylov_up)[part]
        return pltpu.make_async_copy(source.at[:, here, :], held.at[slot], sems.at[slot])

    def copy_low(block):
        here = pl.ds(pl.multiple_of(block * lines, lines), lines)
        slot = lax.rem(block, low_depth)
        return pltpu.make_async_copy(
            krylov_down.at[:, here, pl.ds(low_start, halved)], held_low.at[slot], low_sems.at[slot]
        )

    def copy_out(turn, block, part):
        start = pl.multiple_of(block * lines, lines)
        slot = lax.rem(turn, outs_depth)
        return pltpu.make_async_copy(
            outs.at[slot], targets[part].at[pl.ds(start, lines), :], out_sems.at[slot]
        )

    for block in range(low_depth):
        copy_low(block).start()
    for turn in range(depth):
        copy_in(turn, turn // blocks).start()

    for at, half in enumerate((lower, upper)):
        put_loss(loss, at * halved, info[0], half, splits)
    sums = stats[0]
    for one in range(1, devices):
        sums = sums + stats[one]
    lane = lax.broadcasted_iota(jnp.int32, sums.shape, 1)
    row = lax.broadcasted_iota(jnp.int32, sums.shape, 0)

    def pick(where):
        return jnp.sum(jnp.where(where, sums, 0.0))

    proj = [pick((lane == basis) & (row == one)) / count for one in range(basis)]
    squares = pick((lane == basis + 1) & (row == 0))
    for one in range(basis):
        line = jnp.zeros((1, LANES), F32)
        for two in range(basis):
            line = line + proj[two] * sums[two : two + 1, :]
        dots = pick((lane == basis) & (row == one))
        mixed = jnp.sum(jnp.where(lane[0:1] == one, line, 0.0))
        squares = squares + proj[one] * (mixed - 2.0 * dots)
    mean = jnp.maximum(jnp.full((8, LANES), squares / count, F32), 0.0)
    norm = jnp.sqrt(mean + 1e-06)
    inverse = jnp.max(1.0 / norm)
    for one in range(basis):
        coefficients[one] = proj[one]
    coefficients[basis] = jnp.max(norm)
    scales = [one * inverse for one in proj]

    lane = lax.broadcasted_iota(jnp.int32, (lines, size), 1)
    row = lax.broadcasted_iota(jnp.int32, (lines, size), 0)
    values = jnp.zeros((lines, size), F32)
    for one in range(basis):
        values = jnp.where(lane == one * lines + row, scales[one], values)
    terms = [term.astype(F32) for term in split_three(values)]
    mixer[...] = jnp.concatenate(terms, axis=0).astype(BF16)

    def put(turn, block, part, pieces):
        slot = lax.rem(turn, outs_depth)
        here = pl.ds(pl.multiple_of(block * lines, lines), lines)

        @pl.when(turn >= outs_depth)
        def _():
            copy_out(turn, block, part).wait()

        for first, last, target, read in pieces:
            for start in range(0, last - first, group):
                mixed = dot_nn(mixer[...], stacked(read(slice(start, start + group))))
                mixed = mixed[:lines] + (mixed[lines : 2 * lines] + mixed[2 * lines :])
                value = wide[here, first + start : first + start + group] - mixed
                goal = pl.ds(pl.multiple_of(target + start, group), group)
                outs[slot, :, goal] = value.astype(BF16)
        copy_out(turn, block, part).start()

    for order, part in enumerate((2, 0, 1)):
        left, right, scale = (
            (s_term, normed, inv_d), (r_term, normed, inv_d), (hidden, loss, inv_ff)
        )[part]

        def gradient(at, carry, left=left, right=right, scale=scale):
            columns = pl.ds(pl.multiple_of(at * narrow, narrow), narrow)
            wide[:, columns] = dot_nn(left[...], right[:, columns]) * (scale * inverse)
            return carry

        lax.fori_loop(0, width // narrow, gradient, 0)
        ahead = 0
        for kept in highs if part == 2 else (None,):
            number = kept.shape[0] if part == 2 else blocks

            def body(at, carry, part=part, kept=kept, ahead=ahead, order=order):
                block = ahead + at
                turn = part * blocks + block
                slot = lax.rem(turn, depth)
                low_slot = lax.rem(block, low_depth)
                if part == 2:
                    copy_low(block).wait()
                    pieces = [
                        (0, halved, low_start, lambda columns: held_low[low_slot, :, :, columns]),
                        (halved, width, high_start, lambda columns: kept[at, :, :, columns]),
                    ]
                else:
                    copy_in(turn, part).wait()
                    pieces = [(0, width, 0, lambda columns: held[slot, :, :, columns])]
                put(order * blocks + block, block, part, pieces)
                if part == 2:
                    @pl.when(block + low_depth < blocks)
                    def _():
                        copy_low(block + low_depth).start()

                else:
                    for later in range(part, 2):
                        there = (turn + depth >= later * blocks) & (
                            turn + depth < (later + 1) * blocks
                        )

                        @pl.when(there)
                        def _(later=later):
                            copy_in(turn + depth, later).start()

                return carry

            lax.fori_loop(0, number, body, 0)
            ahead += number
    for turn in range(max(0, 3 * blocks - outs_depth), 3 * blocks):
        copy_out(turn, turn % blocks, 0).wait()


def per_device(
    inputs, norm_gain, lengths, gate_rows, up_rows, down_rows, krylov_gate, krylov_up, krylov_down
):
    basis, rows, width = krylov_gate.shape
    devices = lax.axis_size("fsdp")
    bits = devices.bit_length() - 1
    groups = bit_groups(bits)
    hidden_all = rows * devices
    count = 3.0 * width * hidden_all
    inv_d = 1.0 / math.sqrt(width)
    inv_ff = 1.0 / math.sqrt(hidden_all)
    me = lax.axis_index("fsdp").astype(jnp.int32)
    mirror = reverse_bits(me, bits)
    info = jnp.stack([mirror, lengths[0]])

    splits = devices // (width // LANES)
    chunk_rows = LIVE // splits
    lines = 32 if rows % 32 == 0 else rows
    pieces = rows // lines
    long = block_rows(rows)
    halved = width // 2
    product_flops = 2 * rows * width * LIVE

    size = basis * lines

    def rows_of(krylov, first, number):
        def pairs(_, sources, target):
            return [
                (
                    sources[0].at[:, (first + at) * lines : (first + at + 1) * lines, :],
                    target.at[at],
                )
                for at in range(number)
            ]

        return ((krylov,), (number, basis, lines, width), pairs)

    def half_columns(other, before, number):
        def start(info):
            return pl.ds(half_start(info[0], devices, width, other), halved)

        def pairs(info, sources, target):
            return [
                (
                    sources[0].at[:, at * lines : (at + 1) * lines, start(info)],
                    target.at[at],
                )
                for at in range(number)
            ]

        def down_pairs(info, sources, target):
            return [(sources[0].at[:, start(info)], target.at[0])]

        krylov, down = after((krylov_down, down_rows), before)
        return [
            ((krylov,), (number, basis, lines, halved), pairs),
            ((down,), (1, rows, halved), down_pairs),
        ]

    def keep_columns():
        def pairs(info, sources, target):
            columns = pl.ds(half_start(info[0], devices, width, 0), halved)
            return [
                (sources[0].at[:, columns], target.at[0]),
                (sources[1].at[basis - 1, :, columns], target.at[1]),
            ]

        return ((down_rows, krylov_down), (2, rows, halved), pairs)

    cut = (pieces + 1) // 2
    spans = [span for span in ((0, cut), (cut, pieces - cut)) if span[1]]
    helds, gram_sums = [], []

    def gram_stage(group, before):
        at = len(gram_sums) + 1 if helds else 0
        if at > len(spans):
            return None
        operands, results, body = [near(info)], [], lambda info: None
        if at:
            operands += [near(helds[at - 1])] + [near(one) for one in gram_sums[-1:]]
            results = [jax.ShapeDtypeStruct((size, size), F32)]
            body = functools.partial(gram_kernel, not gram_sums)
        fetches = [rows_of(after(krylov_gate, before), *span) for span in spans[at : at + 1]]
        made = call(
            "gram" if at else "read", body, operands, results, [], fetches,
            cost(2 * size * size * width * (cut if at else 1), 2 * size * width * cut),
        )

        def done(made):
            gram_sums.extend(made[: len(results)])
            helds.extend(made[len(results) :])

        return made, done

    own_tokens = inputs.shape[0]
    tokens = own_tokens * devices
    if own_tokens % GROUP == 0:
        sub = own_tokens // GROUP
        lower, upper = gather_blocks(inputs.reshape(sub, GROUP, width), groups, gram_stage)

        def spots(flip, group):
            return (reverse_bits(group // sub, bits) ^ flip) * sub + group % sub

    else:
        gathered = lax.all_gather(inputs, "fsdp", axis=0, tiled=True)
        gathered = gathered.reshape(tokens // GROUP, GROUP, width)
        lower, upper = jnp.split(gathered, 2)

        def spots(flip, group):
            return group

    while len(gram_sums) < len(spans):
        made, done = gram_stage(None, inputs)
        done(made)

    normed, hidden, tangent_t, hidden_t, weight, act, send, keep_down = call(
        "forward",
        functools.partial(forward_kernel, devices, inv_d, inv_ff, spots, splits),
        [
            near(info), near(lower), near(upper), near(norm_gain.reshape(1, width)),
            *(
                (True, far(one))
                for one in (gate_rows, up_rows, krylov_gate, krylov_up, down_rows, krylov_down)
            ),
        ],
        [
            jax.ShapeDtypeStruct((LIVE, width), BF16),
            jax.ShapeDtypeStruct((rows, LIVE), BF16),
            jax.ShapeDtypeStruct((LIVE, rows), BF16),
            jax.ShapeDtypeStruct((LIVE, rows), BF16),
            jax.ShapeDtypeStruct((rows, LIVE), F32),
            jax.ShapeDtypeStruct((rows, LIVE), F32),
            jax.ShapeDtypeStruct((devices // 2, chunk_rows, LANES), BF16),
        ],
        [
            pltpu.VMEM((rows // long, 4, long, width), BF16),
            pltpu.VMEM((2, rows, halved), BF16),
            pltpu.VMEM((rows, LIVE), BF16),
            pltpu.SemaphoreType.DMA((rows // long, 4)),
            pltpu.SemaphoreType.DMA((2,)),
        ],
        [keep_columns()],
        cost(5 * product_flops, 12 * rows * width, rows * LIVE),
        24,
    )

    got = exchange(send, 1)
    (keep,) = call(
        "keep",
        functools.partial(keep_kernel, inv_ff, splits),
        [near(info), near(tangent_t), near(hidden_t), near(keep_down)],
        [jax.ShapeDtypeStruct((devices // 2, chunk_rows, LANES), F32)],
        [],
        [],
        cost(product_flops, 2 * rows * width + 2 * LIVE * width),
    )

    shares = [pieces - 2 * (pieces // 3), pieces // 3, pieces // 3]
    up_jobs = [(sum(shares[:at]), number) for at, number in enumerate(shares) if number]
    up_spans = [(first * lines, number * lines) for first, number in up_jobs]
    prods_up, ups, ahead = [], [], []

    def product(before):
        return call(
            "product",
            product_kernel,
            [near(info), near(normed)] + [near(one) for one in helds],
            [
                jax.ShapeDtypeStruct((basis, rows, LIVE), F32),
                jax.ShapeDtypeStruct((LIVE, LIVE), F32),
            ],
            [],
            [rows_of(after(krylov_up, before), *up_jobs[0])],
            cost(basis * product_flops, 2 * size * width * up_jobs[0][1]),
        )

    def next_both(before):
        at = len(prods_up)
        if at == len(up_jobs):
            return None
        number = up_jobs[at][1]
        if at + 1 < len(up_jobs):
            fetches = [rows_of(after(krylov_up, before), *up_jobs[at + 1])]
        else:
            fetches = half_columns(0, before, pieces)
        made = call(
            "both",
            both_kernel,
            [near(info), near(normed), near(gram_sums[-1]), near(ups[-1])],
            [
                jax.ShapeDtypeStruct((basis, number * lines, LIVE), F32),
                jax.ShapeDtypeStruct((size, size), F32),
            ],
            [],
            fetches,
            cost(2 * size * (size + LIVE) * width * number, 2 * size * width * number),
        )

        def done(made):
            prods_up.append(made[0])
            gram_sums.append(made[1])
            (ups if len(made) == 3 else ahead).extend(made[2:])

        return made, done

    got = [got]
    for at, group in enumerate(groups[1:]):
        parts = flips(group)
        part = keep.shape[0] // (len(parts) + 1)
        sends = [
            add_up([one[turn * part : (turn + 1) * part].astype(F32) for one in [keep] + got])
            for turn in range(1, len(parts) + 1)
        ]
        keep = add_up([one[:part].astype(F32) for one in [keep] + got])
        sends = [one.astype(BF16) for one in sends]
        got = [exchange(one, flip) for one, flip in zip(sends, parts)]
        if at == 0:
            got, (prod_gate, square, first_up) = lax.optimization_barrier((got, product(sends[0])))
            ups.append(first_up)
        elif len(prods_up) < len(up_jobs):
            made, done = next_both(sends[0])
            got, made = lax.optimization_barrier((got, made))
            done(made)
    loss_own = add_up([one.astype(F32) for one in [keep] + got]).astype(BF16)

    back_flops = (basis + 1) * product_flops // 2 + size * size * width * pieces

    def half_call(lower):
        down_low, rows_low = ahead
        return call(
            "back_half",
            functools.partial(back_half_kernel, inv_ff, splits),
            [
                near(info), near(lower), near(down_low), near(rows_low), near(hidden),
                near(gram_sums[-1]),
            ],
            [
                jax.ShapeDtypeStruct((size, size), F32),
                jax.ShapeDtypeStruct((rows, LIVE), F32),
                jax.ShapeDtypeStruct((2, LIVE, LIVE), F32),
                jax.ShapeDtypeStruct((basis, LIVE), F32),
            ],
            [pltpu.VMEM((LIVE, halved), BF16)],
            half_columns(1, lower, pieces),
            cost(back_flops, (basis + 1) * rows * width),
        )

    halves = []

    def beside(group, block):
        if group[0] == 0:
            return half_call(block), halves.extend
        return next_both(block)

    lower, upper = gather_blocks(loss_own, groups, beside)
    gram_sum, back_half, squares_half, values_half, down_high, rows_high = halves

    more = 0
    s_term, r_term, stats, *rest_high = call(
        "back",
        functools.partial(back_kernel, devices, inv_d, inv_ff, splits, up_spans, more),
        [
            near(one)
            for one in (
                info, upper, down_high, rows_high, hidden, weight, act, square, squares_half,
                back_half, gram_sum, values_half, prod_gate, *prods_up,
            )
        ]
        + ([(True, far(krylov_down))] if more else []),
        [
            jax.ShapeDtypeStruct((rows, LIVE), BF16),
            jax.ShapeDtypeStruct((rows, LIVE), BF16),
            jax.ShapeDtypeStruct((basis, LANES), F32),
        ]
        + ([jax.ShapeDtypeStruct((more, basis, lines, halved), BF16)] if more else []),
        [pltpu.VMEM((LIVE, halved), BF16), pltpu.VMEM((size, size), F32)]
        + ([pltpu.SemaphoreType.DMA((more,))] if more else []),
        [],
        cost(back_flops, 8 * basis * rows * LIVE),
    )
    highs = [down_high] + rest_high

    stats = jnp.broadcast_to(stats[None], (devices, basis, LANES))
    stats = lax.all_to_all(stats, "fsdp", 0, 0, tiled=True)

    depth, outs_depth = min(4, pieces), min(4, 3 * pieces)
    out_shape = jax.ShapeDtypeStruct((rows, width), BF16)
    new_gate, new_up, new_down, coefficients = pl.pallas_call(
        functools.partial(new_kernel, devices, count, inv_d, inv_ff, splits, len(highs)),
        in_specs=[SMALL] + [FAST] * 7 + [FAR] * 3 + [FAST] * len(highs),
        out_specs=[FAR] * 3 + [SMALL],
        out_shape=[out_shape, out_shape, out_shape, jax.ShapeDtypeStruct((basis + 1,), F32)],
        scratch_shapes=[
            pltpu.VMEM((LIVE, width), BF16),
            pltpu.VMEM((3 * lines, size), BF16),
            pltpu.VMEM((rows, width), F32),
            pltpu.VMEM((depth, basis, lines, width), BF16),
            pltpu.VMEM((depth, basis, lines, halved), BF16),
            pltpu.VMEM((outs_depth, lines, width), BF16),
            pltpu.SemaphoreType.DMA((depth,)),
            pltpu.SemaphoreType.DMA((depth,)),
            pltpu.SemaphoreType.DMA((outs_depth,)),
        ],
        compiler_params=params(22),
        cost_estimate=cost(3 * product_flops, 6 * (basis + 1) * rows * width),
        name="new",
    )(
        info, stats, s_term, r_term, hidden, normed, lower, upper, far(krylov_gate),
        far(krylov_up), far(krylov_down), *highs,
    )
    return (new_gate, new_up, new_down, coefficients)


def solution(mesh):
    placed = (
        P("fsdp", None),
        P(),
        P(),
        P("fsdp", None),
        P("fsdp", None),
        P("fsdp", None),
        P(None, "fsdp", None),
        P(None, "fsdp", None),
        P(None, "fsdp", None),
    )
    return jax.shard_map(
        per_device,
        mesh=mesh,
        in_specs=placed,
        out_specs=(P("fsdp", None), P("fsdp", None), P("fsdp", None), P()),
        check_vma=False,
    )
```

```python
import functools
import math

import jax
import jax.numpy as jnp
from jax import lax
from jax.experimental import pallas as pl
from jax.experimental.pallas import tpu as pltpu
from jax.sharding import PartitionSpec as P

LEN = 128
LIVE = 192
GROUP = 8
LANES = 128
F32 = jnp.float32
BF16 = jnp.bfloat16


def gelu_pair(gate_pre):
    coef = math.sqrt(2.0 / math.pi)
    cube = gate_pre * gate_pre * gate_pre
    tanh_val = jnp.tanh(coef * (gate_pre + 0.044715 * cube))
    act = 0.5 * gate_pre * (1.0 + tanh_val)
    slope = 0.5 * (1.0 + tanh_val) + 0.5 * gate_pre * (1.0 - tanh_val * tanh_val) * coef * (
        1.0 + 3.0 * 0.044715 * gate_pre * gate_pre
    )
    return (act, slope)


def dot_nn(left, right):
    return jnp.dot(left, right, preferred_element_type=F32)


def dot_nt(left, right):
    return lax.dot_general(left, right, (((1,), (1,)), ((), ())), preferred_element_type=F32)


def dot_tn(left, right):
    return lax.dot_general(left, right, (((0,), (0,)), ((), ())), preferred_element_type=F32)


def total(values):
    return jnp.sum(jnp.sum(values, axis=0, keepdims=True), axis=1, keepdims=True)


def reverse_bits(value, bits):
    out = value * 0
    for bit in range(bits):
        out = out | (((value >> bit) & 1) << (bits - 1 - bit))
    return out


def exchange(block, flip):
    count = lax.axis_size("fsdp")
    return lax.ppermute(block, "fsdp", [(one, one ^ flip) for one in range(count)])


def bit_groups(bits):
    return [(0, 1)] + [(low, min(2, bits - low)) for low in range(1, bits, 2)]


def flips(group):
    low, size = group
    return [reverse_bits(part, size) << low for part in range(1, 1 << size)]


def gather_blocks(block, groups, beside):
    for group in reversed(groups):
        others = [exchange(block, flip) for flip in flips(group)]
        job = beside(group, block)
        if job is not None:
            work, done = job
            others, made = lax.optimization_barrier((others, work))
            done(made)
        if group[0]:
            block = jnp.concatenate([block] + others, axis=0)
    return block, others[0]


def add_up(values):
    while len(values) > 1:
        values = [one + two for one, two in zip(values[0::2], values[1::2])]
    return values[0]


def far(value):
    return pltpu.with_memory_space_constraint(value, pltpu.HBM)


def after(value, earlier):
    return lax.optimization_barrier((value, earlier))[0]


def stacked(krylov):
    basis, rows, width = krylov.shape
    if rows % 16:
        return krylov.astype(F32).reshape(basis * rows, width).astype(BF16)
    return krylov.reshape(basis * rows, width)


def params(mib):
    return pltpu.CompilerParams(vmem_limit_bytes=mib << 20)


def cost(flops, read, transcendentals=0):
    return pl.CostEstimate(flops=flops, bytes_accessed=read, transcendentals=transcendentals)


FAST = pl.BlockSpec(memory_space=pltpu.VMEM)
SMALL = pl.BlockSpec(memory_space=pltpu.SMEM)
FAR = pl.BlockSpec(memory_space=pltpu.HBM)


def call(name, body, operands, results, scratch, fetches, price, mib=5):
    counts = [len(arrays) for arrays, _, _ in fetches]
    placed = [SMALL] + [FAR if one[0] else FAST for one in operands[1:]]
    values = [one[1] for one in operands]
    for arrays, _, _ in fetches:
        placed += [FAR] * len(arrays)
        values += [far(one) for one in arrays]
    made = [jax.ShapeDtypeStruct(shape, BF16) for _, shape, _ in fetches]
    number = sum(shape[0] * (len(arrays) if len(arrays) > 1 else 1) for arrays, shape, _ in fetches)

    def kernel(*refs):
        at = len(operands)
        own, refs = refs[:at], refs[at:]
        sources, refs = refs[: sum(counts)], refs[sum(counts) :]
        outs, refs = refs[: len(results)], refs[len(results) :]
        targets, refs = refs[: len(fetches)], refs[len(fetches) :]
        copies = []
        for (_, _, pairs), count, target in zip(fetches, counts, targets):
            for source, goal in pairs(own[0], sources[:count], target):
                copies.append(pltpu.make_async_copy(source, goal, refs[-1].at[len(copies)]))
            sources = sources[count:]
        for copy in copies:
            copy.start()
        body(*own, *outs, *refs[: len(scratch)])
        for copy in copies:
            copy.wait()

    return pl.pallas_call(
        kernel,
        in_specs=placed,
        out_specs=[FAST] * (len(results) + len(fetches)),
        out_shape=list(results) + made,
        scratch_shapes=list(scratch) + [pltpu.SemaphoreType.DMA((max(1, number),))],
        compiler_params=params(mib),
        cost_estimate=price,
        name=name,
    )(*values)


def near(value):
    return (False, value)


def block_rows(rows):
    return 64 if rows % 64 == 0 else rows


def half_start(flip, devices, width, other):
    top = lax.div(flip, devices // 2) ^ other
    return pl.multiple_of(top * (width // 2), width // 2)


def live_tokens(info, lower, upper, gain, normed, spots):
    spare = info[1] - (LIVE - LEN)
    shift = lax.rem(spare, GROUP)
    half = (LIVE - LEN) // GROUP
    per = LEN // GROUP
    scale = gain[...].astype(F32)
    row_ids = lax.broadcasted_iota(jnp.int32, (GROUP, 1), 0)

    half_groups = lower.shape[0]

    def load(group):
        spot = spots(info[0], group)
        place = lax.rem(spot, half_groups)
        return jnp.where(spot < half_groups, lower[place], upper[place]).astype(F32)

    def tokens(slot):
        if slot < half:
            return load(slot)
        if slot < 2 * half:
            at = slot - half
            first = load(half + at)
            second = pltpu.roll(load(per + 2 * half - 1 - at), shift, 0)
            return jnp.where(GROUP * at + row_ids < spare, first, second)
        return load(per + slot - 2 * half)

    def norm(wide):
        mean = jnp.mean(wide * wide, axis=1, keepdims=True)
        return wide * lax.rsqrt(mean + 1e-06) * scale

    for pair in range(LIVE // (2 * GROUP)):
        both = [norm(tokens(2 * pair + side)) for side in range(2)]
        normed[2 * GROUP * pair : 2 * GROUP * (pair + 1), :] = jnp.concatenate(both, 0).astype(BF16)


def jvp_half(info, tangent_t, hidden_t, down, probe, out, inv_ff, splits):
    rows = LIVE // splits
    places = out.shape[0]
    width = down.shape[1]
    step = min(512, width)
    each = step // LANES
    for at in range(width // step):
        here = slice(at * step, (at + 1) * step)
        values = dot_nn(tangent_t, down[:, here]) + dot_nn(hidden_t, probe[:, here]) * inv_ff
        for column in range(each):
            for part in range(splits):
                piece = values[
                    part * rows : (part + 1) * rows, column * LANES : (column + 1) * LANES
                ]
                chunk = (at * each + column) * splits + part
                out[chunk ^ (info[0] & (places - 1))] = piece.astype(out.dtype)


def down_copies(info, devices, other, sources, held, sems):
    width = held.shape[2]
    start = half_start(info[0], devices, 2 * width, other)
    return [
        pltpu.make_async_copy(source.at[:, pl.ds(start, width)], held.at[at], sems.at[at])
        for at, source in enumerate(sources)
    ]


def forward_kernel(
    devices, inv_d, inv_ff, spots, splits,
    info, lower, upper, gain, gate, up, krylov_gate, krylov_up, down, krylov_down,
    normed, hidden, tangent_t, hidden_t, weight, act_out, send,
    held, held_down, tangent, row_sems, sems,
):
    basis = krylov_down.shape[0]
    count, _, lines, width = held.shape
    sources = (gate, up, krylov_gate.at[basis - 1], krylov_up.at[basis - 1])
    copies = [
        [
            pltpu.make_async_copy(
                source.at[at * lines : (at + 1) * lines], held.at[at, one], row_sems.at[at, one]
            )
            for one, source in enumerate(sources)
        ]
        for at in range(count)
    ]
    for copy in sum(copies, []):
        copy.start()
    last = down_copies(info, devices, 1, (down, krylov_down.at[basis - 1]), held_down, sems)
    for copy in last:
        copy.start()
    live_tokens(info, lower, upper, gain, normed, spots)
    for at in range(count):
        for copy in copies[at]:
            copy.wait()
        made = dot_nt(stacked(held[at]), normed[...])
        gate_pre, up_pre, tan_gate, tan_up = (
            made[one * lines : (one + 1) * lines] for one in range(4)
        )
        act, slope = gelu_pair(gate_pre)
        here = slice(at * lines, (at + 1) * lines)
        hidden[here, :] = (act * up_pre).astype(BF16)
        tangent[here, :] = (
            slope * (tan_gate * inv_d) * up_pre + act * (tan_up * inv_d)
        ).astype(BF16)
        weight[here, :] = up_pre * slope
        act_out[here, :] = act
    tangent_t[...] = tangent[...].T
    hidden_t[...] = hidden[...].T
    for copy in last:
        copy.wait()
    jvp_half(
        info, tangent_t[...], hidden_t[...], held_down.at[0], held_down.at[1], send, inv_ff, splits
    )


def keep_kernel(inv_ff, splits, info, tangent_t, hidden_t, held_down, keep):
    jvp_half(
        info, tangent_t[...], hidden_t[...], held_down.at[0], held_down.at[1], keep, inv_ff, splits
    )


def fold_gram(sums, basis, lines):
    size = basis * lines
    own = lax.broadcasted_iota(jnp.int32, (size, size), 0)
    other = lax.broadcasted_iota(jnp.int32, (size, size), 1)
    if lines & (lines - 1) == 0:
        same = (own & (lines - 1)) == (other & (lines - 1))
    else:
        same = lax.rem(own, lines) == lax.rem(other, lines)
    kept = jnp.where(same, sums, 0.0)
    rows = [
        jnp.sum(kept[one * lines : (one + 1) * lines], axis=0, keepdims=True)
        for one in range(basis)
    ]
    place = lax.broadcasted_iota(jnp.int32, (size, LANES), 0)
    lane = lax.broadcasted_iota(jnp.int32, (size, LANES), 1) * lines
    picks = jnp.where((place >= lane) & (place < lane + lines), 1.0, 0.0).astype(F32)
    return jnp.dot(
        jnp.concatenate(rows, axis=0), picks,
        precision=lax.Precision.HIGHEST, preferred_element_type=F32,
    )


def gram_kernel(start, info, held, *rest):
    out = rest[-1]
    out[...] = jnp.zeros_like(out) if start else rest[0][...]

    def body(at, carry):
        stack = stacked(held[at])
        out[...] += dot_nt(stack, stack)
        return carry

    lax.fori_loop(0, held.shape[0], body, 0)


def put_products(held, normed, out, ahead, sums):
    count, basis, lines, _ = held.shape

    def body(at, carry):
        stack = stacked(held[at])
        if sums is not None:
            sums[...] += dot_nt(stack, stack)
        made = dot_nt(stack, normed[...])
        here = pl.ds(pl.multiple_of((ahead + at) * lines, lines), lines)
        for one in range(basis):
            out[one, here, :] = made[one * lines : (one + 1) * lines]
        return carry

    lax.fori_loop(0, count, body, 0)


def product_kernel(info, normed, *rest):
    helds, (out, square) = rest[:-2], rest[-2:]
    square[...] = dot_nt(normed[...], normed[...])
    ahead = 0
    for held in helds:
        put_products(held, normed, out, ahead, None)
        ahead += held.shape[0]


def both_kernel(info, normed, earlier, held, out, sums):
    sums[...] = earlier[...]
    put_products(held, normed, out, 0, sums)


def put_loss(loss, first, flip, chunks, splits):
    places = chunks.shape[0]
    for column in range(places // splits):
        pieces = [
            chunks[(column * splits + part) ^ (flip & (places - 1))] for part in range(splits)
        ]
        if splits > 1:
            pieces = [jnp.concatenate([one.astype(F32) for one in pieces], 0).astype(BF16)]
        loss[:, first + column * LANES : first + (column + 1) * LANES] = pieces[0]


def down_products(held, ahead, loss, wide, values, grams):
    count, basis, lines, _ = held.shape
    values = list(values)
    for at in range(count):
        stack = stacked(held[at])
        grams[...] += dot_nt(stack, stack)
        made = dot_nt(stack, loss[...])
        part = wide[(ahead + at) * lines : (ahead + at + 1) * lines]
        for one in range(basis):
            value = part * made[one * lines : (one + 1) * lines]
            values[one] = values[one] + jnp.sum(value, axis=0, keepdims=True)
    return values


def back_half_kernel(
    inv_ff, splits,
    info, chunks, held, held_down, hidden, earlier, grams, back_sum, squares, values, loss,
):
    basis = held.shape[1]
    grams[...] = earlier[...]
    put_loss(loss, 0, info[0], chunks, splits)
    squares[0] = dot_nt(loss[...], loss[...])
    squares[1] = dot_tn(hidden[...], hidden[...]) * (inv_ff * inv_ff)
    back_sum[...] = dot_nt(held_down[0], loss[...])
    wide = hidden[...].astype(F32) * inv_ff
    zeros = [jnp.zeros((1, LIVE), F32) for _ in range(basis)]
    values[...] = jnp.concatenate(down_products(held, 0, loss, wide, zeros, grams), axis=0)


def back_kernel(
    inv_d, inv_ff, splits, spans,
    info, chunks, held, held_down, hidden, weight, act, square, squares_half, back_half, earlier,
    values_half, prod_gate, *rest,
):
    prods_up, rest = rest[: len(spans)], rest[len(spans) :]
    s_out, r_out, stats, loss, grams = rest
    basis, lines = held.shape[1:3]
    grams[...] = earlier[...]
    put_loss(loss, 0, info[0], chunks, splits)
    back = dot_nt(held_down[0], loss[...]) + back_half[...]
    s_term = (back * weight[...]).astype(BF16)
    r_term = (back * act[...]).astype(BF16)
    s_out[...] = s_term
    r_out[...] = r_term
    squares = inv_d * inv_d * ((dot_tn(s_term, s_term) + dot_tn(r_term, r_term)) * square[...])
    other = dot_nt(loss[...], loss[...]) + squares_half[0]
    squares = total(squares + squares_half[1] * other)
    wide_s = s_term.astype(F32) * inv_d
    wide_r = r_term.astype(F32) * inv_d
    values = []
    for one in range(basis):
        value = jnp.sum(wide_s * prod_gate[one], axis=0, keepdims=True)
        for (start, number), prod in zip(spans, prods_up):
            part = wide_r[start : start + number] * prod[one]
            value = value + jnp.sum(part, axis=0, keepdims=True)
        values.append(value + values_half[one : one + 1, :])
    wide = hidden[...].astype(F32) * inv_ff
    values = down_products(held, 0, loss, wide, values, grams)
    lined = jnp.sum(jnp.concatenate(values, axis=0), axis=1, keepdims=True)
    lane = lax.broadcasted_iota(jnp.int32, (basis, LANES), 1)
    made = fold_gram(grams[...], basis, lines)
    stats[...] = made + jnp.where(lane == basis, lined, 0.0) + jnp.where(
        lane == basis + 1, squares, 0.0
    )


def split_three(value):
    first = value.astype(BF16)
    rest = value - first.astype(F32)
    second = rest.astype(BF16)
    return first, second, (rest - second.astype(F32)).astype(BF16)


def new_kernel(
    devices, count, inv_d, inv_ff, splits,
    info, stats, s_term, r_term, hidden, normed, lower, upper, gate, krylov_up,
    krylov_down, high,
    new_gate, new_up, new_down, coefficients,
    loss, mixer, wide, held, held_low, outs, sems, low_sems, out_sems,
):
    depth, basis, lines, width = held.shape
    blocks = s_term.shape[0] // lines
    halved = width // 2
    size = basis * lines
    narrow = min(256, halved)
    group = min(1024, halved)
    outs_depth, low_depth = outs.shape[0], held_low.shape[0]
    targets = (new_gate, new_up, new_down)
    low_start = half_start(info[0], devices, width, 0)
    high_start = half_start(info[0], devices, width, 1)

    def copy_in(block):
        here = pl.ds(pl.multiple_of(block * lines, lines), lines)
        slot = lax.rem(block, depth)
        return pltpu.make_async_copy(krylov_up.at[:, here, :], held.at[slot], sems.at[slot])

    def copy_low(block):
        here = pl.ds(pl.multiple_of(block * lines, lines), lines)
        slot = lax.rem(block, low_depth)
        return pltpu.make_async_copy(
            krylov_down.at[:, here, pl.ds(low_start, halved)], held_low.at[slot], low_sems.at[slot]
        )

    def copy_out(turn, block, part):
        start = pl.multiple_of(block * lines, lines)
        slot = lax.rem(turn, outs_depth)
        return pltpu.make_async_copy(
            outs.at[slot], targets[part].at[pl.ds(start, lines), :], out_sems.at[slot]
        )

    for block in range(low_depth):
        copy_low(block).start()
    for block in range(depth):
        copy_in(block).start()

    for at, half in enumerate((lower, upper)):
        put_loss(loss, at * halved, info[0], half, splits)
    sums = stats[0]
    for one in range(1, devices):
        sums = sums + stats[one]
    lane = lax.broadcasted_iota(jnp.int32, sums.shape, 1)
    row = lax.broadcasted_iota(jnp.int32, sums.shape, 0)

    def pick(where):
        return jnp.sum(jnp.where(where, sums, 0.0))

    proj = [pick((lane == basis) & (row == one)) / count for one in range(basis)]
    squares = pick((lane == basis + 1) & (row == 0))
    for one in range(basis):
        line = jnp.zeros((1, LANES), F32)
        for two in range(basis):
            line = line + proj[two] * sums[two : two + 1, :]
        dots = pick((lane == basis) & (row == one))
        mixed = jnp.sum(jnp.where(lane[0:1] == one, line, 0.0))
        squares = squares + proj[one] * (mixed - 2.0 * dots)
    mean = jnp.maximum(jnp.full((8, LANES), squares / count, F32), 0.0)
    norm = jnp.sqrt(mean + 1e-06)
    inverse = jnp.max(1.0 / norm)
    for one in range(basis):
        coefficients[one] = proj[one]
    coefficients[basis] = jnp.max(norm)
    scales = [one * inverse for one in proj]

    lane = lax.broadcasted_iota(jnp.int32, (lines, size), 1)
    row = lax.broadcasted_iota(jnp.int32, (lines, size), 0)
    values = jnp.zeros((lines, size), F32)
    for one in range(basis):
        values = jnp.where(lane == one * lines + row, scales[one], values)
    terms = [term.astype(F32) for term in split_three(values)]
    mixer[...] = jnp.concatenate(terms, axis=0).astype(BF16)

    def put(turn, here, block, part, pieces):
        slot = lax.rem(turn, outs_depth)

        @pl.when(turn >= outs_depth)
        def _():
            copy_out(turn, block, part).wait()

        for first, last, target, read in pieces:
            for start in range(0, last - first, group):
                mixed = dot_nn(mixer[...], stacked(read(slice(start, start + group))))
                mixed = mixed[:lines] + (mixed[lines : 2 * lines] + mixed[2 * lines :])
                value = wide[here, first + start : first + start + group] - mixed
                goal = pl.ds(pl.multiple_of(target + start, group), group)
                outs[slot, :, goal] = value.astype(BF16)
        copy_out(turn, block, part).start()

    tall = wide.shape[0]
    each = tall // lines
    for order, part in enumerate((0, 2, 1)):
        left, right, scale = (
            (s_term, normed, inv_d), (r_term, normed, inv_d), (hidden, loss, inv_ff)
        )[part]
        for share in range(blocks // each):
            for start in range(0, width, group):
                columns = slice(start, start + group)
                rows_here = slice(share * tall, (share + 1) * tall)
                made = dot_nn(left[rows_here, :], right[:, columns])
                wide[:, columns] = made * (scale * inverse)

            def body(at, carry, part=part, order=order, share=share):
                block = share * each + at
                here = pl.ds(pl.multiple_of(at * lines, lines), lines)
                slot = lax.rem(block, depth)
                low_slot = lax.rem(block, low_depth)
                if part == 0:
                    pieces = [(0, width, 0, lambda columns: gate[block, :, :, columns])]
                elif part == 1:
                    copy_in(block).wait()
                    pieces = [(0, width, 0, lambda columns: held[slot, :, :, columns])]
                else:
                    copy_low(block).wait()
                    pieces = [
                        (0, halved, low_start, lambda columns: held_low[low_slot, :, :, columns]),
                        (halved, width, high_start, lambda columns: high[block, :, :, columns]),
                    ]
                put(order * blocks + block, here, block, part, pieces)
                if part == 1:
                    @pl.when(block + depth < blocks)
                    def _():
                        copy_in(block + depth).start()

                elif part == 2:
                    @pl.when(block + low_depth < blocks)
                    def _():
                        copy_low(block + low_depth).start()

                return carry

            lax.fori_loop(0, each, body, 0)
    for turn in range(max(0, 3 * blocks - outs_depth), 3 * blocks):
        copy_out(turn, turn % blocks, 0).wait()


def per_device(
    inputs, norm_gain, lengths, gate_rows, up_rows, down_rows, krylov_gate, krylov_up, krylov_down
):
    basis, rows, width = krylov_gate.shape
    devices = lax.axis_size("fsdp")
    bits = devices.bit_length() - 1
    groups = bit_groups(bits)
    hidden_all = rows * devices
    count = 3.0 * width * hidden_all
    inv_d = 1.0 / math.sqrt(width)
    inv_ff = 1.0 / math.sqrt(hidden_all)
    me = lax.axis_index("fsdp").astype(jnp.int32)
    mirror = reverse_bits(me, bits)
    info = jnp.stack([mirror, lengths[0]])

    splits = devices // (width // LANES)
    chunk_rows = LIVE // splits
    lines = 32 if rows % 32 == 0 else rows
    pieces = rows // lines
    long = block_rows(rows)
    halved = width // 2
    product_flops = 2 * rows * width * LIVE

    size = basis * lines

    def rows_of(krylov, first, number):
        def pairs(_, sources, target):
            return [
                (
                    sources[0].at[:, (first + at) * lines : (first + at + 1) * lines, :],
                    target.at[at],
                )
                for at in range(number)
            ]

        return ((krylov,), (number, basis, lines, width), pairs)

    def half_columns(other, before, number):
        def start(info):
            return pl.ds(half_start(info[0], devices, width, other), halved)

        def pairs(info, sources, target):
            return [
                (
                    sources[0].at[:, at * lines : (at + 1) * lines, start(info)],
                    target.at[at],
                )
                for at in range(number)
            ]

        def down_pairs(info, sources, target):
            return [(sources[0].at[:, start(info)], target.at[0])]

        krylov, down = after((krylov_down, down_rows), before)
        return [
            ((krylov,), (number, basis, lines, halved), pairs),
            ((down,), (1, rows, halved), down_pairs),
        ]

    def keep_columns():
        def pairs(info, sources, target):
            columns = pl.ds(half_start(info[0], devices, width, 0), halved)
            return [
                (sources[0].at[:, columns], target.at[0]),
                (sources[1].at[basis - 1, :, columns], target.at[1]),
            ]

        return ((down_rows, krylov_down), (2, rows, halved), pairs)

    cut = (pieces + 1) // 2
    spans = [span for span in ((0, cut), (cut, pieces - cut)) if span[1]]
    helds, gram_sums = [], []

    def gram_stage(group, before):
        at = len(gram_sums) + 1 if helds else 0
        if at > len(spans):
            return None
        operands, results, body = [near(info)], [], lambda info: None
        if at:
            operands += [near(helds[at - 1])] + [near(one) for one in gram_sums[-1:]]
            results = [jax.ShapeDtypeStruct((size, size), F32)]
            body = functools.partial(gram_kernel, not gram_sums)
        fetches = [rows_of(after(krylov_gate, before), *span) for span in spans[at : at + 1]]
        made = call(
            "gram" if at else "read", body, operands, results, [], fetches,
            cost(2 * size * size * width * (cut if at else 1), 2 * size * width * cut),
        )

        def done(made):
            gram_sums.extend(made[: len(results)])
            helds.extend(made[len(results) :])

        return made, done

    own_tokens = inputs.shape[0]
    tokens = own_tokens * devices
    if own_tokens % GROUP == 0:
        sub = own_tokens // GROUP
        lower, upper = gather_blocks(inputs.reshape(sub, GROUP, width), groups, gram_stage)

        def spots(flip, group):
            return (reverse_bits(group // sub, bits) ^ flip) * sub + group % sub

    else:
        gathered = lax.all_gather(inputs, "fsdp", axis=0, tiled=True)
        gathered = gathered.reshape(tokens // GROUP, GROUP, width)
        lower, upper = jnp.split(gathered, 2)

        def spots(flip, group):
            return group

    while len(gram_sums) < len(spans):
        made, done = gram_stage(None, inputs)
        done(made)

    normed, hidden, tangent_t, hidden_t, weight, act, send, keep_down = call(
        "forward",
        functools.partial(forward_kernel, devices, inv_d, inv_ff, spots, splits),
        [
            near(info), near(lower), near(upper), near(norm_gain.reshape(1, width)),
            *(
                (True, far(one))
                for one in (gate_rows, up_rows, krylov_gate, krylov_up, down_rows, krylov_down)
            ),
        ],
        [
            jax.ShapeDtypeStruct((LIVE, width), BF16),
            jax.ShapeDtypeStruct((rows, LIVE), BF16),
            jax.ShapeDtypeStruct((LIVE, rows), BF16),
            jax.ShapeDtypeStruct((LIVE, rows), BF16),
            jax.ShapeDtypeStruct((rows, LIVE), F32),
            jax.ShapeDtypeStruct((rows, LIVE), F32),
            jax.ShapeDtypeStruct((devices // 2, chunk_rows, LANES), BF16),
        ],
        [
            pltpu.VMEM((rows // long, 4, long, width), BF16),
            pltpu.VMEM((2, rows, halved), BF16),
            pltpu.VMEM((rows, LIVE), BF16),
            pltpu.SemaphoreType.DMA((rows // long, 4)),
            pltpu.SemaphoreType.DMA((2,)),
        ],
        [keep_columns()],
        cost(5 * product_flops, 12 * rows * width, rows * LIVE),
        24,
    )

    got = exchange(send, 1)
    (keep,) = call(
        "keep",
        functools.partial(keep_kernel, inv_ff, splits),
        [near(info), near(tangent_t), near(hidden_t), near(keep_down)],
        [jax.ShapeDtypeStruct((devices // 2, chunk_rows, LANES), F32)],
        [],
        [],
        cost(product_flops, 2 * rows * width + 2 * LIVE * width),
    )

    shares = [pieces - 2 * (pieces // 3), pieces // 3, pieces // 3]
    up_jobs = [(sum(shares[:at]), number) for at, number in enumerate(shares) if number]
    up_spans = [(first * lines, number * lines) for first, number in up_jobs]
    prods_up, ups, ahead = [], [], []

    def product(before):
        return call(
            "product",
            product_kernel,
            [near(info), near(normed)] + [near(one) for one in helds],
            [
                jax.ShapeDtypeStruct((basis, rows, LIVE), F32),
                jax.ShapeDtypeStruct((LIVE, LIVE), F32),
            ],
            [],
            [rows_of(after(krylov_up, before), *up_jobs[0])],
            cost(basis * product_flops, 2 * size * width * up_jobs[0][1]),
        )

    def next_both(before):
        at = len(prods_up)
        if at == len(up_jobs):
            return None
        number = up_jobs[at][1]
        if at + 1 < len(up_jobs):
            fetches = [rows_of(after(krylov_up, before), *up_jobs[at + 1])]
        else:
            fetches = half_columns(0, before, pieces)
        made = call(
            "both",
            both_kernel,
            [near(info), near(normed), near(gram_sums[-1]), near(ups[-1])],
            [
                jax.ShapeDtypeStruct((basis, number * lines, LIVE), F32),
                jax.ShapeDtypeStruct((size, size), F32),
            ],
            [],
            fetches,
            cost(2 * size * (size + LIVE) * width * number, 2 * size * width * number),
        )

        def done(made):
            prods_up.append(made[0])
            gram_sums.append(made[1])
            (ups if len(made) == 3 else ahead).extend(made[2:])

        return made, done

    got = [got]
    for at, group in enumerate(groups[1:]):
        parts = flips(group)
        part = keep.shape[0] // (len(parts) + 1)
        sends = [
            add_up([one[turn * part : (turn + 1) * part].astype(F32) for one in [keep] + got])
            for turn in range(1, len(parts) + 1)
        ]
        keep = add_up([one[:part].astype(F32) for one in [keep] + got])
        sends = [one.astype(BF16) for one in sends]
        got = [exchange(one, flip) for one, flip in zip(sends, parts)]
        if at == 0:
            got, (prod_gate, square, first_up) = lax.optimization_barrier((got, product(sends[0])))
            ups.append(first_up)
        elif len(prods_up) < len(up_jobs):
            made, done = next_both(sends[0])
            got, made = lax.optimization_barrier((got, made))
            done(made)
    loss_own = add_up([one.astype(F32) for one in [keep] + got]).astype(BF16)

    back_flops = (basis + 1) * product_flops // 2 + size * size * width * pieces

    def half_call(lower):
        down_low, rows_low = ahead
        return call(
            "back_half",
            functools.partial(back_half_kernel, inv_ff, splits),
            [
                near(info), near(lower), near(down_low), near(rows_low), near(hidden),
                near(gram_sums[-1]),
            ],
            [
                jax.ShapeDtypeStruct((size, size), F32),
                jax.ShapeDtypeStruct((rows, LIVE), F32),
                jax.ShapeDtypeStruct((2, LIVE, LIVE), F32),
                jax.ShapeDtypeStruct((basis, LIVE), F32),
            ],
            [pltpu.VMEM((LIVE, halved), BF16)],
            half_columns(1, lower, pieces),
            cost(back_flops, (basis + 1) * rows * width),
        )

    halves = []

    def beside(group, block):
        if group[0] == 0:
            return half_call(block), halves.extend
        return next_both(block)

    lower, upper = gather_blocks(loss_own, groups, beside)
    gram_sum, back_half, squares_half, values_half, down_high, rows_high = halves

    s_term, r_term, stats, held_gate = call(
        "back",
        functools.partial(back_kernel, inv_d, inv_ff, splits, up_spans),
        [
            near(one)
            for one in (
                info, upper, down_high, rows_high, hidden, weight, act, square, squares_half,
                back_half, gram_sum, values_half, prod_gate, *prods_up,
            )
        ],
        [
            jax.ShapeDtypeStruct((rows, LIVE), BF16),
            jax.ShapeDtypeStruct((rows, LIVE), BF16),
            jax.ShapeDtypeStruct((basis, LANES), F32),
        ],
        [pltpu.VMEM((LIVE, halved), BF16), pltpu.VMEM((size, size), F32)],
        [rows_of(after(krylov_gate, upper), 0, pieces)],
        cost(back_flops, 8 * basis * rows * LIVE),
    )

    stats = jnp.broadcast_to(stats[None], (devices, basis, LANES))
    stats = lax.all_to_all(stats, "fsdp", 0, 0, tiled=True)

    depth, outs_depth = min(3, pieces), min(4, 3 * pieces)
    tall = cut * lines if pieces == 2 * cut else rows
    out_shape = jax.ShapeDtypeStruct((rows, width), BF16)
    new_gate, new_up, new_down, coefficients = pl.pallas_call(
        functools.partial(new_kernel, devices, count, inv_d, inv_ff, splits),
        in_specs=[SMALL] + [FAST] * 8 + [FAR] * 2 + [FAST],
        out_specs=[FAR] * 3 + [SMALL],
        out_shape=[out_shape, out_shape, out_shape, jax.ShapeDtypeStruct((basis + 1,), F32)],
        scratch_shapes=[
            pltpu.VMEM((LIVE, width), BF16),
            pltpu.VMEM((3 * lines, size), BF16),
            pltpu.VMEM((tall, width), F32),
            pltpu.VMEM((depth, basis, lines, width), BF16),
            pltpu.VMEM((depth, basis, lines, halved), BF16),
            pltpu.VMEM((outs_depth, lines, width), BF16),
            pltpu.SemaphoreType.DMA((depth,)),
            pltpu.SemaphoreType.DMA((depth,)),
            pltpu.SemaphoreType.DMA((outs_depth,)),
        ],
        compiler_params=params(18),
        cost_estimate=cost(3 * product_flops, 6 * (basis + 1) * rows * width),
        name="new",
    )(
        info, stats, s_term, r_term, hidden, normed, lower, upper, held_gate,
        far(krylov_up), far(krylov_down), down_high,
    )
    return (new_gate, new_up, new_down, coefficients)


def solution(mesh):
    placed = (
        P("fsdp", None),
        P(),
        P(),
        P("fsdp", None),
        P("fsdp", None),
        P("fsdp", None),
        P(None, "fsdp", None),
        P(None, "fsdp", None),
        P(None, "fsdp", None),
    )
    return jax.shard_map(
        per_device,
        mesh=mesh,
        in_specs=placed,
        out_specs=(P("fsdp", None), P("fsdp", None), P("fsdp", None), P()),
        check_vma=False,
    )
```

```python
import functools
import math

import jax
import jax.numpy as jnp
from jax import lax
from jax.experimental import pallas as pl
from jax.experimental.pallas import tpu as pltpu
from jax.sharding import PartitionSpec as P

LEN = 128
LIVE = 192
GROUP = 8
LANES = 128
F32 = jnp.float32
BF16 = jnp.bfloat16


def gelu_pair(gate_pre):
    coef = math.sqrt(2.0 / math.pi)
    cube = gate_pre * gate_pre * gate_pre
    tanh_val = jnp.tanh(coef * (gate_pre + 0.044715 * cube))
    act = 0.5 * gate_pre * (1.0 + tanh_val)
    slope = 0.5 * (1.0 + tanh_val) + 0.5 * gate_pre * (1.0 - tanh_val * tanh_val) * coef * (
        1.0 + 3.0 * 0.044715 * gate_pre * gate_pre
    )
    return (act, slope)


def dot_nn(left, right):
    return jnp.dot(left, right, preferred_element_type=F32)


def dot_nt(left, right):
    return lax.dot_general(left, right, (((1,), (1,)), ((), ())), preferred_element_type=F32)


def dot_tn(left, right):
    return lax.dot_general(left, right, (((0,), (0,)), ((), ())), preferred_element_type=F32)


def total(values):
    return jnp.sum(jnp.sum(values, axis=0, keepdims=True), axis=1, keepdims=True)


def reverse_bits(value, bits):
    out = value * 0
    for bit in range(bits):
        out = out | (((value >> bit) & 1) << (bits - 1 - bit))
    return out


def exchange(block, flip):
    count = lax.axis_size("fsdp")
    return lax.ppermute(block, "fsdp", [(one, one ^ flip) for one in range(count)])


def bit_groups(bits):
    return [(0, 1)] + [(low, min(2, bits - low)) for low in range(1, bits, 2)]


def flips(group):
    low, size = group
    return [reverse_bits(part, size) << low for part in range(1, 1 << size)]


def gather_blocks(block, groups, beside):
    for group in reversed(groups):
        others = [exchange(block, flip) for flip in flips(group)]
        job = beside(group, block)
        if job is not None:
            work, done = job
            others, made = lax.optimization_barrier((others, work))
            done(made)
        if group[0]:
            block = jnp.concatenate([block] + others, axis=0)
    return block, others[0]


def add_up(values):
    while len(values) > 1:
        values = [one + two for one, two in zip(values[0::2], values[1::2])]
    return values[0]


def far(value):
    return pltpu.with_memory_space_constraint(value, pltpu.HBM)


def after(value, earlier):
    return lax.optimization_barrier((value, earlier))[0]


def stacked(krylov):
    basis, rows, width = krylov.shape
    if rows % 16:
        return krylov.astype(F32).reshape(basis * rows, width).astype(BF16)
    return krylov.reshape(basis * rows, width)


def params(mib):
    return pltpu.CompilerParams(vmem_limit_bytes=mib << 20)


def cost(flops, read, transcendentals=0):
    return pl.CostEstimate(flops=flops, bytes_accessed=read, transcendentals=transcendentals)


FAST = pl.BlockSpec(memory_space=pltpu.VMEM)
SMALL = pl.BlockSpec(memory_space=pltpu.SMEM)
FAR = pl.BlockSpec(memory_space=pltpu.HBM)


def call(name, body, operands, results, scratch, fetches, price, mib=5):
    counts = [len(arrays) for arrays, _, _ in fetches]
    placed = [SMALL] + [FAR if one[0] else FAST for one in operands[1:]]
    values = [one[1] for one in operands]
    for arrays, _, _ in fetches:
        placed += [FAR] * len(arrays)
        values += [far(one) for one in arrays]
    made = [jax.ShapeDtypeStruct(shape, BF16) for _, shape, _ in fetches]
    number = sum(shape[0] * (len(arrays) if len(arrays) > 1 else 1) for arrays, shape, _ in fetches)

    def kernel(*refs):
        at = len(operands)
        own, refs = refs[:at], refs[at:]
        sources, refs = refs[: sum(counts)], refs[sum(counts) :]
        outs, refs = refs[: len(results)], refs[len(results) :]
        targets, refs = refs[: len(fetches)], refs[len(fetches) :]
        copies = []
        for (_, _, pairs), count, target in zip(fetches, counts, targets):
            for source, goal in pairs(own[0], sources[:count], target):
                copies.append(pltpu.make_async_copy(source, goal, refs[-1].at[len(copies)]))
            sources = sources[count:]
        for copy in copies:
            copy.start()
        body(*own, *outs, *refs[: len(scratch)])
        for copy in copies:
            copy.wait()

    return pl.pallas_call(
        kernel,
        in_specs=placed,
        out_specs=[FAST] * (len(results) + len(fetches)),
        out_shape=list(results) + made,
        scratch_shapes=list(scratch) + [pltpu.SemaphoreType.DMA((max(1, number),))],
        compiler_params=params(mib),
        cost_estimate=price,
        name=name,
    )(*values)


def near(value):
    return (False, value)


def block_rows(rows):
    return 64 if rows % 64 == 0 else rows


def half_start(flip, devices, width, other):
    top = lax.div(flip, devices // 2) ^ other
    return pl.multiple_of(top * (width // 2), width // 2)


def live_tokens(info, lower, upper, gain, normed, spots):
    spare = info[1] - (LIVE - LEN)
    shift = lax.rem(spare, GROUP)
    half = (LIVE - LEN) // GROUP
    per = LEN // GROUP
    scale = gain[...].astype(F32)
    row_ids = lax.broadcasted_iota(jnp.int32, (GROUP, 1), 0)

    half_groups = lower.shape[0]

    def load(group):
        spot = spots(info[0], group)
        place = lax.rem(spot, half_groups)
        return jnp.where(spot < half_groups, lower[place], upper[place]).astype(F32)

    def tokens(slot):
        if slot < half:
            return load(slot)
        if slot < 2 * half:
            at = slot - half
            first = load(half + at)
            second = pltpu.roll(load(per + 2 * half - 1 - at), shift, 0)
            return jnp.where(GROUP * at + row_ids < spare, first, second)
        return load(per + slot - 2 * half)

    def norm(wide):
        mean = jnp.mean(wide * wide, axis=1, keepdims=True)
        return wide * lax.rsqrt(mean + 1e-06) * scale

    for pair in range(LIVE // (2 * GROUP)):
        both = [norm(tokens(2 * pair + side)) for side in range(2)]
        normed[2 * GROUP * pair : 2 * GROUP * (pair + 1), :] = jnp.concatenate(both, 0).astype(BF16)


def jvp_half(info, tangent_t, hidden_t, down, probe, out, inv_ff, splits):
    rows = LIVE // splits
    places = out.shape[0]
    width = down.shape[1]
    step = min(512, width)
    each = step // LANES
    for at in range(width // step):
        here = slice(at * step, (at + 1) * step)
        values = dot_nn(tangent_t, down[:, here]) + dot_nn(hidden_t, probe[:, here]) * inv_ff
        for column in range(each):
            for part in range(splits):
                piece = values[
                    part * rows : (part + 1) * rows, column * LANES : (column + 1) * LANES
                ]
                chunk = (at * each + column) * splits + part
                out[chunk ^ (info[0] & (places - 1))] = piece.astype(out.dtype)


def down_copies(info, devices, other, sources, held, sems):
    width = held.shape[2]
    start = half_start(info[0], devices, 2 * width, other)
    return [
        pltpu.make_async_copy(source.at[:, pl.ds(start, width)], held.at[at], sems.at[at])
        for at, source in enumerate(sources)
    ]


def forward_kernel(
    devices, inv_d, inv_ff, spots, splits,
    info, lower, upper, gain, gate, up, krylov_gate, krylov_up, down, krylov_down,
    normed, hidden, tangent_t, hidden_t, weight, act_out, send,
    held, held_down, tangent, row_sems, sems,
):
    basis = krylov_down.shape[0]
    count, _, lines, width = held.shape
    sources = (gate, up, krylov_gate.at[basis - 1], krylov_up.at[basis - 1])
    copies = [
        [
            pltpu.make_async_copy(
                source.at[at * lines : (at + 1) * lines], held.at[at, one], row_sems.at[at, one]
            )
            for one, source in enumerate(sources)
        ]
        for at in range(count)
    ]
    for copy in sum(copies, []):
        copy.start()
    last = down_copies(info, devices, 1, (down, krylov_down.at[basis - 1]), held_down, sems)
    for copy in last:
        copy.start()
    live_tokens(info, lower, upper, gain, normed, spots)
    for at in range(count):
        for copy in copies[at]:
            copy.wait()
        made = dot_nt(stacked(held[at]), normed[...])
        gate_pre, up_pre, tan_gate, tan_up = (
            made[one * lines : (one + 1) * lines] for one in range(4)
        )
        act, slope = gelu_pair(gate_pre)
        here = slice(at * lines, (at + 1) * lines)
        hidden[here, :] = (act * up_pre).astype(BF16)
        tangent[here, :] = (
            slope * (tan_gate * inv_d) * up_pre + act * (tan_up * inv_d)
        ).astype(BF16)
        weight[here, :] = up_pre * slope
        act_out[here, :] = act
    tangent_t[...] = tangent[...].T
    hidden_t[...] = hidden[...].T
    for copy in last:
        copy.wait()
    jvp_half(
        info, tangent_t[...], hidden_t[...], held_down.at[0], held_down.at[1], send, inv_ff, splits
    )


def keep_kernel(inv_ff, splits, info, tangent_t, hidden_t, held_down, keep):
    jvp_half(
        info, tangent_t[...], hidden_t[...], held_down.at[0], held_down.at[1], keep, inv_ff, splits
    )


def fold_gram(sums, basis, lines):
    size = basis * lines
    own = lax.broadcasted_iota(jnp.int32, (size, size), 0)
    other = lax.broadcasted_iota(jnp.int32, (size, size), 1)
    if lines & (lines - 1) == 0:
        same = (own & (lines - 1)) == (other & (lines - 1))
    else:
        same = lax.rem(own, lines) == lax.rem(other, lines)
    kept = jnp.where(same, sums, 0.0)
    rows = [
        jnp.sum(kept[one * lines : (one + 1) * lines], axis=0, keepdims=True)
        for one in range(basis)
    ]
    place = lax.broadcasted_iota(jnp.int32, (size, LANES), 0)
    lane = lax.broadcasted_iota(jnp.int32, (size, LANES), 1) * lines
    picks = jnp.where((place >= lane) & (place < lane + lines), 1.0, 0.0).astype(F32)
    return jnp.dot(
        jnp.concatenate(rows, axis=0), picks,
        precision=lax.Precision.HIGHEST, preferred_element_type=F32,
    )


def gram_kernel(start, info, held, *rest):
    out = rest[-1]
    out[...] = jnp.zeros_like(out) if start else rest[0][...]

    def body(at, carry):
        stack = stacked(held[at])
        out[...] += dot_nt(stack, stack)
        return carry

    lax.fori_loop(0, held.shape[0], body, 0)


def put_products(held, normed, out, ahead, sums):
    count, basis, lines, _ = held.shape

    def body(at, carry):
        stack = stacked(held[at])
        if sums is not None:
            sums[...] += dot_nt(stack, stack)
        made = dot_nt(stack, normed[...])
        here = pl.ds(pl.multiple_of((ahead + at) * lines, lines), lines)
        for one in range(basis):
            out[one, here, :] = made[one * lines : (one + 1) * lines]
        return carry

    lax.fori_loop(0, count, body, 0)


def product_kernel(info, normed, *rest):
    helds, (out, square) = rest[:-2], rest[-2:]
    square[...] = dot_nt(normed[...], normed[...])
    ahead = 0
    for held in helds:
        put_products(held, normed, out, ahead, None)
        ahead += held.shape[0]


def both_kernel(info, normed, earlier, held, out, sums):
    sums[...] = earlier[...]
    put_products(held, normed, out, 0, sums)


def put_loss(loss, first, flip, chunks, splits):
    places = chunks.shape[0]
    for column in range(places // splits):
        pieces = [
            chunks[(column * splits + part) ^ (flip & (places - 1))] for part in range(splits)
        ]
        if splits > 1:
            pieces = [jnp.concatenate([one.astype(F32) for one in pieces], 0).astype(BF16)]
        loss[:, first + column * LANES : first + (column + 1) * LANES] = pieces[0]


def down_products(held, ahead, loss, wide, values, grams):
    count, basis, lines, _ = held.shape
    values = list(values)
    for at in range(count):
        stack = stacked(held[at])
        grams[...] += dot_nt(stack, stack)
        made = dot_nt(stack, loss[...])
        part = wide[(ahead + at) * lines : (ahead + at + 1) * lines]
        for one in range(basis):
            value = part * made[one * lines : (one + 1) * lines]
            values[one] = values[one] + jnp.sum(value, axis=0, keepdims=True)
    return values


def back_half_kernel(
    inv_ff, splits,
    info, chunks, held, held_down, hidden, earlier, grams, back_sum, squares, values, loss,
):
    basis = held.shape[1]
    grams[...] = earlier[...]
    put_loss(loss, 0, info[0], chunks, splits)
    squares[0] = dot_nt(loss[...], loss[...])
    squares[1] = dot_tn(hidden[...], hidden[...]) * (inv_ff * inv_ff)
    back_sum[...] = dot_nt(held_down[0], loss[...])
    wide = hidden[...].astype(F32) * inv_ff
    zeros = [jnp.zeros((1, LIVE), F32) for _ in range(basis)]
    values[...] = jnp.concatenate(down_products(held, 0, loss, wide, zeros, grams), axis=0)


def back_kernel(
    inv_d, inv_ff, splits, spans,
    info, chunks, held, held_down, hidden, weight, act, square, squares_half, back_half, earlier,
    values_half, prod_gate, *rest,
):
    prods_up, rest = rest[: len(spans)], rest[len(spans) :]
    s_out, r_out, stats, loss, grams = rest
    basis, lines = held.shape[1:3]
    grams[...] = earlier[...]
    put_loss(loss, 0, info[0], chunks, splits)
    back = dot_nt(held_down[0], loss[...]) + back_half[...]
    s_term = (back * weight[...]).astype(BF16)
    r_term = (back * act[...]).astype(BF16)
    s_out[...] = s_term
    r_out[...] = r_term
    squares = inv_d * inv_d * ((dot_tn(s_term, s_term) + dot_tn(r_term, r_term)) * square[...])
    other = dot_nt(loss[...], loss[...]) + squares_half[0]
    squares = total(squares + squares_half[1] * other)
    wide_s = s_term.astype(F32) * inv_d
    wide_r = r_term.astype(F32) * inv_d
    values = []
    for one in range(basis):
        value = jnp.sum(wide_s * prod_gate[one], axis=0, keepdims=True)
        for (start, number), prod in zip(spans, prods_up):
            part = wide_r[start : start + number] * prod[one]
            value = value + jnp.sum(part, axis=0, keepdims=True)
        values.append(value + values_half[one : one + 1, :])
    wide = hidden[...].astype(F32) * inv_ff
    values = down_products(held, 0, loss, wide, values, grams)
    lined = jnp.sum(jnp.concatenate(values, axis=0), axis=1, keepdims=True)
    lane = lax.broadcasted_iota(jnp.int32, (basis, LANES), 1)
    made = fold_gram(grams[...], basis, lines)
    stats[...] = made + jnp.where(lane == basis, lined, 0.0) + jnp.where(
        lane == basis + 1, squares, 0.0
    )


def split_three(value):
    first = value.astype(BF16)
    rest = value - first.astype(F32)
    second = rest.astype(BF16)
    return first, second, (rest - second.astype(F32)).astype(BF16)


def new_kernel(
    devices, count, inv_d, inv_ff, splits,
    info, stats, s_term, r_term, hidden, normed, lower, upper, krylov_gate, krylov_up,
    krylov_down, high,
    new_gate, new_up, new_down, coefficients,
    loss, mixer, wide, held, held_low, outs, sems, low_sems, out_sems,
):
    depth, basis, lines, width = held.shape
    blocks = s_term.shape[0] // lines
    halved = width // 2
    size = basis * lines
    narrow = min(256, halved)
    group = min(1024, halved)
    outs_depth, low_depth = outs.shape[0], held_low.shape[0]
    targets = (new_gate, new_up, new_down)
    low_start = half_start(info[0], devices, width, 0)
    high_start = half_start(info[0], devices, width, 1)

    def copy_in(turn, part):
        block = turn - part * blocks
        here = pl.ds(pl.multiple_of(block * lines, lines), lines)
        slot = lax.rem(turn, depth)
        source = (krylov_gate, krylov_up)[part]
        return pltpu.make_async_copy(source.at[:, here, :], held.at[slot], sems.at[slot])

    def copy_low(block):
        here = pl.ds(pl.multiple_of(block * lines, lines), lines)
        slot = lax.rem(block, low_depth)
        return pltpu.make_async_copy(
            krylov_down.at[:, here, pl.ds(low_start, halved)], held_low.at[slot], low_sems.at[slot]
        )

    def copy_out(turn, block, part):
        start = pl.multiple_of(block * lines, lines)
        slot = lax.rem(turn, outs_depth)
        return pltpu.make_async_copy(
            outs.at[slot], targets[part].at[pl.ds(start, lines), :], out_sems.at[slot]
        )

    for block in range(low_depth):
        copy_low(block).start()
    for turn in range(depth):
        copy_in(turn, 0).start()

    for at, half in enumerate((lower, upper)):
        put_loss(loss, at * halved, info[0], half, splits)
    sums = stats[0]
    for one in range(1, devices):
        sums = sums + stats[one]
    lane = lax.broadcasted_iota(jnp.int32, sums.shape, 1)
    row = lax.broadcasted_iota(jnp.int32, sums.shape, 0)

    def pick(where):
        return jnp.sum(jnp.where(where, sums, 0.0))

    proj = [pick((lane == basis) & (row == one)) / count for one in range(basis)]
    squares = pick((lane == basis + 1) & (row == 0))
    for one in range(basis):
        line = jnp.zeros((1, LANES), F32)
        for two in range(basis):
            line = line + proj[two] * sums[two : two + 1, :]
        dots = pick((lane == basis) & (row == one))
        mixed = jnp.sum(jnp.where(lane[0:1] == one, line, 0.0))
        squares = squares + proj[one] * (mixed - 2.0 * dots)
    mean = jnp.maximum(jnp.full((8, LANES), squares / count, F32), 0.0)
    norm = jnp.sqrt(mean + 1e-06)
    inverse = jnp.max(1.0 / norm)
    for one in range(basis):
        coefficients[one] = proj[one]
    coefficients[basis] = jnp.max(norm)
    scales = [one * inverse for one in proj]

    lane = lax.broadcasted_iota(jnp.int32, (lines, size), 1)
    row = lax.broadcasted_iota(jnp.int32, (lines, size), 0)
    values = jnp.zeros((lines, size), F32)
    for one in range(basis):
        values = jnp.where(lane == one * lines + row, scales[one], values)
    terms = [term.astype(F32) for term in split_three(values)]
    mixer[...] = jnp.concatenate(terms, axis=0).astype(BF16)

    def put(turn, here, block, part, pieces):
        slot = lax.rem(turn, outs_depth)

        @pl.when(turn >= outs_depth)
        def _():
            copy_out(turn, block, part).wait()

        for first, last, target, read in pieces:
            broad = min(2048, last - first)
            for start in range(0, last - first, broad):
                mixed = dot_nn(mixer[...], stacked(read(slice(start, start + broad))))
                mixed = mixed[:lines] + (mixed[lines : 2 * lines] + mixed[2 * lines :])
                value = wide[here, first + start : first + start + broad] - mixed
                goal = pl.ds(pl.multiple_of(target + start, broad), broad)
                outs[slot, :, goal] = value.astype(BF16)
        copy_out(turn, block, part).start()

    tall = wide.shape[0]
    each = tall // lines
    for order, part in enumerate((2, 0, 1)):
        left, right, scale = (
            (s_term, normed, inv_d), (r_term, normed, inv_d), (hidden, loss, inv_ff)
        )[part]
        for share in range(blocks // each):
            for start in range(0, width, group):
                columns = slice(start, start + group)
                rows_here = slice(share * tall, (share + 1) * tall)
                made = dot_nn(left[rows_here, :], right[:, columns])
                wide[:, columns] = made * (scale * inverse)

            def body(at, carry, part=part, order=order, share=share):
                block = share * each + at
                here = pl.ds(pl.multiple_of(at * lines, lines), lines)
                turn = part * blocks + block
                slot = lax.rem(turn, depth)
                low_slot = lax.rem(block, low_depth)
                if part != 2:
                    copy_in(turn, part).wait()
                    pieces = [(0, width, 0, lambda columns: held[slot, :, :, columns])]
                else:
                    copy_low(block).wait()
                    pieces = [
                        (0, halved, low_start, lambda columns: held_low[low_slot, :, :, columns]),
                        (halved, width, high_start, lambda columns: high[block, :, :, columns]),
                    ]
                put(order * blocks + block, here, block, part, pieces)
                if part != 2:
                    for later in range(part, 2):
                        there = (turn + depth >= later * blocks) & (
                            turn + depth < (later + 1) * blocks
                        )

                        @pl.when(there)
                        def _(later=later):
                            copy_in(turn + depth, later).start()

                else:
                    @pl.when(block + low_depth < blocks)
                    def _():
                        copy_low(block + low_depth).start()

                return carry

            lax.fori_loop(0, each, body, 0)
    for turn in range(max(0, 3 * blocks - outs_depth), 3 * blocks):
        copy_out(turn, turn % blocks, 0).wait()


def per_device(
    inputs, norm_gain, lengths, gate_rows, up_rows, down_rows, krylov_gate, krylov_up, krylov_down
):
    basis, rows, width = krylov_gate.shape
    devices = lax.axis_size("fsdp")
    bits = devices.bit_length() - 1
    groups = bit_groups(bits)
    hidden_all = rows * devices
    count = 3.0 * width * hidden_all
    inv_d = 1.0 / math.sqrt(width)
    inv_ff = 1.0 / math.sqrt(hidden_all)
    me = lax.axis_index("fsdp").astype(jnp.int32)
    mirror = reverse_bits(me, bits)
    info = jnp.stack([mirror, lengths[0]])

    splits = devices // (width // LANES)
    chunk_rows = LIVE // splits
    lines = 32 if rows % 32 == 0 else rows
    pieces = rows // lines
    long = block_rows(rows)
    halved = width // 2
    product_flops = 2 * rows * width * LIVE

    size = basis * lines

    def rows_of(krylov, first, number):
        def pairs(_, sources, target):
            return [
                (
                    sources[0].at[:, (first + at) * lines : (first + at + 1) * lines, :],
                    target.at[at],
                )
                for at in range(number)
            ]

        return ((krylov,), (number, basis, lines, width), pairs)

    def half_columns(other, before, number):
        def start(info):
            return pl.ds(half_start(info[0], devices, width, other), halved)

        def pairs(info, sources, target):
            return [
                (
                    sources[0].at[:, at * lines : (at + 1) * lines, start(info)],
                    target.at[at],
                )
                for at in range(number)
            ]

        def down_pairs(info, sources, target):
            return [(sources[0].at[:, start(info)], target.at[0])]

        krylov, down = after((krylov_down, down_rows), before)
        return [
            ((krylov,), (number, basis, lines, halved), pairs),
            ((down,), (1, rows, halved), down_pairs),
        ]

    def keep_columns():
        def pairs(info, sources, target):
            columns = pl.ds(half_start(info[0], devices, width, 0), halved)
            return [
                (sources[0].at[:, columns], target.at[0]),
                (sources[1].at[basis - 1, :, columns], target.at[1]),
            ]

        return ((down_rows, krylov_down), (2, rows, halved), pairs)

    cut = (pieces + 1) // 2
    spans = [span for span in ((0, cut), (cut, pieces - cut)) if span[1]]
    helds, gram_sums = [], []

    def gram_stage(group, before):
        at = len(gram_sums) + 1 if helds else 0
        if at > len(spans):
            return None
        operands, results, body = [near(info)], [], lambda info: None
        if at:
            operands += [near(helds[at - 1])] + [near(one) for one in gram_sums[-1:]]
            results = [jax.ShapeDtypeStruct((size, size), F32)]
            body = functools.partial(gram_kernel, not gram_sums)
        fetches = [rows_of(after(krylov_gate, before), *span) for span in spans[at : at + 1]]
        made = call(
            "gram" if at else "read", body, operands, results, [], fetches,
            cost(2 * size * size * width * (cut if at else 1), 2 * size * width * cut),
        )

        def done(made):
            gram_sums.extend(made[: len(results)])
            helds.extend(made[len(results) :])

        return made, done

    own_tokens = inputs.shape[0]
    tokens = own_tokens * devices
    if own_tokens % GROUP == 0:
        sub = own_tokens // GROUP
        lower, upper = gather_blocks(inputs.reshape(sub, GROUP, width), groups, gram_stage)

        def spots(flip, group):
            return (reverse_bits(group // sub, bits) ^ flip) * sub + group % sub

    else:
        gathered = lax.all_gather(inputs, "fsdp", axis=0, tiled=True)
        gathered = gathered.reshape(tokens // GROUP, GROUP, width)
        lower, upper = jnp.split(gathered, 2)

        def spots(flip, group):
            return group

    while len(gram_sums) < len(spans):
        made, done = gram_stage(None, inputs)
        done(made)

    normed, hidden, tangent_t, hidden_t, weight, act, send, keep_down = call(
        "forward",
        functools.partial(forward_kernel, devices, inv_d, inv_ff, spots, splits),
        [
            near(info), near(lower), near(upper), near(norm_gain.reshape(1, width)),
            *(
                (True, far(one))
                for one in (gate_rows, up_rows, krylov_gate, krylov_up, down_rows, krylov_down)
            ),
        ],
        [
            jax.ShapeDtypeStruct((LIVE, width), BF16),
            jax.ShapeDtypeStruct((rows, LIVE), BF16),
            jax.ShapeDtypeStruct((LIVE, rows), BF16),
            jax.ShapeDtypeStruct((LIVE, rows), BF16),
            jax.ShapeDtypeStruct((rows, LIVE), F32),
            jax.ShapeDtypeStruct((rows, LIVE), F32),
            jax.ShapeDtypeStruct((devices // 2, chunk_rows, LANES), BF16),
        ],
        [
            pltpu.VMEM((rows // long, 4, long, width), BF16),
            pltpu.VMEM((2, rows, halved), BF16),
            pltpu.VMEM((rows, LIVE), BF16),
            pltpu.SemaphoreType.DMA((rows // long, 4)),
            pltpu.SemaphoreType.DMA((2,)),
        ],
        [keep_columns()],
        cost(5 * product_flops, 12 * rows * width, rows * LIVE),
        24,
    )

    got = exchange(send, 1)
    (keep,) = call(
        "keep",
        functools.partial(keep_kernel, inv_ff, splits),
        [near(info), near(tangent_t), near(hidden_t), near(keep_down)],
        [jax.ShapeDtypeStruct((devices // 2, chunk_rows, LANES), F32)],
        [],
        [],
        cost(product_flops, 2 * rows * width + 2 * LIVE * width),
    )

    shares = [pieces - 2 * (pieces // 3), pieces // 3, pieces // 3]
    up_jobs = [(sum(shares[:at]), number) for at, number in enumerate(shares) if number]
    up_spans = [(first * lines, number * lines) for first, number in up_jobs]
    prods_up, ups, ahead = [], [], []

    def product(before):
        return call(
            "product",
            product_kernel,
            [near(info), near(normed)] + [near(one) for one in helds],
            [
                jax.ShapeDtypeStruct((basis, rows, LIVE), F32),
                jax.ShapeDtypeStruct((LIVE, LIVE), F32),
            ],
            [],
            [rows_of(after(krylov_up, before), *up_jobs[0])],
            cost(basis * product_flops, 2 * size * width * up_jobs[0][1]),
        )

    def next_both(before):
        at = len(prods_up)
        if at == len(up_jobs):
            return None
        number = up_jobs[at][1]
        if at + 1 < len(up_jobs):
            fetches = [rows_of(after(krylov_up, before), *up_jobs[at + 1])]
        else:
            fetches = half_columns(0, before, pieces)
        made = call(
            "both",
            both_kernel,
            [near(info), near(normed), near(gram_sums[-1]), near(ups[-1])],
            [
                jax.ShapeDtypeStruct((basis, number * lines, LIVE), F32),
                jax.ShapeDtypeStruct((size, size), F32),
            ],
            [],
            fetches,
            cost(2 * size * (size + LIVE) * width * number, 2 * size * width * number),
        )

        def done(made):
            prods_up.append(made[0])
            gram_sums.append(made[1])
            (ups if len(made) == 3 else ahead).extend(made[2:])

        return made, done

    got = [got]
    for at, group in enumerate(groups[1:]):
        parts = flips(group)
        part = keep.shape[0] // (len(parts) + 1)
        sends = [
            add_up([one[turn * part : (turn + 1) * part].astype(F32) for one in [keep] + got])
            for turn in range(1, len(parts) + 1)
        ]
        keep = add_up([one[:part].astype(F32) for one in [keep] + got])
        sends = [one.astype(BF16) for one in sends]
        got = [exchange(one, flip) for one, flip in zip(sends, parts)]
        if at == 0:
            got, (prod_gate, square, first_up) = lax.optimization_barrier((got, product(sends[0])))
            ups.append(first_up)
        elif len(prods_up) < len(up_jobs):
            made, done = next_both(sends[0])
            got, made = lax.optimization_barrier((got, made))
            done(made)
    loss_own = add_up([one.astype(F32) for one in [keep] + got]).astype(BF16)

    back_flops = (basis + 1) * product_flops // 2 + size * size * width * pieces

    def half_call(lower):
        down_low, rows_low = ahead
        return call(
            "back_half",
            functools.partial(back_half_kernel, inv_ff, splits),
            [
                near(info), near(lower), near(down_low), near(rows_low), near(hidden),
                near(gram_sums[-1]),
            ],
            [
                jax.ShapeDtypeStruct((size, size), F32),
                jax.ShapeDtypeStruct((rows, LIVE), F32),
                jax.ShapeDtypeStruct((2, LIVE, LIVE), F32),
                jax.ShapeDtypeStruct((basis, LIVE), F32),
            ],
            [pltpu.VMEM((LIVE, halved), BF16)],
            half_columns(1, lower, pieces),
            cost(back_flops, (basis + 1) * rows * width),
        )

    halves = []

    def beside(group, block):
        if group[0] == 0:
            return half_call(block), halves.extend
        return next_both(block)

    lower, upper = gather_blocks(loss_own, groups, beside)
    gram_sum, back_half, squares_half, values_half, down_high, rows_high = halves

    s_term, r_term, stats = call(
        "back",
        functools.partial(back_kernel, inv_d, inv_ff, splits, up_spans),
        [
            near(one)
            for one in (
                info, upper, down_high, rows_high, hidden, weight, act, square, squares_half,
                back_half, gram_sum, values_half, prod_gate, *prods_up,
            )
        ],
        [
            jax.ShapeDtypeStruct((rows, LIVE), BF16),
            jax.ShapeDtypeStruct((rows, LIVE), BF16),
            jax.ShapeDtypeStruct((basis, LANES), F32),
        ],
        [pltpu.VMEM((LIVE, halved), BF16), pltpu.VMEM((size, size), F32)],
        [],
        cost(back_flops, 8 * basis * rows * LIVE),
    )

    stats = jnp.broadcast_to(stats[None], (devices, basis, LANES))
    stats = lax.all_to_all(stats, "fsdp", 0, 0, tiled=True)

    depth, outs_depth = min(6, pieces), min(4, 3 * pieces)
    tall = cut * lines if pieces == 2 * cut else rows
    out_shape = jax.ShapeDtypeStruct((rows, width), BF16)
    new_gate, new_up, new_down, coefficients = pl.pallas_call(
        functools.partial(new_kernel, devices, count, inv_d, inv_ff, splits),
        in_specs=[SMALL] + [FAST] * 7 + [FAR] * 3 + [FAST],
        out_specs=[FAR] * 3 + [SMALL],
        out_shape=[out_shape, out_shape, out_shape, jax.ShapeDtypeStruct((basis + 1,), F32)],
        scratch_shapes=[
            pltpu.VMEM((LIVE, width), BF16),
            pltpu.VMEM((3 * lines, size), BF16),
            pltpu.VMEM((tall, width), F32),
            pltpu.VMEM((depth, basis, lines, width), BF16),
            pltpu.VMEM((min(4, depth), basis, lines, halved), BF16),
            pltpu.VMEM((outs_depth, lines, width), BF16),
            pltpu.SemaphoreType.DMA((depth,)),
            pltpu.SemaphoreType.DMA((min(4, depth),)),
            pltpu.SemaphoreType.DMA((outs_depth,)),
        ],
        compiler_params=params(28),
        cost_estimate=cost(3 * product_flops, 6 * (basis + 1) * rows * width),
        name="new",
    )(
        info, stats, s_term, r_term, hidden, normed, lower, upper, far(krylov_gate),
        far(krylov_up), far(krylov_down), down_high,
    )
    return (new_gate, new_up, new_down, coefficients)


def solution(mesh):
    placed = (
        P("fsdp", None),
        P(),
        P(),
        P("fsdp", None),
        P("fsdp", None),
        P("fsdp", None),
        P(None, "fsdp", None),
        P(None, "fsdp", None),
        P(None, "fsdp", None),
    )
    return jax.shard_map(
        per_device,
        mesh=mesh,
        in_specs=placed,
        out_specs=(P("fsdp", None), P("fsdp", None), P("fsdp", None), P()),
        check_vma=False,
    )
```

```python
import functools
import math

import jax
import jax.numpy as jnp
from jax import lax
from jax.experimental import pallas as pl
from jax.experimental.pallas import tpu as pltpu
from jax.sharding import PartitionSpec as P

LEN = 128
LIVE = 192
GROUP = 8
LANES = 128
F32 = jnp.float32
BF16 = jnp.bfloat16


def gelu_pair(gate_pre):
    coef = math.sqrt(2.0 / math.pi)
    cube = gate_pre * gate_pre * gate_pre
    tanh_val = jnp.tanh(coef * (gate_pre + 0.044715 * cube))
    act = 0.5 * gate_pre * (1.0 + tanh_val)
    slope = 0.5 * (1.0 + tanh_val) + 0.5 * gate_pre * (1.0 - tanh_val * tanh_val) * coef * (
        1.0 + 3.0 * 0.044715 * gate_pre * gate_pre
    )
    return (act, slope)


def dot_nn(left, right):
    return jnp.dot(left, right, preferred_element_type=F32)


def dot_nt(left, right):
    return lax.dot_general(left, right, (((1,), (1,)), ((), ())), preferred_element_type=F32)


def dot_tn(left, right):
    return lax.dot_general(left, right, (((0,), (0,)), ((), ())), preferred_element_type=F32)


def total(values):
    return jnp.sum(jnp.sum(values, axis=0, keepdims=True), axis=1, keepdims=True)


def reverse_bits(value, bits):
    out = value * 0
    for bit in range(bits):
        out = out | (((value >> bit) & 1) << (bits - 1 - bit))
    return out


def exchange(block, flip):
    count = lax.axis_size("fsdp")
    return lax.ppermute(block, "fsdp", [(one, one ^ flip) for one in range(count)])


def bit_groups(bits):
    return [(0, 1)] + [(low, min(2, bits - low)) for low in range(1, bits, 2)]


def flips(group):
    low, size = group
    return [reverse_bits(part, size) << low for part in range(1, 1 << size)]


def gather_blocks(block, groups, beside):
    for group in reversed(groups):
        others = [exchange(block, flip) for flip in flips(group)]
        job = beside(group, block)
        if job is not None:
            work, done = job
            others, made = lax.optimization_barrier((others, work))
            done(made)
        if group[0]:
            block = jnp.concatenate([block] + others, axis=0)
    return block, others[0]


def add_up(values):
    while len(values) > 1:
        values = [one + two for one, two in zip(values[0::2], values[1::2])]
    return values[0]


def far(value):
    return pltpu.with_memory_space_constraint(value, pltpu.HBM)


def after(value, earlier):
    return lax.optimization_barrier((value, earlier))[0]


def stacked(krylov):
    basis, rows, width = krylov.shape
    if rows % 16:
        return krylov.astype(F32).reshape(basis * rows, width).astype(BF16)
    return krylov.reshape(basis * rows, width)


def params(mib):
    return pltpu.CompilerParams(vmem_limit_bytes=mib << 20)


def cost(flops, read, transcendentals=0):
    return pl.CostEstimate(flops=flops, bytes_accessed=read, transcendentals=transcendentals)


FAST = pl.BlockSpec(memory_space=pltpu.VMEM)
SMALL = pl.BlockSpec(memory_space=pltpu.SMEM)
FAR = pl.BlockSpec(memory_space=pltpu.HBM)


def call(name, body, operands, results, scratch, fetches, price, mib=5):
    counts = [len(arrays) for arrays, _, _ in fetches]
    placed = [SMALL] + [FAR if one[0] else FAST for one in operands[1:]]
    values = [one[1] for one in operands]
    for arrays, _, _ in fetches:
        placed += [FAR] * len(arrays)
        values += [far(one) for one in arrays]
    made = [jax.ShapeDtypeStruct(shape, BF16) for _, shape, _ in fetches]
    number = sum(shape[0] * (len(arrays) if len(arrays) > 1 else 1) for arrays, shape, _ in fetches)

    def kernel(*refs):
        at = len(operands)
        own, refs = refs[:at], refs[at:]
        sources, refs = refs[: sum(counts)], refs[sum(counts) :]
        outs, refs = refs[: len(results)], refs[len(results) :]
        targets, refs = refs[: len(fetches)], refs[len(fetches) :]
        copies = []
        for (_, _, pairs), count, target in zip(fetches, counts, targets):
            for source, goal in pairs(own[0], sources[:count], target):
                copies.append(pltpu.make_async_copy(source, goal, refs[-1].at[len(copies)]))
            sources = sources[count:]
        for copy in copies:
            copy.start()
        body(*own, *outs, *refs[: len(scratch)])
        for copy in copies:
            copy.wait()

    return pl.pallas_call(
        kernel,
        in_specs=placed,
        out_specs=[FAST] * (len(results) + len(fetches)),
        out_shape=list(results) + made,
        scratch_shapes=list(scratch) + [pltpu.SemaphoreType.DMA((max(1, number),))],
        compiler_params=params(mib),
        cost_estimate=price,
        name=name,
    )(*values)


def near(value):
    return (False, value)


def block_rows(rows):
    return 64 if rows % 64 == 0 else rows


def half_start(flip, devices, width, other):
    top = lax.div(flip, devices // 2) ^ other
    return pl.multiple_of(top * (width // 2), width // 2)


def live_tokens(info, lower, upper, gain, normed, spots):
    spare = info[1] - (LIVE - LEN)
    shift = lax.rem(spare, GROUP)
    half = (LIVE - LEN) // GROUP
    per = LEN // GROUP
    scale = gain[...].astype(F32)
    row_ids = lax.broadcasted_iota(jnp.int32, (GROUP, 1), 0)

    half_groups = lower.shape[0]

    def load(group):
        spot = spots(info[0], group)
        place = lax.rem(spot, half_groups)
        return jnp.where(spot < half_groups, lower[place], upper[place]).astype(F32)

    def tokens(slot):
        if slot < half:
            return load(slot)
        if slot < 2 * half:
            at = slot - half
            first = load(half + at)
            second = pltpu.roll(load(per + 2 * half - 1 - at), shift, 0)
            return jnp.where(GROUP * at + row_ids < spare, first, second)
        return load(per + slot - 2 * half)

    def norm(wide):
        mean = jnp.mean(wide * wide, axis=1, keepdims=True)
        return wide * lax.rsqrt(mean + 1e-06) * scale

    for pair in range(LIVE // (2 * GROUP)):
        both = [norm(tokens(2 * pair + side)) for side in range(2)]
        normed[2 * GROUP * pair : 2 * GROUP * (pair + 1), :] = jnp.concatenate(both, 0).astype(BF16)


def jvp_half(info, tangent_t, hidden_t, down, probe, out, inv_ff, splits):
    rows = LIVE // splits
    places = out.shape[0]
    width = down.shape[1]
    step = min(512, width)
    each = step // LANES
    for at in range(width // step):
        here = slice(at * step, (at + 1) * step)
        values = dot_nn(tangent_t, down[:, here]) + dot_nn(hidden_t, probe[:, here]) * inv_ff
        for column in range(each):
            for part in range(splits):
                piece = values[
                    part * rows : (part + 1) * rows, column * LANES : (column + 1) * LANES
                ]
                chunk = (at * each + column) * splits + part
                out[chunk ^ (info[0] & (places - 1))] = piece.astype(out.dtype)


def down_copies(info, devices, other, sources, held, sems):
    width = held.shape[2]
    start = half_start(info[0], devices, 2 * width, other)
    return [
        pltpu.make_async_copy(source.at[:, pl.ds(start, width)], held.at[at], sems.at[at])
        for at, source in enumerate(sources)
    ]


def forward_kernel(
    devices, inv_d, inv_ff, spots, splits,
    info, lower, upper, gain, gate, up, krylov_gate, krylov_up, down, krylov_down,
    normed, hidden, tangent_t, hidden_t, weight, act_out, send,
    held, held_down, tangent, row_sems, sems,
):
    basis = krylov_down.shape[0]
    count, _, lines, width = held.shape
    sources = (gate, up, krylov_gate.at[basis - 1], krylov_up.at[basis - 1])
    copies = [
        [
            pltpu.make_async_copy(
                source.at[at * lines : (at + 1) * lines], held.at[at, one], row_sems.at[at, one]
            )
            for one, source in enumerate(sources)
        ]
        for at in range(count)
    ]
    for copy in sum(copies, []):
        copy.start()
    last = down_copies(info, devices, 1, (down, krylov_down.at[basis - 1]), held_down, sems)
    for copy in last:
        copy.start()
    live_tokens(info, lower, upper, gain, normed, spots)
    for at in range(count):
        for copy in copies[at]:
            copy.wait()
        made = dot_nt(stacked(held[at]), normed[...])
        gate_pre, up_pre, tan_gate, tan_up = (
            made[one * lines : (one + 1) * lines] for one in range(4)
        )
        act, slope = gelu_pair(gate_pre)
        here = slice(at * lines, (at + 1) * lines)
        hidden[here, :] = (act * up_pre).astype(BF16)
        tangent[here, :] = (
            slope * (tan_gate * inv_d) * up_pre + act * (tan_up * inv_d)
        ).astype(BF16)
        weight[here, :] = up_pre * slope
        act_out[here, :] = act
    tangent_t[...] = tangent[...].T
    hidden_t[...] = hidden[...].T
    for copy in last:
        copy.wait()
    jvp_half(
        info, tangent_t[...], hidden_t[...], held_down.at[0], held_down.at[1], send, inv_ff, splits
    )


def keep_kernel(inv_ff, splits, info, tangent_t, hidden_t, held_down, keep):
    jvp_half(
        info, tangent_t[...], hidden_t[...], held_down.at[0], held_down.at[1], keep, inv_ff, splits
    )


def fold_gram(sums, basis, lines):
    size = basis * lines
    own = lax.broadcasted_iota(jnp.int32, (size, size), 0)
    other = lax.broadcasted_iota(jnp.int32, (size, size), 1)
    if lines & (lines - 1) == 0:
        same = (own & (lines - 1)) == (other & (lines - 1))
    else:
        same = lax.rem(own, lines) == lax.rem(other, lines)
    kept = jnp.where(same, sums, 0.0)
    rows = [
        jnp.sum(kept[one * lines : (one + 1) * lines], axis=0, keepdims=True)
        for one in range(basis)
    ]
    place = lax.broadcasted_iota(jnp.int32, (size, LANES), 0)
    lane = lax.broadcasted_iota(jnp.int32, (size, LANES), 1) * lines
    picks = jnp.where((place >= lane) & (place < lane + lines), 1.0, 0.0).astype(F32)
    return jnp.dot(
        jnp.concatenate(rows, axis=0), picks,
        precision=lax.Precision.HIGHEST, preferred_element_type=F32,
    )


def gram_kernel(start, info, held, *rest):
    out = rest[-1]
    out[...] = jnp.zeros_like(out) if start else rest[0][...]

    def body(at, carry):
        stack = stacked(held[at])
        out[...] += dot_nt(stack, stack)
        return carry

    lax.fori_loop(0, held.shape[0], body, 0)


def put_products(held, normed, out, ahead, sums):
    count, basis, lines, _ = held.shape

    def body(at, carry):
        stack = stacked(held[at])
        if sums is not None:
            sums[...] += dot_nt(stack, stack)
        made = dot_nt(stack, normed[...])
        here = pl.ds(pl.multiple_of((ahead + at) * lines, lines), lines)
        for one in range(basis):
            out[one, here, :] = made[one * lines : (one + 1) * lines]
        return carry

    lax.fori_loop(0, count, body, 0)


def product_kernel(info, normed, *rest):
    helds, (out, square) = rest[:-2], rest[-2:]
    square[...] = dot_nt(normed[...], normed[...])
    ahead = 0
    for held in helds:
        put_products(held, normed, out, ahead, None)
        ahead += held.shape[0]


def both_kernel(info, normed, earlier, held, out, sums):
    sums[...] = earlier[...]
    put_products(held, normed, out, 0, sums)


def put_loss(loss, first, flip, chunks, splits):
    places = chunks.shape[0]
    for column in range(places // splits):
        pieces = [
            chunks[(column * splits + part) ^ (flip & (places - 1))] for part in range(splits)
        ]
        if splits > 1:
            pieces = [jnp.concatenate([one.astype(F32) for one in pieces], 0).astype(BF16)]
        loss[:, first + column * LANES : first + (column + 1) * LANES] = pieces[0]


def down_products(held, ahead, loss, wide, values, grams):
    count, basis, lines, _ = held.shape
    values = list(values)
    for at in range(count):
        stack = stacked(held[at])
        grams[...] += dot_nt(stack, stack)
        made = dot_nt(stack, loss[...])
        part = wide[(ahead + at) * lines : (ahead + at + 1) * lines]
        for one in range(basis):
            value = part * made[one * lines : (one + 1) * lines]
            values[one] = values[one] + jnp.sum(value, axis=0, keepdims=True)
    return values


def back_half_kernel(
    inv_ff, splits,
    info, chunks, held, held_down, hidden, earlier, grams, back_sum, squares, values, loss,
):
    basis = held.shape[1]
    grams[...] = earlier[...]
    put_loss(loss, 0, info[0], chunks, splits)
    squares[0] = dot_nt(loss[...], loss[...])
    squares[1] = dot_tn(hidden[...], hidden[...]) * (inv_ff * inv_ff)
    back_sum[...] = dot_nt(held_down[0], loss[...])
    wide = hidden[...].astype(F32) * inv_ff
    zeros = [jnp.zeros((1, LIVE), F32) for _ in range(basis)]
    values[...] = jnp.concatenate(down_products(held, 0, loss, wide, zeros, grams), axis=0)


def back_kernel(
    inv_d, inv_ff, splits, spans,
    info, chunks, held, held_down, hidden, weight, act, square, squares_half, back_half, earlier,
    values_half, prod_gate, *rest,
):
    prods_up, rest = rest[: len(spans)], rest[len(spans) :]
    s_out, r_out, stats, loss, grams = rest
    basis, lines = held.shape[1:3]
    grams[...] = earlier[...]
    put_loss(loss, 0, info[0], chunks, splits)
    back = dot_nt(held_down[0], loss[...]) + back_half[...]
    s_term = (back * weight[...]).astype(BF16)
    r_term = (back * act[...]).astype(BF16)
    s_out[...] = s_term
    r_out[...] = r_term
    squares = inv_d * inv_d * ((dot_tn(s_term, s_term) + dot_tn(r_term, r_term)) * square[...])
    other = dot_nt(loss[...], loss[...]) + squares_half[0]
    squares = total(squares + squares_half[1] * other)
    wide_s = s_term.astype(F32) * inv_d
    wide_r = r_term.astype(F32) * inv_d
    values = []
    for one in range(basis):
        value = jnp.sum(wide_s * prod_gate[one], axis=0, keepdims=True)
        for (start, number), prod in zip(spans, prods_up):
            part = wide_r[start : start + number] * prod[one]
            value = value + jnp.sum(part, axis=0, keepdims=True)
        values.append(value + values_half[one : one + 1, :])
    wide = hidden[...].astype(F32) * inv_ff
    values = down_products(held, 0, loss, wide, values, grams)
    lined = jnp.sum(jnp.concatenate(values, axis=0), axis=1, keepdims=True)
    lane = lax.broadcasted_iota(jnp.int32, (basis, LANES), 1)
    made = fold_gram(grams[...], basis, lines)
    stats[...] = made + jnp.where(lane == basis, lined, 0.0) + jnp.where(
        lane == basis + 1, squares, 0.0
    )


def split_three(value):
    first = value.astype(BF16)
    rest = value - first.astype(F32)
    second = rest.astype(BF16)
    return first, second, (rest - second.astype(F32)).astype(BF16)


def new_kernel(
    devices, count, inv_d, inv_ff, splits,
    info, stats, s_term, r_term, hidden, normed, lower, upper, krylov_gate, krylov_up,
    krylov_down, high,
    new_gate, new_up, new_down, coefficients,
    loss, mixer, wide, held, held_low, outs, sems, low_sems, out_sems,
):
    depth, basis, lines, width = held.shape
    blocks = s_term.shape[0] // lines
    halved = width // 2
    size = basis * lines
    narrow = min(256, halved)
    group = min(1024, halved)
    outs_depth, low_depth = outs.shape[0], held_low.shape[0]
    targets = (new_gate, new_up, new_down)
    low_start = half_start(info[0], devices, width, 0)
    high_start = half_start(info[0], devices, width, 1)

    def copy_in(turn, part):
        block = turn - part * blocks
        here = pl.ds(pl.multiple_of(block * lines, lines), lines)
        slot = lax.rem(turn, depth)
        source = (krylov_gate, krylov_up)[part]
        return pltpu.make_async_copy(source.at[:, here, :], held.at[slot], sems.at[slot])

    def copy_low(block):
        here = pl.ds(pl.multiple_of(block * lines, lines), lines)
        slot = lax.rem(block, low_depth)
        return pltpu.make_async_copy(
            krylov_down.at[:, here, pl.ds(low_start, halved)], held_low.at[slot], low_sems.at[slot]
        )

    def copy_out(turn, block, part):
        start = pl.multiple_of(block * lines, lines)
        slot = lax.rem(turn, outs_depth)
        return pltpu.make_async_copy(
            outs.at[slot], targets[part].at[pl.ds(start, lines), :], out_sems.at[slot]
        )

    for block in range(low_depth):
        copy_low(block).start()
    for turn in range(depth):
        copy_in(turn, 0).start()

    for at, half in enumerate((lower, upper)):
        put_loss(loss, at * halved, info[0], half, splits)
    sums = stats[0]
    for one in range(1, devices):
        sums = sums + stats[one]
    lane = lax.broadcasted_iota(jnp.int32, sums.shape, 1)
    row = lax.broadcasted_iota(jnp.int32, sums.shape, 0)

    def pick(where):
        return jnp.sum(jnp.where(where, sums, 0.0))

    proj = [pick((lane == basis) & (row == one)) / count for one in range(basis)]
    squares = pick((lane == basis + 1) & (row == 0))
    for one in range(basis):
        line = jnp.zeros((1, LANES), F32)
        for two in range(basis):
            line = line + proj[two] * sums[two : two + 1, :]
        dots = pick((lane == basis) & (row == one))
        mixed = jnp.sum(jnp.where(lane[0:1] == one, line, 0.0))
        squares = squares + proj[one] * (mixed - 2.0 * dots)
    mean = jnp.maximum(jnp.full((8, LANES), squares / count, F32), 0.0)
    norm = jnp.sqrt(mean + 1e-06)
    inverse = jnp.max(1.0 / norm)
    for one in range(basis):
        coefficients[one] = proj[one]
    coefficients[basis] = jnp.max(norm)
    scales = [one * inverse for one in proj]

    lane = lax.broadcasted_iota(jnp.int32, (lines, size), 1)
    row = lax.broadcasted_iota(jnp.int32, (lines, size), 0)
    values = jnp.zeros((lines, size), F32)
    for one in range(basis):
        values = jnp.where(lane == one * lines + row, scales[one], values)
    terms = [term.astype(F32) for term in split_three(values)]
    mixer[...] = jnp.concatenate(terms, axis=0).astype(BF16)

    def put(turn, here, block, part, pieces):
        slot = lax.rem(turn, outs_depth)

        @pl.when(turn >= outs_depth)
        def _():
            copy_out(turn, block, part).wait()

        for first, last, target, read in pieces:
            broad = min(1024, last - first)
            for start in range(0, last - first, broad):
                mixed = dot_nn(mixer[...], stacked(read(slice(start, start + broad))))
                mixed = mixed[:lines] + (mixed[lines : 2 * lines] + mixed[2 * lines :])
                value = wide[here, first + start : first + start + broad] - mixed
                goal = pl.ds(pl.multiple_of(target + start, broad), broad)
                outs[slot, :, goal] = value.astype(BF16)
        copy_out(turn, block, part).start()

    tall = wide.shape[0]
    each = tall // lines
    for order, part in enumerate((2, 0, 1)):
        left, right, scale = (
            (s_term, normed, inv_d), (r_term, normed, inv_d), (hidden, loss, inv_ff)
        )[part]
        for share in range(blocks // each):
            for start in range(0, width, group):
                columns = slice(start, start + group)
                rows_here = slice(share * tall, (share + 1) * tall)
                made = dot_nn(left[rows_here, :], right[:, columns])
                wide[:, columns] = made * (scale * inverse)

            def body(at, carry, part=part, order=order, share=share):
                block = share * each + at
                here = pl.ds(pl.multiple_of(at * lines, lines), lines)
                turn = part * blocks + block
                slot = lax.rem(turn, depth)
                low_slot = lax.rem(block, low_depth)
                if part != 2:
                    copy_in(turn, part).wait()
                    pieces = [(0, width, 0, lambda columns: held[slot, :, :, columns])]
                else:
                    copy_low(block).wait()
                    pieces = [
                        (0, halved, low_start, lambda columns: held_low[low_slot, :, :, columns]),
                        (halved, width, high_start, lambda columns: high[block, :, :, columns]),
                    ]
                put(order * blocks + block, here, block, part, pieces)
                if part != 2:
                    for later in range(part, 2):
                        there = (turn + depth >= later * blocks) & (
                            turn + depth < (later + 1) * blocks
                        )

                        @pl.when(there)
                        def _(later=later):
                            copy_in(turn + depth, later).start()

                else:
                    @pl.when(block + low_depth < blocks)
                    def _():
                        copy_low(block + low_depth).start()

                return carry

            lax.fori_loop(0, each, body, 0, unroll=True)
    for turn in range(max(0, 3 * blocks - outs_depth), 3 * blocks):
        copy_out(turn, turn % blocks, 0).wait()


def per_device(
    inputs, norm_gain, lengths, gate_rows, up_rows, down_rows, krylov_gate, krylov_up, krylov_down
):
    basis, rows, width = krylov_gate.shape
    devices = lax.axis_size("fsdp")
    bits = devices.bit_length() - 1
    groups = bit_groups(bits)
    hidden_all = rows * devices
    count = 3.0 * width * hidden_all
    inv_d = 1.0 / math.sqrt(width)
    inv_ff = 1.0 / math.sqrt(hidden_all)
    me = lax.axis_index("fsdp").astype(jnp.int32)
    mirror = reverse_bits(me, bits)
    info = jnp.stack([mirror, lengths[0]])

    splits = devices // (width // LANES)
    chunk_rows = LIVE // splits
    lines = 32 if rows % 32 == 0 else rows
    pieces = rows // lines
    long = block_rows(rows)
    halved = width // 2
    product_flops = 2 * rows * width * LIVE

    size = basis * lines

    def rows_of(krylov, first, number):
        def pairs(_, sources, target):
            return [
                (
                    sources[0].at[:, (first + at) * lines : (first + at + 1) * lines, :],
                    target.at[at],
                )
                for at in range(number)
            ]

        return ((krylov,), (number, basis, lines, width), pairs)

    def half_columns(other, before, number):
        def start(info):
            return pl.ds(half_start(info[0], devices, width, other), halved)

        def pairs(info, sources, target):
            return [
                (
                    sources[0].at[:, at * lines : (at + 1) * lines, start(info)],
                    target.at[at],
                )
                for at in range(number)
            ]

        def down_pairs(info, sources, target):
            return [(sources[0].at[:, start(info)], target.at[0])]

        krylov, down = after((krylov_down, down_rows), before)
        return [
            ((krylov,), (number, basis, lines, halved), pairs),
            ((down,), (1, rows, halved), down_pairs),
        ]

    def keep_columns():
        def pairs(info, sources, target):
            columns = pl.ds(half_start(info[0], devices, width, 0), halved)
            return [
                (sources[0].at[:, columns], target.at[0]),
                (sources[1].at[basis - 1, :, columns], target.at[1]),
            ]

        return ((down_rows, krylov_down), (2, rows, halved), pairs)

    cut = (pieces + 1) // 2
    spans = [span for span in ((0, cut), (cut, pieces - cut)) if span[1]]
    helds, gram_sums = [], []

    def gram_stage(group, before):
        at = len(gram_sums) + 1 if helds else 0
        if at > len(spans):
            return None
        operands, results, body = [near(info)], [], lambda info: None
        if at:
            operands += [near(helds[at - 1])] + [near(one) for one in gram_sums[-1:]]
            results = [jax.ShapeDtypeStruct((size, size), F32)]
            body = functools.partial(gram_kernel, not gram_sums)
        fetches = [rows_of(after(krylov_gate, before), *span) for span in spans[at : at + 1]]
        made = call(
            "gram" if at else "read", body, operands, results, [], fetches,
            cost(2 * size * size * width * (cut if at else 1), 2 * size * width * cut),
        )

        def done(made):
            gram_sums.extend(made[: len(results)])
            helds.extend(made[len(results) :])

        return made, done

    own_tokens = inputs.shape[0]
    tokens = own_tokens * devices
    if own_tokens % GROUP == 0:
        sub = own_tokens // GROUP
        lower, upper = gather_blocks(inputs.reshape(sub, GROUP, width), groups, gram_stage)

        def spots(flip, group):
            return (reverse_bits(group // sub, bits) ^ flip) * sub + group % sub

    else:
        gathered = lax.all_gather(inputs, "fsdp", axis=0, tiled=True)
        gathered = gathered.reshape(tokens // GROUP, GROUP, width)
        lower, upper = jnp.split(gathered, 2)

        def spots(flip, group):
            return group

    while len(gram_sums) < len(spans):
        made, done = gram_stage(None, inputs)
        done(made)

    normed, hidden, tangent_t, hidden_t, weight, act, send, keep_down = call(
        "forward",
        functools.partial(forward_kernel, devices, inv_d, inv_ff, spots, splits),
        [
            near(info), near(lower), near(upper), near(norm_gain.reshape(1, width)),
            *(
                (True, far(one))
                for one in (gate_rows, up_rows, krylov_gate, krylov_up, down_rows, krylov_down)
            ),
        ],
        [
            jax.ShapeDtypeStruct((LIVE, width), BF16),
            jax.ShapeDtypeStruct((rows, LIVE), BF16),
            jax.ShapeDtypeStruct((LIVE, rows), BF16),
            jax.ShapeDtypeStruct((LIVE, rows), BF16),
            jax.ShapeDtypeStruct((rows, LIVE), F32),
            jax.ShapeDtypeStruct((rows, LIVE), F32),
            jax.ShapeDtypeStruct((devices // 2, chunk_rows, LANES), BF16),
        ],
        [
            pltpu.VMEM((rows // long, 4, long, width), BF16),
            pltpu.VMEM((2, rows, halved), BF16),
            pltpu.VMEM((rows, LIVE), BF16),
            pltpu.SemaphoreType.DMA((rows // long, 4)),
            pltpu.SemaphoreType.DMA((2,)),
        ],
        [keep_columns()],
        cost(5 * product_flops, 12 * rows * width, rows * LIVE),
        24,
    )

    got = exchange(send, 1)
    (keep,) = call(
        "keep",
        functools.partial(keep_kernel, inv_ff, splits),
        [near(info), near(tangent_t), near(hidden_t), near(keep_down)],
        [jax.ShapeDtypeStruct((devices // 2, chunk_rows, LANES), F32)],
        [],
        [],
        cost(product_flops, 2 * rows * width + 2 * LIVE * width),
    )

    shares = [pieces - 2 * (pieces // 3), pieces // 3, pieces // 3]
    up_jobs = [(sum(shares[:at]), number) for at, number in enumerate(shares) if number]
    up_spans = [(first * lines, number * lines) for first, number in up_jobs]
    prods_up, ups, ahead = [], [], []

    def product(before):
        return call(
            "product",
            product_kernel,
            [near(info), near(normed)] + [near(one) for one in helds],
            [
                jax.ShapeDtypeStruct((basis, rows, LIVE), F32),
                jax.ShapeDtypeStruct((LIVE, LIVE), F32),
            ],
            [],
            [rows_of(after(krylov_up, before), *up_jobs[0])],
            cost(basis * product_flops, 2 * size * width * up_jobs[0][1]),
        )

    def next_both(before):
        at = len(prods_up)
        if at == len(up_jobs):
            return None
        number = up_jobs[at][1]
        if at + 1 < len(up_jobs):
            fetches = [rows_of(after(krylov_up, before), *up_jobs[at + 1])]
        else:
            fetches = half_columns(0, before, pieces)
        made = call(
            "both",
            both_kernel,
            [near(info), near(normed), near(gram_sums[-1]), near(ups[-1])],
            [
                jax.ShapeDtypeStruct((basis, number * lines, LIVE), F32),
                jax.ShapeDtypeStruct((size, size), F32),
            ],
            [],
            fetches,
            cost(2 * size * (size + LIVE) * width * number, 2 * size * width * number),
        )

        def done(made):
            prods_up.append(made[0])
            gram_sums.append(made[1])
            (ups if len(made) == 3 else ahead).extend(made[2:])

        return made, done

    got = [got]
    for at, group in enumerate(groups[1:]):
        parts = flips(group)
        part = keep.shape[0] // (len(parts) + 1)
        sends = [
            add_up([one[turn * part : (turn + 1) * part].astype(F32) for one in [keep] + got])
            for turn in range(1, len(parts) + 1)
        ]
        keep = add_up([one[:part].astype(F32) for one in [keep] + got])
        sends = [one.astype(BF16) for one in sends]
        got = [exchange(one, flip) for one, flip in zip(sends, parts)]
        if at == 0:
            got, (prod_gate, square, first_up) = lax.optimization_barrier((got, product(sends[0])))
            ups.append(first_up)
        elif len(prods_up) < len(up_jobs):
            made, done = next_both(sends[0])
            got, made = lax.optimization_barrier((got, made))
            done(made)
    loss_own = add_up([one.astype(F32) for one in [keep] + got]).astype(BF16)

    back_flops = (basis + 1) * product_flops // 2 + size * size * width * pieces

    def half_call(lower):
        down_low, rows_low = ahead
        return call(
            "back_half",
            functools.partial(back_half_kernel, inv_ff, splits),
            [
                near(info), near(lower), near(down_low), near(rows_low), near(hidden),
                near(gram_sums[-1]),
            ],
            [
                jax.ShapeDtypeStruct((size, size), F32),
                jax.ShapeDtypeStruct((rows, LIVE), F32),
                jax.ShapeDtypeStruct((2, LIVE, LIVE), F32),
                jax.ShapeDtypeStruct((basis, LIVE), F32),
            ],
            [pltpu.VMEM((LIVE, halved), BF16)],
            half_columns(1, lower, pieces),
            cost(back_flops, (basis + 1) * rows * width),
        )

    halves = []

    def beside(group, block):
        if group[0] == 0:
            return half_call(block), halves.extend
        return next_both(block)

    lower, upper = gather_blocks(loss_own, groups, beside)
    gram_sum, back_half, squares_half, values_half, down_high, rows_high = halves

    s_term, r_term, stats = call(
        "back",
        functools.partial(back_kernel, inv_d, inv_ff, splits, up_spans),
        [
            near(one)
            for one in (
                info, upper, down_high, rows_high, hidden, weight, act, square, squares_half,
                back_half, gram_sum, values_half, prod_gate, *prods_up,
            )
        ],
        [
            jax.ShapeDtypeStruct((rows, LIVE), BF16),
            jax.ShapeDtypeStruct((rows, LIVE), BF16),
            jax.ShapeDtypeStruct((basis, LANES), F32),
        ],
        [pltpu.VMEM((LIVE, halved), BF16), pltpu.VMEM((size, size), F32)],
        [],
        cost(back_flops, 8 * basis * rows * LIVE),
    )

    stats = jnp.broadcast_to(stats[None], (devices, basis, LANES))
    stats = lax.all_to_all(stats, "fsdp", 0, 0, tiled=True)

    depth, outs_depth = min(6, pieces), min(4, 3 * pieces)
    tall = cut * lines if pieces == 2 * cut else rows
    out_shape = jax.ShapeDtypeStruct((rows, width), BF16)
    new_gate, new_up, new_down, coefficients = pl.pallas_call(
        functools.partial(new_kernel, devices, count, inv_d, inv_ff, splits),
        in_specs=[SMALL] + [FAST] * 7 + [FAR] * 3 + [FAST],
        out_specs=[FAR] * 3 + [SMALL],
        out_shape=[out_shape, out_shape, out_shape, jax.ShapeDtypeStruct((basis + 1,), F32)],
        scratch_shapes=[
            pltpu.VMEM((LIVE, width), BF16),
            pltpu.VMEM((3 * lines, size), BF16),
            pltpu.VMEM((tall, width), F32),
            pltpu.VMEM((depth, basis, lines, width), BF16),
            pltpu.VMEM((min(4, depth), basis, lines, halved), BF16),
            pltpu.VMEM((outs_depth, lines, width), BF16),
            pltpu.SemaphoreType.DMA((depth,)),
            pltpu.SemaphoreType.DMA((min(4, depth),)),
            pltpu.SemaphoreType.DMA((outs_depth,)),
        ],
        compiler_params=params(28),
        cost_estimate=cost(3 * product_flops, 6 * (basis + 1) * rows * width),
        name="new",
    )(
        info, stats, s_term, r_term, hidden, normed, lower, upper, far(krylov_gate),
        far(krylov_up), far(krylov_down), down_high,
    )
    return (new_gate, new_up, new_down, coefficients)


def solution(mesh):
    placed = (
        P("fsdp", None),
        P(),
        P(),
        P("fsdp", None),
        P("fsdp", None),
        P("fsdp", None),
        P(None, "fsdp", None),
        P(None, "fsdp", None),
        P(None, "fsdp", None),
    )
    return jax.shard_map(
        per_device,
        mesh=mesh,
        in_specs=placed,
        out_specs=(P("fsdp", None), P("fsdp", None), P("fsdp", None), P()),
        check_vma=False,
    )
```
